512 devices in a mesh: layer: 8 (over z_hi, core), row: 64 (over x, y, z_lo).
Axes of the slice: x: 4, y: 8, z: 8 (z_hi: 4, z_lo: 2; z = z_hi * 2 + z_lo), core: 2. Of those that a mesh axis runs over, the one named last changes fastest.
Arguments:
- state: float32 [8, 2048, 2048], P('layer', 'row'), may hold values from -6 to 6
- start_state: float32 [8, 2048, 2048], P('layer', 'row'), may hold values from -6 to 6
- to_modes: float32 [8, 8], replicated, may hold values from -2 to 2
- from_modes: float32 [8, 8], replicated, may hold values from -2 to 2
- deform: float32 [8], replicated, may hold values from 4 to 900
Outputs:
- tendency: float32 [8, 2048, 2048], P('layer', 'row')
- new_state: float32 [8, 2048, 2048], P('layer', 'row')
The draws below stay inside these ranges and needn't reach their ends.
All inputs are finite; a program needn't handle non-finite values.
Results may differ from the reference program's by a relative error of at most 0.0005.
Values sent between devices are 32-bit elements; how exact they have to be, the bound alone decides.
No kernel may reach another device: no remote copies, remote signals or barrier semaphores. Data moves between devices by JAX's collectives and lax.ppermute only.
A program may use at most 64 MiB of HBM per device.

```python
import math
import jax
import jax.numpy as jnp
from jax import lax

GRID = 2048
LAYERS = 8
KCUT = 672


def draw_state(key, part):
    key = jax.random.fold_in(key, 7)
    return jnp.clip(jax.random.normal(key, (LAYERS, GRID, GRID), jnp.float32), -6.0, 6.0)


def block_scale(key, extent, pieces, low, high):
    factor_of = 1.0
    for dim, parts in pieces:
        steps = jax.random.uniform(jax.random.fold_in(jax.random.fold_in(key, 6), dim), (parts,), jnp.float32, low / len(pieces), high / len(pieces))
        factor_of = factor_of * jnp.repeat(jnp.exp(steps), extent[dim] // parts).reshape((-1,) + (1,) * (len(extent) - 1 - dim))
    return factor_of


def normal_values(own_key, extent, deviation, most, cuts=(), kind=jnp.bfloat16):
    loudness = block_scale(own_key, extent, cuts, -0.22, 0.18) if cuts else 1.0
    result = jax.random.normal(own_key, extent, jnp.float32) * deviation * loudness
    return jnp.minimum(jnp.maximum(result, -most), most).astype(kind)


def setup_inputs(seed: int = 0) -> dict:
    keys = jax.random.split(jax.random.key(seed), 6)
    state = draw_state(jax.random.fold_in(keys[5], 71), 0)
    start_state = normal_values(keys[1], (LAYERS, GRID, GRID), 1.0, 6.0, ((0, 8), (1, 64)), jnp.float32)
    to_modes = normal_values(keys[2], (LAYERS, LAYERS), LAYERS ** -0.5, 2.0, (), jnp.float32)
    from_modes = normal_values(keys[3], (LAYERS, LAYERS), LAYERS ** -0.5, 2.0, (), jnp.float32)
    deform = jnp.clip(jnp.exp(jax.random.uniform(keys[4], (LAYERS,), jnp.float32, math.log(4.0), math.log(900.0))), 4.0, 900.0)
    return {"state": state, "start_state": start_state, "to_modes": to_modes, "from_modes": from_modes, "deform": deform}


HYPER_RATE = 0.2
STEP_SIZE = 0.5


def wavenumbers():
    index = jnp.arange(GRID)
    return jnp.where(index < GRID // 2, index, index - GRID).astype(jnp.float32)


def reference(state, start_state, to_modes, from_modes, deform):
    waves = wavenumbers()
    wave_y = waves[:, None]
    wave_x = waves[None, :]
    retained = ((jnp.abs(wave_x) < KCUT) & (jnp.abs(wave_y) < KCUT)).astype(jnp.float32)
    square = wave_x * wave_x + wave_y * wave_y
    spectrum = jnp.fft.fft2(state) * retained
    modal = jnp.einsum('mn,nyx->myx', to_modes.astype(spectrum.dtype), spectrum, precision=lax.Precision.HIGHEST)
    modal = modal * (-1.0 / (square[None, :, :] + deform[:, None, None]))
    stream = jnp.einsum('lm,myx->lyx', from_modes.astype(spectrum.dtype), modal, precision=lax.Precision.HIGHEST)
    damping = HYPER_RATE * (square / (KCUT * KCUT)) ** 4

    def layer_step(halves):
        stream_layer, vort_layer = halves
        eastward = jnp.real(jnp.fft.ifft2(-1j * wave_y * stream_layer))
        northward = jnp.real(jnp.fft.ifft2(1j * wave_x * stream_layer))
        slope_x = jnp.real(jnp.fft.ifft2(1j * wave_x * vort_layer))
        slope_y = jnp.real(jnp.fft.ifft2(1j * wave_y * vort_layer))
        jacobian = eastward * slope_x + northward * slope_y
        flux = jnp.fft.fft2(jacobian) * retained
        total = -flux - damping * vort_layer
        return jnp.real(jnp.fft.ifft2(total)).astype(jnp.float32)

    tendency = lax.map(layer_step, (stream, spectrum))
    new_state = 0.75 * start_state + 0.25 * (state + STEP_SIZE * tendency)
    return tendency, new_state
```

```python
import functools
import math

import jax
import jax.numpy as jnp
import ml_dtypes
import numpy as np
from jax import lax
from jax.experimental import pallas as pl
from jax.experimental.pallas import tpu as pltpu
from jax.sharding import PartitionSpec as P

GRID = 2048
KCUT = 672
ROWS = 32
HALF = 14
CHUNK = 6
KAP = 64
JP = 21
PIECE = 8 * JP
SPAN = 512
HYPER_RATE = 0.2
STEP_SIZE = 0.5
BF16 = jnp.bfloat16
F32 = jnp.float32


def halves(table):
    high = table.astype(ml_dtypes.bfloat16)
    low = (table - high.astype(np.float64)).astype(ml_dtypes.bfloat16)
    return np.stack([high, low])


def turn(numerator, denominator):
    angle = 2.0 * math.pi * (np.mod(numerator, denominator) / denominator)
    return np.cos(angle), np.sin(angle)


def x_forward_table():
    b = np.arange(128)
    table = np.zeros((2, 16, 8, 2, 128))
    for half in range(2):
        for tau in range(HALF):
            for j3 in range(3):
                c, s = turn((3 * tau + j3 - 42 * half) * b, 128)
                table[half, tau, j3, 0] = c
                table[half, tau, j3, 1] = s
                table[half, tau, 3 + j3, 0] = -s
                table[half, tau, 3 + j3, 1] = c
    return halves(table.reshape(2, 128, 256))


def x_inverse_table(times_i):
    b = np.arange(128)
    table = np.zeros((2, 2, 3, 16, 2, 128))
    for half in range(2):
        for tau in range(HALF):
            for j3 in range(3):
                c, s = turn((3 * tau + j3 - 42 * half) * b, 128)
                if times_i:
                    c, s = -s, c
                table[half, 0, j3, tau, 0] = c
                table[half, 0, j3, tau, 1] = s
                table[half, 1, j3, tau, 0] = -s
                table[half, 1, j3, tau, 1] = c
    return halves(table.reshape(192, 256) * (2.0 / (GRID * GRID)))


def x_twiddle():
    table = np.zeros((32, 128))
    c, s = turn(np.arange(9)[:, None] * np.arange(128)[None, :], GRID)
    table[0:9] = c
    table[16:25] = s
    return table.astype(np.float32)


def y_radix_table():
    c, s = turn(np.arange(KAP)[:, None] * np.arange(64)[None, :] + 32 * np.arange(64)[None, :], 64)
    return halves(np.block([[c, s], [-s, c]]))


def y_radix_inverse_table():
    c, s = turn(np.arange(64)[:, None] * np.arange(KAP)[None, :] + 32 * np.arange(64)[:, None], 64)
    return halves(np.block([[c, -s], [s, c]]))


def y_twiddle():
    c, s = turn((np.arange(KAP)[:, None] - KCUT) * np.arange(ROWS)[None, :], GRID)
    return np.stack([np.tile(c, (1, 4)), np.tile(s, (1, 4))]).astype(np.float32)


def y_lane_table():
    c, s = turn(np.arange(ROWS)[:, None] * np.arange(JP)[None, :], ROWS)
    table = np.zeros((3, 2, 4, ROWS, 256))
    for j3 in range(3):
        for slot in range(4):
            re = 40 * j3 + slot * JP
            im = re + 4 * JP
            table[j3, 0, slot, :, re : re + JP] = c
            table[j3, 1, slot, :, re : re + JP] = s
            table[j3, 0, slot, :, im : im + JP] = -s
            table[j3, 1, slot, :, im : im + JP] = c
    return halves(table.reshape(3, 256, 256))


def y_lane_inverse_table():
    high, low = y_lane_table()
    return np.stack([np.swapaxes(high, 1, 2), np.swapaxes(low, 1, 2)])


def lane_facts():
    lane = np.arange(SPAN)
    j3 = lane // PIECE
    slot = (lane % (4 * JP)) // JP
    facts = np.zeros((8, SPAN))
    facts[0] = 16 * j3
    facts[1] = slot
    facts[2] = 64 * (lane % JP) - KCUT
    facts[3] = slot == 0
    return facts.astype(np.float32)


def split(value):
    high = value.astype(BF16)
    low = (value - high.astype(F32)).astype(BF16)
    return high, low


def matmul(left, right, dims):
    def one(a, b):
        return lax.dot_general(a, b, (dims, ((), ())), preferred_element_type=F32)

    return one(left[0], right[0]) + (one(left[0], right[1]) + one(left[1], right[0]))


NN = ((1,), (0,))
NT = ((1,), (1,))
TN = ((0,), (0,))

C1 = math.cos(math.pi / 8)
C2 = math.cos(math.pi / 4)
C3 = math.cos(3 * math.pi / 8)


def real_analysis(x):
    s = [x[a] + x[a + 8] for a in range(8)]
    d = [x[a] - x[a + 8] for a in range(8)]
    e = [None] + [d[a] - d[8 - a] for a in range(1, 4)]
    f = [None] + [d[a] + d[8 - a] for a in range(1, 4)]
    e2, f2 = e[2] * C2, f[2] * C2
    plus, minus = d[0] + e2, d[0] - e2
    first, second = e[1] * C1 + e[3] * C3, e[1] * C3 - e[3] * C1
    third, fourth = f[1] * C3 + f[3] * C1, f[1] * C1 - f[3] * C3
    u, v = d[4] + f2, f2 - d[4]
    p = [s[a] + s[a + 4] for a in range(4)]
    q = [s[a] - s[a + 4] for a in range(4)]
    even, odd = p[0] + p[2], p[1] + p[3]
    hd, hs = (q[1] - q[3]) * C2, (q[1] + q[3]) * C2
    real = [
        even + odd,
        plus + first,
        q[0] + hd,
        minus + second,
        p[0] - p[2],
        minus - second,
        q[0] - hd,
        plus - first,
        even - odd,
    ]
    imag = [
        None,
        -(third + u),
        -(q[2] + hs),
        -(fourth + v),
        p[3] - p[1],
        v - fourth,
        q[2] - hs,
        u - third,
        None,
    ]
    return real, imag


def real_synthesis(real, imag):
    plus, first = real[1] + real[7], real[1] - real[7]
    minus, second = real[3] + real[5], real[3] - real[5]
    third, u = -(imag[1] + imag[7]), imag[7] - imag[1]
    fourth, v = -(imag[3] + imag[5]), imag[5] - imag[3]
    d = [None] * 8
    d[0], d[4] = plus + minus, u - v
    e = [None, first * C1 + second * C3, (plus - minus) * C2, first * C3 - second * C1]
    f = [None, third * C3 + fourth * C1, (u + v) * C2, third * C1 - fourth * C3]
    for a in range(1, 4):
        d[a], d[8 - a] = f[a] + e[a], f[a] - e[a]
    even, odd = real[0] + real[8], real[0] - real[8]
    p = [even + real[4], odd - imag[4], even - real[4], odd + imag[4]]
    hr, hi = (real[2] - real[6]) * C2, (imag[2] + imag[6]) * C2
    q = [real[2] + real[6], hr - hi, imag[6] - imag[2], -(hr + hi)]
    s = [p[a] + q[a] for a in range(4)] + [p[a] - q[a] for a in range(4)]
    return [s[a] + d[a] for a in range(8)] + [s[a] - d[a] for a in range(8)]


def x_forward(real, imag, twiddle, table):
    pieces = []
    for k in range(9):
        if k == 0:
            pieces.append(jnp.concatenate([real[0], jnp.zeros_like(real[0])], axis=1))
            continue
        c, s = twiddle[k : k + 1], twiddle[16 + k : 17 + k]
        if k == 8:
            re, im = real[8] * c, -(real[8] * s)
        else:
            re, im = real[k] * c + imag[k] * s, imag[k] * c - real[k] * s
        pieces.append(jnp.concatenate([re, im], axis=1))
    shared = split(jnp.concatenate(pieces[1:8], axis=0))
    results = []
    for half, own in enumerate((pieces[0], pieces[8])):
        own = split(own)
        right = [jnp.concatenate([own[i], shared[i]], axis=0) for i in range(2)]
        results.append(matmul([table[0, half], table[1, half]], right, NT))
    return results


def x_inverse(left, right, fields, table):
    left = split(left)
    right = split(right)
    upper = [table[i][:96] for i in range(2)]
    lower = [table[i][96:] for i in range(2)]
    first = matmul([part[:96] for part in left], upper, TN)
    second = matmul([part[96:] for part in left], lower, TN)
    rest = matmul(right, [table[i] for i in range(2)], TN)
    return first, second, rest


def modes_of(first, second, rest, field, rows, twiddle):
    real, imag = [], []
    for k in range(9):
        c, s = twiddle[k : k + 1], twiddle[16 + k : 17 + k]
        base = field * 128 + rows.start
        size = rows.stop - rows.start
        if k in (0, 8):
            source = first if k == 0 else second
            z = source[base : base + size]
        elif k < 4:
            start = base + 32 * k
            z = first[start : start + size] + second[start : start + size]
        else:
            start = base + 32 * (k - 4)
            z = rest[start : start + size]
        re, im = z[:, :128], z[:, 128:]
        if k == 0:
            real.append(re)
            imag.append(None)
        else:
            real.append(re * c - im * s)
            imag.append(None if k == 8 else re * s + im * c)
    return real, imag


def y_forward(pieces, radix, twiddle, lanes, facts):
    stacked = jnp.concatenate(
        [jnp.concatenate(pieces[0], axis=1), jnp.concatenate(pieces[1], axis=1)], axis=0
    )
    mixed = matmul([radix[0], radix[1]], split(stacked), NN)
    c, s = twiddle[0], twiddle[1]
    windows = []
    for j3 in range(3):
        re, im = mixed[:KAP, 128 * j3 : 128 * j3 + 128], mixed[KAP:, 128 * j3 : 128 * j3 + 128]
        turned = jnp.concatenate([re * c + im * s, im * c - re * s], axis=1)
        windows.append(matmul(split(turned), [lanes[0, j3], lanes[1, j3]], NN))
    first, second, third = windows
    spectrum = jnp.concatenate(
        [
            first[:, :128],
            first[:, 128:] + second[:, :128],
            second[:, 128:] + third[:, :128],
            third[:, 128:],
        ],
        axis=1,
    )
    wave_y = y_waves(facts)
    return jnp.where(wave_y > -KCUT, spectrum, 0.0)


def y_waves(facts):
    kap = lax.broadcasted_iota(jnp.int32, (KAP, 1), 0).astype(F32)
    return kap + facts[2:3]


def x_waves(facts, owner):
    group = owner // 32
    half = (owner % 32) // 16
    tau = owner % 16
    base = (4 * group + 16 * (3 * tau - 42 * half)).astype(F32)
    shift = (8 * half * (1 - group)).astype(F32)
    return facts[0:1] + facts[1:2] + base + shift * facts[3:4]


def y_inverse(spectra, radix, twiddle, lanes):
    count = len(spectra)
    stacked = split(jnp.concatenate(spectra, axis=0) if count > 1 else spectra[0])
    c, s = twiddle[0], twiddle[1]
    real, imag = [], []
    for j3 in range(3):
        window = [part[:, 128 * j3 : 128 * j3 + 256] for part in stacked]
        out = matmul(window, [lanes[0, j3], lanes[1, j3]], NN)
        for field in range(count):
            own = out[KAP * field : KAP * field + KAP]
            re, im = own[:, :128], own[:, 128:]
            real.append(re * c - im * s)
            imag.append(re * s + im * c)
    right = split(
        jnp.concatenate([jnp.concatenate(real, axis=1), jnp.concatenate(imag, axis=1)], axis=0)
    )
    out = matmul([radix[0], radix[1]], right, NN)
    fields = []
    for field in range(count):
        columns = [slice(128 * (count * j3 + field), 128 * (count * j3 + field) + 128) for j3 in range(3)]
        fields.append([[out[:64, own] for own in columns], [out[64:, own] for own in columns]])
    return fields


def stream_function(gathered, to_modes, from_modes, deform, layer, square):
    weights = [from_modes(layer, m) * (-1.0 / (square + deform(m))) for m in range(8)]
    total = None
    for n in range(8):
        factor = None
        for m in range(8):
            term = weights[m] * to_modes(m, n)
            factor = term if factor is None else factor + term
        term = factor * gathered(n)
        total = term if total is None else total + term
    return total


def store_x(out_ref, results):
    for half in range(2):
        for group in range(2):
            block = results[half][:, 128 * group : 128 * group + 128]
            for tau in range(16):
                start = (32 * group + 16 * half + tau) * CHUNK
                out_ref[start : start + CHUNK, :] = block[8 * tau : 8 * tau + CHUNK]


def load_pieces(ref):
    return [
        [ref[pl.ds(3 * part + j3, 64, stride=CHUNK), :] for j3 in range(3)] for part in range(2)
    ]


def store_pieces(ref, fields):
    stride = CHUNK * len(fields)
    for field, pieces in enumerate(fields):
        for part in range(2):
            for j3 in range(3):
                ref[pl.ds(CHUNK * field + 3 * part + j3, 64, stride=stride), :] = pieces[part][j3]


def load_x(ref, fields):
    stride = CHUNK * fields
    groups = []
    for group in range(2):
        columns = []
        for field in range(fields):
            rows = []
            for half in range(2):
                for part in range(CHUNK):
                    start = (32 * group + 16 * half) * stride + CHUNK * field + part
                    rows.append(ref[pl.ds(start, 16, stride=stride), :])
            columns.append(jnp.concatenate(rows, axis=0))
        groups.append(columns)
    return groups


def state_kernel(state_ref, twiddle_ref, table_ref, out_ref):
    x = [state_ref[0, :, 128 * a : 128 * a + 128] for a in range(16)]
    real, imag = real_analysis(x)
    store_x(out_ref, x_forward(real, imag, twiddle_ref[...], table_ref))


def spectrum_kernel(in_ref, radix_ref, unradix_ref, turn_ref, lanes_ref, unlanes_ref, facts_ref, spec_ref, out_ref):
    facts = facts_ref[...]
    spectrum = y_forward(load_pieces(in_ref), radix_ref, turn_ref, lanes_ref, facts)
    spec_ref[...] = spectrum
    wave_x = x_waves(facts, lax.axis_index("row"))
    wave_y = y_waves(facts)
    weight = jnp.where(wave_x == 0.0, 0.5, 1.0)
    fields = [wave_x * spectrum, (wave_y * weight) * spectrum]
    store_pieces(out_ref, y_inverse(fields, unradix_ref, turn_ref, unlanes_ref))


def stream_kernel(
    to_ref, from_ref, deform_ref, all_ref, unradix_ref, turn_ref, unlanes_ref, facts_ref, out_ref
):
    facts = facts_ref[...]
    wave_x = x_waves(facts, lax.axis_index("row"))
    wave_y = y_waves(facts)
    square = wave_x * wave_x + wave_y * wave_y
    stream = stream_function(
        lambda n: all_ref[n],
        lambda m, n: to_ref[m, n],
        lambda l, m: from_ref[l, m],
        lambda m: deform_ref[m],
        lax.axis_index("layer"),
        square,
    )
    weight = jnp.where(wave_x == 0.0, 0.5, 1.0)
    fields = [-(wave_y * weight) * stream, wave_x * stream]
    store_pieces(out_ref, y_inverse(fields, unradix_ref, turn_ref, unlanes_ref))


def jacobian_kernel(flow_ref, slope_ref, twiddle_ref, untable_ref, table_ref, out_ref, z0, z1, z2, jac):
    flow = load_x(flow_ref, 2)
    slope = load_x(slope_ref, 2)
    left = jnp.concatenate(flow[0] + slope[0], axis=1)
    right = jnp.concatenate(flow[1] + slope[1], axis=1)
    z0[...], z1[...], z2[...] = x_inverse(left, right, 4, untable_ref)
    twiddle = twiddle_ref[...]
    for block in range(4):
        rows = slice(8 * block, 8 * block + 8)

        def physical(field):
            return real_synthesis(*modes_of(z0, z1, z2, field, rows, twiddle))

        east, slope_x = physical(0), physical(2)
        product = [a * b for a, b in zip(east, slope_x)]
        north, slope_y = physical(1), physical(3)
        product = [p + a * b for p, a, b in zip(product, north, slope_y)]
        real, imag = real_analysis(product)
        for k in range(9):
            jac[0, k, rows, :] = real[k]
            if imag[k] is not None:
                jac[1, k, rows, :] = imag[k]
    real = [jac[0, k] for k in range(9)]
    imag = [None] + [jac[1, k] for k in range(1, 8)] + [None]
    store_x(out_ref, x_forward(real, imag, twiddle, table_ref))


def tendency_kernel(
    in_ref, spec_ref, radix_ref, unradix_ref, turn_ref, lanes_ref, unlanes_ref, facts_ref, out_ref
):
    facts = facts_ref[...]
    flux = y_forward(load_pieces(in_ref), radix_ref, turn_ref, lanes_ref, facts)
    wave_x = x_waves(facts, lax.axis_index("row"))
    wave_y = y_waves(facts)
    ratio = (wave_x * wave_x + wave_y * wave_y) * (1.0 / (KCUT * KCUT))
    ratio = ratio * ratio
    damping = HYPER_RATE * (ratio * ratio)
    weight = jnp.where(wave_x == 0.0, 0.5, 1.0)
    total = -(flux + damping * spec_ref[...]) * weight
    store_pieces(out_ref, y_inverse([total], unradix_ref, turn_ref, unlanes_ref))


def state_update_kernel(
    in_ref, state_ref, start_ref, twiddle_ref, untable_ref, tendency_ref, new_ref, z0, z1, z2
):
    groups = load_x(in_ref, 1)
    z0[...], z1[...], z2[...] = x_inverse(groups[0][0], groups[1][0], 1, untable_ref)
    twiddle = twiddle_ref[...]
    for block in range(4):
        rows = slice(8 * block, 8 * block + 8)
        tendency = real_synthesis(*modes_of(z0, z1, z2, 0, rows, twiddle))
        for a in range(16):
            columns = slice(128 * a, 128 * a + 128)
            tendency_ref[0, rows, columns] = tendency[a]
            new_ref[0, rows, columns] = 0.75 * start_ref[0, rows, columns] + 0.25 * (
                state_ref[0, rows, columns] + STEP_SIZE * tendency[a]
            )


VMEM = pl.BlockSpec(memory_space=pltpu.VMEM)
SMEM = pl.BlockSpec(memory_space=pltpu.SMEM)


def call(kernel, outs, operands, scalars=0, scratch=()):
    return pl.pallas_call(
        kernel,
        out_shape=[jax.ShapeDtypeStruct(shape, F32) for shape in outs],
        in_specs=[SMEM] * scalars + [VMEM] * (len(operands) - scalars),
        out_specs=[VMEM] * len(outs),
        scratch_shapes=[pltpu.VMEM(shape, F32) for shape in scratch],
        compiler_params=pltpu.CompilerParams(vmem_limit_bytes=40 * 1024 * 1024),
    )(*operands)


def exchange(chunks, devices):
    length = chunks.shape[0]
    sent = chunks.reshape(devices, 1, length * 128 // devices)
    return lax.all_to_all(sent, "row", split_axis=0, concat_axis=0, tiled=True).reshape(length, 128)


def per_device(state, start_state, to_modes, from_modes, deform):
    devices = lax.axis_size("row")
    turn_x = jnp.asarray(x_twiddle())
    forward_x = jnp.asarray(x_forward_table())
    inverse_x = jnp.asarray(x_inverse_table(False))
    inverse_ix = jnp.asarray(x_inverse_table(True))
    radix = jnp.asarray(y_radix_table())
    unradix = jnp.asarray(y_radix_inverse_table())
    turn_y = jnp.asarray(y_twiddle())
    lanes = jnp.asarray(y_lane_table())
    unlanes = jnp.asarray(y_lane_inverse_table())
    facts = jnp.asarray(lane_facts())

    one, two = (64 * CHUNK, 128), (128 * CHUNK, 128)
    (columns,) = call(state_kernel, [one], [state, turn_x, forward_x])
    columns = exchange(columns, devices)
    spectrum, slopes = call(
        spectrum_kernel,
        [(KAP, SPAN), two],
        [columns, radix, unradix, turn_y, lanes, unlanes, facts],
    )
    slopes = exchange(slopes, devices)
    gathered = lax.all_gather(spectrum, "layer", axis=0, tiled=False)
    (flow,) = call(
        stream_kernel,
        [two],
        [to_modes, from_modes, deform, gathered, unradix, turn_y, unlanes, facts],
        scalars=3,
    )
    flow = exchange(flow, devices)
    (flux,) = call(
        jacobian_kernel,
        [one],
        [flow, slopes, turn_x, inverse_ix, forward_x],
        scratch=[(512, 256)] * 3 + [(2, 9, ROWS, 128)],
    )
    flux = exchange(flux, devices)
    (total,) = call(
        tendency_kernel, [one], [flux, spectrum, radix, unradix, turn_y, lanes, unlanes, facts]
    )
    total = exchange(total, devices)
    return tuple(
        call(
            state_update_kernel,
            [(1, ROWS, GRID)] * 2,
            [total, state, start_state, turn_x, inverse_x],
            scratch=[(128, 256)] * 3,
        )
    )


def solution(mesh):
    in_specs = (P("layer", "row", None), P("layer", "row", None), P(), P(), P())
    out_specs = (P("layer", "row", None), P("layer", "row", None))
    return jax.shard_map(
        per_device, mesh=mesh, in_specs=in_specs, out_specs=out_specs, check_vma=False
    )
```

```python
import functools
import math

import jax
import jax.numpy as jnp
import ml_dtypes
import numpy as np
from jax import lax
from jax.experimental import pallas as pl
from jax.experimental.pallas import tpu as pltpu
from jax.sharding import PartitionSpec as P

GRID = 2048
KCUT = 672
ROWS = 32
HALF = 14
CHUNK = 6
KAP = 64
JP = 21
PIECE = 8 * JP
SPAN = 512
USED = 504
HYPER_RATE = 0.2
STEP_SIZE = 0.5
BF16 = jnp.bfloat16
F32 = jnp.float32


def halves(table):
    high = table.astype(ml_dtypes.bfloat16)
    low = (table - high.astype(np.float64)).astype(ml_dtypes.bfloat16)
    return np.stack([high, low])


def turn(numerator, denominator):
    angle = 2.0 * math.pi * (np.mod(numerator, denominator) / denominator)
    return np.cos(angle), np.sin(angle)


def x_forward_table():
    b = np.arange(128)
    table = np.zeros((2, 16, 8, 2, 128))
    for half in range(2):
        for tau in range(HALF):
            for j3 in range(3):
                c, s = turn((3 * tau + j3 - 42 * half) * b, 128)
                table[half, tau, j3, 0] = c
                table[half, tau, j3, 1] = s
                table[half, tau, 3 + j3, 0] = -s
                table[half, tau, 3 + j3, 1] = c
    return halves(table.reshape(2, 128, 256))


def x_inverse_table(times_i):
    b = np.arange(128)
    table = np.zeros((2, 2, 3, 16, 2, 128))
    for half in range(2):
        for tau in range(HALF):
            for j3 in range(3):
                c, s = turn((3 * tau + j3 - 42 * half) * b, 128)
                if times_i:
                    c, s = -s, c
                table[half, 0, j3, tau, 0] = c
                table[half, 0, j3, tau, 1] = s
                table[half, 1, j3, tau, 0] = -s
                table[half, 1, j3, tau, 1] = c
    return halves(table.reshape(192, 256) * (2.0 / (GRID * GRID)))


def x_twiddle():
    table = np.zeros((32, 128))
    c, s = turn(np.arange(9)[:, None] * np.arange(128)[None, :], GRID)
    table[0:9] = c
    table[16:25] = s
    return table.astype(np.float32)


def y_radix_table():
    c, s = turn(np.arange(KAP)[:, None] * np.arange(64)[None, :] + 32 * np.arange(64)[None, :], 64)
    return halves(np.block([[c, s], [-s, c]]))


def y_radix_inverse_table():
    c, s = turn(np.arange(64)[:, None] * np.arange(KAP)[None, :] + 32 * np.arange(64)[:, None], 64)
    return halves(np.block([[c, -s], [s, c]]))


def y_twiddle():
    c, s = turn((np.arange(KAP)[:, None] - KCUT) * np.arange(ROWS)[None, :], GRID)
    return np.stack([np.tile(c, (1, 4)), np.tile(s, (1, 4))]).astype(np.float32)


def y_lane_table():
    c, s = turn(np.arange(ROWS)[:, None] * np.arange(JP)[None, :], ROWS)
    table = np.zeros((3, 2, 4, ROWS, 256))
    for j3 in range(3):
        for slot in range(4):
            re = 40 * j3 + slot * JP
            im = re + 4 * JP
            table[j3, 0, slot, :, re : re + JP] = c
            table[j3, 1, slot, :, re : re + JP] = s
            table[j3, 0, slot, :, im : im + JP] = -s
            table[j3, 1, slot, :, im : im + JP] = c
    return halves(table.reshape(3, 256, 256))


def y_lane_inverse_table():
    high, low = y_lane_table()
    return np.stack([np.swapaxes(high, 1, 2), np.swapaxes(low, 1, 2)])


def lane_facts():
    lane = np.arange(SPAN)
    j3 = lane // PIECE
    slot = (lane % (4 * JP)) // JP
    facts = np.zeros((8, SPAN))
    facts[0] = 16 * j3
    facts[1] = slot
    facts[2] = 64 * (lane % JP) - KCUT
    facts[3] = slot == 0
    return facts.astype(np.float32)


def split(value):
    high = value.astype(BF16)
    low = (value - high.astype(F32)).astype(BF16)
    return high, low


def matmul(left, right, dims):
    def one(a, b):
        return lax.dot_general(a, b, (dims, ((), ())), preferred_element_type=F32)

    return one(left[0], right[0]) + (one(left[0], right[1]) + one(left[1], right[0]))


NN = ((1,), (0,))
NT = ((1,), (1,))
TN = ((0,), (0,))

C1 = math.cos(math.pi / 8)
C2 = math.cos(math.pi / 4)
C3 = math.cos(3 * math.pi / 8)


def real_analysis(x):
    s = [x[a] + x[a + 8] for a in range(8)]
    d = [x[a] - x[a + 8] for a in range(8)]
    e = [None] + [d[a] - d[8 - a] for a in range(1, 4)]
    f = [None] + [d[a] + d[8 - a] for a in range(1, 4)]
    e2, f2 = e[2] * C2, f[2] * C2
    plus, minus = d[0] + e2, d[0] - e2
    first, second = e[1] * C1 + e[3] * C3, e[1] * C3 - e[3] * C1
    third, fourth = f[1] * C3 + f[3] * C1, f[1] * C1 - f[3] * C3
    u, v = d[4] + f2, f2 - d[4]
    p = [s[a] + s[a + 4] for a in range(4)]
    q = [s[a] - s[a + 4] for a in range(4)]
    even, odd = p[0] + p[2], p[1] + p[3]
    hd, hs = (q[1] - q[3]) * C2, (q[1] + q[3]) * C2
    real = [
        even + odd,
        plus + first,
        q[0] + hd,
        minus + second,
        p[0] - p[2],
        minus - second,
        q[0] - hd,
        plus - first,
        even - odd,
    ]
    imag = [
        None,
        -(third + u),
        -(q[2] + hs),
        -(fourth + v),
        p[3] - p[1],
        v - fourth,
        q[2] - hs,
        u - third,
        None,
    ]
    return real, imag


def real_synthesis(real, imag):
    plus, first = real[1] + real[7], real[1] - real[7]
    minus, second = real[3] + real[5], real[3] - real[5]
    third, u = -(imag[1] + imag[7]), imag[7] - imag[1]
    fourth, v = -(imag[3] + imag[5]), imag[5] - imag[3]
    d = [None] * 8
    d[0], d[4] = plus + minus, u - v
    e = [None, first * C1 + second * C3, (plus - minus) * C2, first * C3 - second * C1]
    f = [None, third * C3 + fourth * C1, (u + v) * C2, third * C1 - fourth * C3]
    for a in range(1, 4):
        d[a], d[8 - a] = f[a] + e[a], f[a] - e[a]
    even, odd = real[0] + real[8], real[0] - real[8]
    p = [even + real[4], odd - imag[4], even - real[4], odd + imag[4]]
    hr, hi = (real[2] - real[6]) * C2, (imag[2] + imag[6]) * C2
    q = [real[2] + real[6], hr - hi, imag[6] - imag[2], -(hr + hi)]
    s = [p[a] + q[a] for a in range(4)] + [p[a] - q[a] for a in range(4)]
    return [s[a] + d[a] for a in range(8)] + [s[a] - d[a] for a in range(8)]


def x_forward(real, imag, twiddle, table):
    pieces = []
    for k in range(9):
        if k == 0:
            pieces.append(jnp.concatenate([real[0], jnp.zeros_like(real[0])], axis=1))
            continue
        c, s = twiddle[k : k + 1], twiddle[16 + k : 17 + k]
        if k == 8:
            re, im = real[8] * c, -(real[8] * s)
        else:
            re, im = real[k] * c + imag[k] * s, imag[k] * c - real[k] * s
        pieces.append(jnp.concatenate([re, im], axis=1))
    shared = split(jnp.concatenate(pieces[1:8], axis=0))
    results = []
    for half, own in enumerate((pieces[0], pieces[8])):
        own = split(own)
        right = [jnp.concatenate([own[i], shared[i]], axis=0) for i in range(2)]
        results.append(matmul([table[0, half], table[1, half]], right, NT))
    return results


def x_inverse(left, right, fields, table):
    left = split(left)
    right = split(right)
    upper = [table[i][:96] for i in range(2)]
    lower = [table[i][96:] for i in range(2)]
    first = matmul([part[:96] for part in left], upper, TN)
    second = matmul([part[96:] for part in left], lower, TN)
    rest = matmul(right, [table[i] for i in range(2)], TN)
    return first, second, rest


def modes_of(first, second, rest, field, rows, twiddle):
    real, imag = [], []
    for k in range(9):
        c, s = twiddle[k : k + 1], twiddle[16 + k : 17 + k]
        base = field * 128 + rows.start
        size = rows.stop - rows.start
        if k in (0, 8):
            source = first if k == 0 else second
            z = source[base : base + size]
        elif k < 4:
            start = base + 32 * k
            z = first[start : start + size] + second[start : start + size]
        else:
            start = base + 32 * (k - 4)
            z = rest[start : start + size]
        re, im = z[:, :128], z[:, 128:]
        if k == 0:
            real.append(re)
            imag.append(None)
        else:
            real.append(re * c - im * s)
            imag.append(None if k == 8 else re * s + im * c)
    return real, imag


def y_forward(pieces, radix, twiddle, lanes, facts):
    stacked = jnp.concatenate(
        [jnp.concatenate(pieces[0], axis=1), jnp.concatenate(pieces[1], axis=1)], axis=0
    )
    mixed = matmul([radix[0], radix[1]], split(stacked), NN)
    c, s = twiddle[0], twiddle[1]
    windows = []
    for j3 in range(3):
        re, im = mixed[:KAP, 128 * j3 : 128 * j3 + 128], mixed[KAP:, 128 * j3 : 128 * j3 + 128]
        turned = jnp.concatenate([re * c + im * s, im * c - re * s], axis=1)
        windows.append(matmul(split(turned), [lanes[0, j3], lanes[1, j3]], NN))
    first, second, third = windows
    spectrum = jnp.concatenate(
        [
            first[:, :128],
            first[:, 128:] + second[:, :128],
            second[:, 128:] + third[:, :128],
            third[:, 128:],
        ],
        axis=1,
    )
    wave_y = y_waves(facts)
    return jnp.where(wave_y > -KCUT, spectrum, 0.0)


def y_waves(facts):
    kap = lax.broadcasted_iota(jnp.int32, (KAP, 1), 0).astype(F32)
    return kap + facts[2:3]


def x_waves(facts, owner):
    group = owner // 32
    half = (owner % 32) // 16
    tau = owner % 16
    base = (4 * group + 16 * (3 * tau - 42 * half)).astype(F32)
    shift = (8 * half * (1 - group)).astype(F32)
    return facts[0:1] + facts[1:2] + base + shift * facts[3:4]


def y_inverse(spectra, radix, twiddle, lanes):
    count = len(spectra)
    stacked = split(jnp.concatenate(spectra, axis=0) if count > 1 else spectra[0])
    c, s = twiddle[0], twiddle[1]
    real, imag = [], []
    for j3 in range(3):
        window = [part[:, 128 * j3 : 128 * j3 + 256] for part in stacked]
        out = matmul(window, [lanes[0, j3], lanes[1, j3]], NN)
        for field in range(count):
            own = out[KAP * field : KAP * field + KAP]
            re, im = own[:, :128], own[:, 128:]
            real.append(re * c - im * s)
            imag.append(re * s + im * c)
    right = split(
        jnp.concatenate([jnp.concatenate(real, axis=1), jnp.concatenate(imag, axis=1)], axis=0)
    )
    out = matmul([radix[0], radix[1]], right, NN)
    fields = []
    for field in range(count):
        columns = [slice(128 * (count * j3 + field), 128 * (count * j3 + field) + 128) for j3 in range(3)]
        fields.append([[out[:64, own] for own in columns], [out[64:, own] for own in columns]])
    return fields


def stream_function(gathered, to_modes, from_modes, deform, layer, square):
    weights = [from_modes(layer, m) * (-1.0 / (square + deform(m))) for m in range(8)]
    total = None
    for n in range(8):
        factor = None
        for m in range(8):
            term = weights[m] * to_modes(m, n)
            factor = term if factor is None else factor + term
        term = factor * gathered(n)
        total = term if total is None else total + term
    return total


def store_x(out_ref, results):
    for half in range(2):
        for group in range(2):
            block = results[half][:, 128 * group : 128 * group + 128]
            for tau in range(16):
                start = (32 * group + 16 * half + tau) * CHUNK
                out_ref[start : start + CHUNK, :] = block[8 * tau : 8 * tau + CHUNK]


def load_pieces(ref):
    return [
        [ref[pl.ds(3 * part + j3, 64, stride=CHUNK), :] for j3 in range(3)] for part in range(2)
    ]


def store_pieces(ref, fields):
    stride = CHUNK * len(fields)
    for field, pieces in enumerate(fields):
        for part in range(2):
            for j3 in range(3):
                ref[pl.ds(CHUNK * field + 3 * part + j3, 64, stride=stride), :] = pieces[part][j3]


def load_x(ref, fields):
    stride = CHUNK * fields
    groups = []
    for group in range(2):
        columns = []
        for field in range(fields):
            rows = []
            for half in range(2):
                for part in range(CHUNK):
                    start = (32 * group + 16 * half) * stride + CHUNK * field + part
                    rows.append(ref[pl.ds(start, 16, stride=stride), :])
            columns.append(jnp.concatenate(rows, axis=0))
        groups.append(columns)
    return groups


def state_kernel(state_hbm, twiddle_hbm, table_hbm, out_ref, state_ref, twiddle_ref, table_ref, sems):
    pairs = ((state_hbm, state_ref), (twiddle_hbm, twiddle_ref), (table_hbm, table_ref))
    copies = [pltpu.make_async_copy(a, b, sems.at[i]) for i, (a, b) in enumerate(pairs)]
    for copy in copies:
        copy.start()
    for copy in copies:
        copy.wait()
    x = [state_ref[0, :, 128 * a : 128 * a + 128] for a in range(16)]
    real, imag = real_analysis(x)
    store_x(out_ref, x_forward(real, imag, twiddle_ref[...], table_ref))


def spectrum_kernel(in_ref, radix_ref, turn_ref, lanes_ref, facts_ref, spec_ref, used_ref):
    facts = facts_ref[...]
    spectrum = y_forward(load_pieces(in_ref), radix_ref, turn_ref, lanes_ref, facts)
    spec_ref[...] = spectrum
    used_ref[...] = spectrum[:, :USED]


def stream_kernel(
    to_ref,
    from_ref,
    deform_ref,
    all_ref,
    spec_ref,
    unradix_ref,
    turn_ref,
    unlanes_ref,
    facts_ref,
    out_ref,
    stream_ref,
):
    facts = facts_ref[...]
    wave_x = x_waves(facts, lax.axis_index("row"))
    wave_y = y_waves(facts)
    square = (wave_x * wave_x + wave_y * wave_y)[:, :USED]
    stream = stream_function(
        lambda n: all_ref[n],
        lambda m, n: to_ref[m, n],
        lambda l, m: from_ref[l, m],
        lambda m: deform_ref[m],
        lax.axis_index("layer"),
        square,
    )
    stream_ref[:, SPAN - 128 :] = jnp.zeros((KAP, 128), F32)
    stream_ref[:, :USED] = stream
    stream = stream_ref[...]
    spectrum = spec_ref[...]
    along_y = wave_y * jnp.where(wave_x == 0.0, 0.5, 1.0)
    fields = [-along_y * stream, wave_x * stream, wave_x * spectrum, along_y * spectrum]
    store_pieces(out_ref, y_inverse(fields, unradix_ref, turn_ref, unlanes_ref))


def jacobian_kernel(in_ref, twiddle_ref, untable_ref, table_ref, out_ref, z0, z1, z2, jac):
    groups = load_x(in_ref, 4)
    left = jnp.concatenate(groups[0], axis=1)
    right = jnp.concatenate(groups[1], axis=1)
    z0[...], z1[...], z2[...] = x_inverse(left, right, 4, untable_ref)
    twiddle = twiddle_ref[...]
    for block in range(4):
        rows = slice(8 * block, 8 * block + 8)

        def physical(field):
            return real_synthesis(*modes_of(z0, z1, z2, field, rows, twiddle))

        east, slope_x = physical(0), physical(2)
        product = [a * b for a, b in zip(east, slope_x)]
        north, slope_y = physical(1), physical(3)
        product = [p + a * b for p, a, b in zip(product, north, slope_y)]
        real, imag = real_analysis(product)
        for k in range(9):
            jac[0, k, rows, :] = real[k]
            if imag[k] is not None:
                jac[1, k, rows, :] = imag[k]
    real = [jac[0, k] for k in range(9)]
    imag = [None] + [jac[1, k] for k in range(1, 8)] + [None]
    store_x(out_ref, x_forward(real, imag, twiddle, table_ref))


def tendency_kernel(
    in_ref, spec_ref, radix_ref, unradix_ref, turn_ref, lanes_ref, unlanes_ref, facts_ref, out_ref
):
    facts = facts_ref[...]
    flux = y_forward(load_pieces(in_ref), radix_ref, turn_ref, lanes_ref, facts)
    wave_x = x_waves(facts, lax.axis_index("row"))
    wave_y = y_waves(facts)
    ratio = (wave_x * wave_x + wave_y * wave_y) * (1.0 / (KCUT * KCUT))
    ratio = ratio * ratio
    damping = HYPER_RATE * (ratio * ratio)
    weight = jnp.where(wave_x == 0.0, 0.5, 1.0)
    total = -(flux + damping * spec_ref[...]) * weight
    store_pieces(out_ref, y_inverse([total], unradix_ref, turn_ref, unlanes_ref))


def state_update_kernel(
    in_ref, state_ref, start_ref, twiddle_ref, untable_ref, tendency_ref, new_ref, z0, z1, z2
):
    groups = load_x(in_ref, 1)
    z0[...], z1[...], z2[...] = x_inverse(groups[0][0], groups[1][0], 1, untable_ref)
    twiddle = twiddle_ref[...]
    for block in range(4):
        rows = slice(8 * block, 8 * block + 8)
        tendency = real_synthesis(*modes_of(z0, z1, z2, 0, rows, twiddle))
        for a in range(16):
            columns = slice(128 * a, 128 * a + 128)
            tendency_ref[0, rows, columns] = tendency[a]
            new_ref[0, rows, columns] = 0.75 * start_ref[0, rows, columns] + 0.25 * (
                state_ref[0, rows, columns] + STEP_SIZE * tendency[a]
            )


VMEM = pl.BlockSpec(memory_space=pltpu.VMEM)
SMEM = pl.BlockSpec(memory_space=pltpu.SMEM)
ANY = pl.BlockSpec(memory_space=pl.ANY)


def call(kernel, outs, operands, scalars=0, scratch=(), fetched=False):
    if fetched:
        in_specs = [ANY] * len(operands)
        scratch_shapes = [pltpu.VMEM(operand.shape, operand.dtype) for operand in operands]
        scratch_shapes.append(pltpu.SemaphoreType.DMA((len(operands),)))
    else:
        in_specs = [SMEM] * scalars + [VMEM] * (len(operands) - scalars)
        scratch_shapes = [pltpu.VMEM(shape, F32) for shape in scratch]
    return pl.pallas_call(
        kernel,
        out_shape=[jax.ShapeDtypeStruct(shape, F32) for shape in outs],
        in_specs=in_specs,
        out_specs=[VMEM] * len(outs),
        scratch_shapes=scratch_shapes,
        compiler_params=pltpu.CompilerParams(vmem_limit_bytes=40 * 1024 * 1024),
    )(*operands)


def exchange(chunks, devices):
    length = chunks.shape[0]
    sent = chunks.reshape(devices, 1, length * 128 // devices)
    return lax.all_to_all(sent, "row", split_axis=0, concat_axis=0, tiled=True).reshape(length, 128)


def per_device(state, start_state, to_modes, from_modes, deform):
    devices = lax.axis_size("row")
    turn_x = jnp.asarray(x_twiddle())
    forward_x = jnp.asarray(x_forward_table())
    inverse_x = jnp.asarray(x_inverse_table(False))
    inverse_ix = jnp.asarray(x_inverse_table(True))
    radix = jnp.asarray(y_radix_table())
    unradix = jnp.asarray(y_radix_inverse_table())
    turn_y = jnp.asarray(y_twiddle())
    lanes = jnp.asarray(y_lane_table())
    unlanes = jnp.asarray(y_lane_inverse_table())
    facts = jnp.asarray(lane_facts())

    one, four = (64 * CHUNK, 128), (256 * CHUNK, 128)
    (columns,) = call(state_kernel, [one], [state, turn_x, forward_x], fetched=True)
    columns = exchange(columns, devices)
    spectrum, used = call(
        spectrum_kernel, [(KAP, SPAN), (KAP, USED)], [columns, radix, turn_y, lanes, facts]
    )
    gathered = lax.all_gather(used, "layer", axis=0, tiled=False)
    (fields,) = call(
        stream_kernel,
        [four],
        [to_modes, from_modes, deform, gathered, spectrum, unradix, turn_y, unlanes, facts],
        scalars=3,
        scratch=[(KAP, SPAN)],
    )
    fields = exchange(fields, devices)
    (flux,) = call(
        jacobian_kernel,
        [one],
        [fields, turn_x, inverse_ix, forward_x],
        scratch=[(512, 256)] * 3 + [(2, 9, ROWS, 128)],
    )
    flux = exchange(flux, devices)
    (total,) = call(
        tendency_kernel, [one], [flux, spectrum, radix, unradix, turn_y, lanes, unlanes, facts]
    )
    total = exchange(total, devices)
    return tuple(
        call(
            state_update_kernel,
            [(1, ROWS, GRID)] * 2,
            [total, state, start_state, turn_x, inverse_x],
            scratch=[(128, 256)] * 3,
        )
    )


def solution(mesh):
    in_specs = (P("layer", "row", None), P("layer", "row", None), P(), P(), P())
    out_specs = (P("layer", "row", None), P("layer", "row", None))
    return jax.shard_map(
        per_device, mesh=mesh, in_specs=in_specs, out_specs=out_specs, check_vma=False
    )
```

```python
import functools
import math

import jax
import jax.numpy as jnp
import ml_dtypes
import numpy as np
from jax import lax
from jax.experimental import pallas as pl
from jax.experimental.pallas import tpu as pltpu
from jax.sharding import PartitionSpec as P

GRID = 2048
KCUT = 672
ROWS = 32
HALF = 14
CHUNK = 6
KAP = 64
JP = 21
USED = 6 * JP
WIDE = 256
FIELDS = 4
HYPER_RATE = 0.2
STEP_SIZE = 0.5
BF16 = jnp.bfloat16
F32 = jnp.float32


def halves(table):
    high = table.astype(ml_dtypes.bfloat16)
    low = (table - high.astype(np.float64)).astype(ml_dtypes.bfloat16)
    return np.stack([high, low])


def turn(numerator, denominator):
    angle = 2.0 * math.pi * (np.mod(numerator, denominator) / denominator)
    return np.cos(angle), np.sin(angle)


def x_forward_table(apart):
    b = np.arange(128)
    table = np.zeros((2, 3, 16, 2, 2, 128))
    for half in range(2):
        for tau in range(HALF):
            for j3 in range(3):
                c, s = turn((3 * tau + j3 - 42 * half) * b, 128)
                table[half, j3, tau, 0, 0] = c
                table[half, j3, tau, 0, 1] = s
                table[half, j3, tau, 1, 0] = -s
                table[half, j3, tau, 1, 1] = c
    if apart:
        table = np.swapaxes(table, 2, 3)
    return halves(table.reshape(2, 96, 256))


def x_inverse_table(times_i):
    b = np.arange(128)
    table = np.zeros((2, 2, 3, 16, 2, 128))
    for half in range(2):
        for tau in range(HALF):
            for j3 in range(3):
                c, s = turn((3 * tau + j3 - 42 * half) * b, 128)
                if times_i:
                    c, s = -s, c
                table[half, 0, j3, tau, 0] = c
                table[half, 0, j3, tau, 1] = s
                table[half, 1, j3, tau, 0] = -s
                table[half, 1, j3, tau, 1] = c
    return halves(table.reshape(192, 256) * (2.0 / (GRID * GRID)))


def x_twiddle():
    table = np.zeros((32, 128))
    c, s = turn(np.arange(9)[:, None] * np.arange(128)[None, :], GRID)
    table[0:9] = c
    table[16:25] = s
    return table.astype(np.float32)


def paired(table):
    high, low = halves(table)
    return np.concatenate([high, high, low], axis=1)


def y_radix_table():
    c, s = turn(np.arange(KAP)[:, None] * np.arange(64)[None, :] + 32 * np.arange(64)[None, :], 64)
    return paired(np.block([[c, s], [-s, c]]))


def y_radix_inverse_table():
    c, s = turn(np.arange(64)[:, None] * np.arange(KAP)[None, :] + 32 * np.arange(64)[:, None], 64)
    return paired(np.block([[c, -s], [s, c]]))


def y_twiddle():
    c, s = turn((np.arange(KAP)[:, None] - KCUT) * np.arange(ROWS)[None, :], GRID)
    return np.stack([np.tile(c, (1, 4)), np.tile(s, (1, 4))]).astype(np.float32)


def lanes_of(block, j3):
    c, s = turn(np.arange(ROWS)[:, None] * np.arange(JP)[None, :], ROWS)
    table = np.zeros((2, 4, ROWS, 128))
    re = 2 * JP * j3
    im = re + JP
    table[0, block, :, re : re + JP] = c
    table[1, block, :, re : re + JP] = s
    table[0, block, :, im : im + JP] = -s
    table[1, block, :, im : im + JP] = c
    return table.reshape(256, 128)


def y_lane_table():
    return halves(sum(lanes_of(j3, j3) for j3 in range(3)))


def y_lane_inverse_table():
    own = sum(lanes_of(j3, j3) for j3 in range(3)).T
    return halves(np.stack([np.concatenate([own, lanes_of(3, f).T], axis=0) for f in range(3)]))


def y_projection_table():
    difference = np.arange(ROWS)[None, :] - np.arange(ROWS)[:, None]
    c, s = turn(difference[:, :, None] * np.arange(JP)[None, None, :], ROWS)
    c, s = np.kron(np.eye(4), c.sum(-1)), np.kron(np.eye(4), s.sum(-1))
    return halves(np.block([[c, s], [-s, c]]))


def y_mean_table():
    return np.kron(np.eye(8), np.ones((ROWS, ROWS))).astype(ml_dtypes.bfloat16)


def lane_facts():
    lane = np.arange(128)
    facts = np.zeros((8, 128))
    facts[0] = 16 * (lane // (2 * JP))
    facts[1] = 64 * (lane % JP) - KCUT
    return facts.astype(np.float32)


def split(value):
    high = value.astype(BF16)
    low = (value - high.astype(F32)).astype(BF16)
    return high, low


def matmul(left, right, dims):
    def one(a, b):
        return lax.dot_general(a, b, (dims, ((), ())), preferred_element_type=F32)

    return one(left[0], right[0]) + (one(left[0], right[1]) + one(left[1], right[0]))


def matmul_deep(table, right):
    depth = right[0].shape[0]

    def one(a, b):
        return lax.dot_general(a, b, (NN, ((), ())), preferred_element_type=F32)

    both = jnp.concatenate(right, axis=0)
    return one(table[:, : 2 * depth], both) + one(table[:, 2 * depth :], right[0])


NN = ((1,), (0,))
NT = ((1,), (1,))
TN = ((0,), (0,))

C1 = math.cos(math.pi / 8)
C2 = math.cos(math.pi / 4)
C3 = math.cos(3 * math.pi / 8)


def real_analysis(x):
    s = [x[a] + x[a + 8] for a in range(8)]
    d = [x[a] - x[a + 8] for a in range(8)]
    e = [None] + [d[a] - d[8 - a] for a in range(1, 4)]
    f = [None] + [d[a] + d[8 - a] for a in range(1, 4)]
    e2, f2 = e[2] * C2, f[2] * C2
    plus, minus = d[0] + e2, d[0] - e2
    first, second = e[1] * C1 + e[3] * C3, e[1] * C3 - e[3] * C1
    third, fourth = f[1] * C3 + f[3] * C1, f[1] * C1 - f[3] * C3
    u, v = d[4] + f2, f2 - d[4]
    p = [s[a] + s[a + 4] for a in range(4)]
    q = [s[a] - s[a + 4] for a in range(4)]
    even, odd = p[0] + p[2], p[1] + p[3]
    hd, hs = (q[1] - q[3]) * C2, (q[1] + q[3]) * C2
    real = [
        even + odd,
        plus + first,
        q[0] + hd,
        minus + second,
        p[0] - p[2],
        minus - second,
        q[0] - hd,
        plus - first,
        even - odd,
    ]
    imag = [
        None,
        -(third + u),
        -(q[2] + hs),
        -(fourth + v),
        p[3] - p[1],
        v - fourth,
        q[2] - hs,
        u - third,
        None,
    ]
    return real, imag


def real_synthesis(real, imag):
    plus, first = real[1] + real[7], real[1] - real[7]
    minus, second = real[3] + real[5], real[3] - real[5]
    third, u = -(imag[1] + imag[7]), imag[7] - imag[1]
    fourth, v = -(imag[3] + imag[5]), imag[5] - imag[3]
    d = [None] * 8
    d[0], d[4] = plus + minus, u - v
    e = [None, first * C1 + second * C3, (plus - minus) * C2, first * C3 - second * C1]
    f = [None, third * C3 + fourth * C1, (u + v) * C2, third * C1 - fourth * C3]
    for a in range(1, 4):
        d[a], d[8 - a] = f[a] + e[a], f[a] - e[a]
    even, odd = real[0] + real[8], real[0] - real[8]
    p = [even + real[4], odd - imag[4], even - real[4], odd + imag[4]]
    hr, hi = (real[2] - real[6]) * C2, (imag[2] + imag[6]) * C2
    q = [real[2] + real[6], hr - hi, imag[6] - imag[2], -(hr + hi)]
    s = [p[a] + q[a] for a in range(4)] + [p[a] - q[a] for a in range(4)]
    return [s[a] + d[a] for a in range(8)] + [s[a] - d[a] for a in range(8)]


def regroup(blocks, wanted):
    block = lax.broadcasted_iota(jnp.int32, (1, 128), 1) // 32
    turned = [
        b if b is None or i == 0 else pltpu.roll(b, 32 * i, 1) for i, b in enumerate(blocks)
    ]
    results = []
    for p in wanted:
        total = None
        for i in range(4):
            part = jnp.zeros_like(turned[0]) if turned[i] is None else turned[i]
            total = part if total is None else jnp.where(block == (p + i) % 4, part, total)
        results.append(total if p == 0 else pltpu.roll(total, 128 - 32 * p, 1))
    return results


def x_forward(real, imag, twiddle, table):
    pieces = []
    for k in range(9):
        if k == 0:
            pieces.append(jnp.concatenate([real[0], jnp.zeros_like(real[0])], axis=1))
            continue
        c, s = twiddle[k : k + 1], twiddle[16 + k : 17 + k]
        if k == 8:
            re, im = real[8] * c, -(real[8] * s)
        else:
            re, im = real[k] * c + imag[k] * s, imag[k] * c - real[k] * s
        pieces.append(jnp.concatenate([re, im], axis=1))
    shared = split(jnp.concatenate(pieces[1:8], axis=0))
    results = []
    for half, own in enumerate((pieces[0], pieces[8])):
        own = split(own)
        right = [jnp.concatenate([own[i], shared[i]], axis=0) for i in range(2)]
        results.append(matmul([table[0, half], table[1, half]], right, NT))
    return results


def x_inverse(left, right, fields, table):
    left = split(left)
    right = split(right)
    upper = [table[i][:96] for i in range(2)]
    lower = [table[i][96:] for i in range(2)]
    first = matmul([part[:96] for part in left], upper, TN)
    second = matmul([part[96:] for part in left], lower, TN)
    rest = matmul(right, [table[i] for i in range(2)], TN)
    return first, second, rest


def modes_of(first, second, rest, field, rows, twiddle):
    real, imag = [], []
    for k in range(9):
        c, s = twiddle[k : k + 1], twiddle[16 + k : 17 + k]
        base = field * 128 + rows.start
        size = rows.stop - rows.start
        if k in (0, 8):
            source = first if k == 0 else second
            z = source[base : base + size]
        elif k < 4:
            start = base + 32 * k
            z = first[start : start + size] + second[start : start + size]
        else:
            start = base + 32 * (k - 4)
            z = rest[start : start + size]
        re, im = z[:, :128], z[:, 128:]
        if k == 0:
            real.append(re)
            imag.append(None)
        else:
            real.append(re * c - im * s)
            imag.append(None if k == 8 else re * s + im * c)
    return real, imag


def turn_by(re, im, c, s):
    return re * c + im * s, im * c - re * s


def retained_y(facts):
    kap = lax.broadcasted_iota(jnp.int32, (KAP, 1), 0).astype(F32)
    return kap + facts[1:2]


def place():
    layer = lax.axis_index("layer")
    return layer // 2, layer % 2, lax.axis_index("row")


def x_waves(facts, z, place_index):
    group = place_index // 32
    half = (place_index % 32) // 16
    tau = place_index % 16
    eight = jnp.where((group == 0) & (z == 0), 8 * half, 0)
    return facts[0:1] + (4 * group + z + eight + 16 * (3 * tau - 42 * half)).astype(F32)


def store_wide(out_ref, results):
    for half in range(2):
        for group in range(2):
            lanes = slice(128 * group, 128 * group + 128)
            blocks = [results[half][32 * j3 : 32 * j3 + 32, lanes] for j3 in range(3)] + [None]
            for z, block in enumerate(regroup(blocks, range(4))):
                start = 2 * (64 * z + 32 * group + 16 * half)
                out_ref[start : start + 32, :] = block


def state_kernel(
    state_hbm,
    twiddle_hbm,
    table_hbm,
    to_hbm,
    from_hbm,
    deform_hbm,
    out_ref,
    scalars_ref,
    state_ref,
    twiddle_ref,
    table_ref,
    to_ref,
    from_ref,
    deform_ref,
    sems,
):
    pairs = (
        (state_hbm, state_ref),
        (twiddle_hbm, twiddle_ref),
        (table_hbm, table_ref),
        (to_hbm, to_ref),
        (from_hbm, from_ref),
        (deform_hbm, deform_ref),
    )
    copies = [pltpu.make_async_copy(a, b, sems.at[i]) for i, (a, b) in enumerate(pairs)]
    for copy in copies:
        copy.start()
    for copy in copies:
        copy.wait()
    x = [state_ref[0, :, 128 * a : 128 * a + 128] for a in range(16)]
    real, imag = real_analysis(x)
    store_wide(out_ref, x_forward(real, imag, twiddle_ref[...], table_ref))
    for n in range(8):
        scalars_ref[8 * n : 8 * n + 8, :] = jnp.broadcast_to(to_ref[:, n : n + 1], (8, 128))
        start = 64 + 8 * n
        scalars_ref[start : start + 8, :] = jnp.broadcast_to(from_ref[:, n : n + 1], (8, 128))
    equal = lax.broadcasted_iota(jnp.int32, (8, 8), 0) == lax.broadcasted_iota(jnp.int32, (8, 8), 1)
    column = jnp.sum(jnp.where(equal, deform_ref[...], 0.0), axis=1, keepdims=True)
    scalars_ref[128:136, :] = jnp.broadcast_to(column, (8, 128))


def spectrum_kernel(in_ref, radix_ref, turn_ref, lanes_ref, facts_ref, spec_ref):
    def rows(part):
        return jnp.concatenate(
            [in_ref[pl.ds(128 * z + part, 64, stride=2), :] for z in range(4)], axis=1
        )

    mixed = matmul_deep(radix_ref, split(jnp.concatenate([rows(0), rows(1)], axis=0)))
    c, s = turn_ref[0], turn_ref[1]
    turned = []
    for z in range(4):
        lanes = slice(128 * z, 128 * z + 128)
        turned.append(jnp.concatenate(turn_by(mixed[:KAP, lanes], mixed[KAP:, lanes], c, s), axis=1))
    spectrum = matmul(split(jnp.concatenate(turned, axis=0)), lanes_ref, NN)
    wave_y = retained_y(facts_ref[...])
    for z in range(4):
        own = jnp.where(wave_y > -KCUT, spectrum[64 * z : 64 * z + 64], 0.0)
        spec_ref[64 * z : 64 * z + 64, :] = own[:, :USED]


def stream_kernel(
    scalars_ref, all_ref, unradix_ref, turn_ref, unlanes_ref, facts_ref, out_ref, full_ref
):
    z_own, core, row = place()
    for i in range(2):
        rows = slice(256 * i, 256 * i + 256)
        full_ref[rows, :] = jnp.zeros((256, 128), F32)
        full_ref[rows, :USED] = all_ref[i]

    def scalar(index):
        return scalars_ref[pl.ds(index, 1), :]

    facts = facts_ref[...]
    wave_x = x_waves(facts, z_own, row)
    wave_y = retained_y(facts)
    square = wave_x * wave_x + wave_y * wave_y
    modal = []
    for m in range(8):
        total = None
        for n in range(8):
            start = 256 * (n % 2) + 64 * (n // 2)
            term = scalar(8 * n + m) * full_ref[start : start + 64, :]
            total = term if total is None else total + term
        modal.append(total * (-1.0 / (square + scalar(128 + m))))
    ratio = square * (1.0 / (KCUT * KCUT))
    ratio = ratio * ratio
    weight = jnp.where(wave_x == 0.0, 0.5, 1.0)
    damping = (-HYPER_RATE * weight) * (ratio * ratio)
    along_y = wave_y * weight
    fields = [[] for _ in range(5)]
    for z in range(4):
        stream = None
        for m in range(8):
            term = scalar(64 + 8 * m + 2 * z + core) * modal[m]
            stream = term if stream is None else stream + term
        own = full_ref[pl.ds(256 * core + 64 * z, 64), :]
        fields[0].append(-along_y * stream)
        fields[1].append(wave_x * stream)
        fields[2].append(wave_x * own)
        fields[3].append(along_y * own)
        fields[4].append(damping * own)
    fields = [split(jnp.concatenate(field, axis=0)) for field in fields]
    c, s = turn_ref[0], turn_ref[1]
    for f in range(FIELDS):
        if f < 3:
            left = [jnp.concatenate([fields[f][i], fields[4][i]], axis=1) for i in range(2)]
            out = matmul(left, [unlanes_ref[i, f] for i in range(2)], NN)
        else:
            out = matmul(fields[f], [unlanes_ref[i, 0, :128] for i in range(2)], NN)
        real, imag = [], []
        for z in range(4):
            own = out[64 * z : 64 * z + 64]
            re, im = turn_by(own[:, :128], own[:, 128:], c, -s)
            real.append(re)
            imag.append(im)
        right = jnp.concatenate(
            [jnp.concatenate(real, axis=1), jnp.concatenate(imag, axis=1)], axis=0
        )
        out = matmul_deep(unradix_ref, split(right))
        for z in range(4):
            for part in range(2):
                out_ref[pl.ds(512 * z + 2 * f + part, 64, stride=8), :] = out[
                    64 * part : 64 * part + 64, 128 * z : 128 * z + 128
                ]


def jacobian_kernel(
    in_ref, twiddle_ref, untable_ref, table_ref, out_ref, damp_ref, z0, z1, z2, jac
):
    sides = []
    for group in range(2):
        columns = []
        for f in range(FIELDS):
            parts = []
            for part in range(2):
                blocks = [
                    in_ref[pl.ds((64 * z + 32 * group) * 8 + 2 * f + part, 32, stride=8), :]
                    for z in range(4)
                ]
                found = regroup(blocks, range(4 if f < 3 else 3))
                if f < 3:
                    for half in range(2):
                        start = 192 * group + 96 * half + 48 * part + 16 * f
                        damp_ref[start : start + 16, :] = found[3][16 * half : 16 * half + 16]
                parts.append(found)
            rows = [
                parts[part][j3][16 * half : 16 * half + 16]
                for half in range(2)
                for part in range(2)
                for j3 in range(3)
            ]
            columns.append(jnp.concatenate(rows, axis=0))
        sides.append(jnp.concatenate(columns, axis=1))
    z0[...], z1[...], z2[...] = x_inverse(sides[0], sides[1], 4, untable_ref)
    twiddle = twiddle_ref[...]
    for block in range(4):
        rows = slice(8 * block, 8 * block + 8)

        def physical(field):
            return real_synthesis(*modes_of(z0, z1, z2, field, rows, twiddle))

        east, slope_x = physical(0), physical(2)
        product = [a * b for a, b in zip(east, slope_x)]
        north, slope_y = physical(1), physical(3)
        product = [p + a * b for p, a, b in zip(product, north, slope_y)]
        real, imag = real_analysis(product)
        for k in range(9):
            jac[0, k, rows, :] = real[k]
            if imag[k] is not None:
                jac[1, k, rows, :] = imag[k]
    real = [jac[0, k] for k in range(9)]
    imag = [None] + [jac[1, k] for k in range(1, 8)] + [None]
    results = x_forward(real, imag, twiddle, table_ref)
    for half in range(2):
        for group in range(2):
            for j3 in range(3):
                for part in range(2):
                    rows = slice(32 * j3 + 16 * part, 32 * j3 + 16 * part + 16)
                    start = (32 * group + 16 * half) * CHUNK + 2 * j3 + part
                    out_ref[pl.ds(start, 16, stride=CHUNK), :] = results[half][
                        rows, 128 * group : 128 * group + 128
                    ]


def projection_kernel(in_ref, radix_ref, unradix_ref, turn_ref, project_ref, mean_ref, out_ref):
    def rows(part):
        return jnp.concatenate(
            [in_ref[pl.ds(2 * j3 + part, 64, stride=CHUNK), :] for j3 in range(3)], axis=1
        )

    mixed = matmul_deep(radix_ref, split(jnp.concatenate([rows(0), rows(1)], axis=0)))
    c, s = turn_ref[0], turn_ref[1]
    turned = []
    for j3 in range(3):
        lanes = slice(128 * j3, 128 * j3 + 128)
        turned.append(jnp.concatenate(turn_by(mixed[:KAP, lanes], mixed[KAP:, lanes], c, s), axis=1))
    left = split(jnp.concatenate(turned, axis=0))
    out = matmul(left, project_ref, NN)
    first = lax.broadcasted_iota(jnp.int32, (16, 1), 0) == 0
    lane = lax.broadcasted_iota(jnp.int32, (1, 128), 1)
    real, imag = [], []
    for j3 in range(3):
        own = out[64 * j3 : 64 * j3 + 64]
        mean = sum(
            lax.dot_general(
                left[i][64 * j3 : 64 * j3 + 16],
                mean_ref[...],
                (NN, ((), ())),
                preferred_element_type=F32,
            )
            for i in range(2)
        )
        own = jnp.concatenate([own[:16] - jnp.where(first, mean, 0.0), own[16:]], axis=0)
        re, im = turn_by(own[:, :128], own[:, 128:], c, -s)
        if j3 == 0:
            zero_wave = (lax.axis_index("row") == 0) & (lane < 32)
            weight = jnp.where(zero_wave, -0.5, -1.0)
            re, im = re * weight, im * weight
        else:
            re, im = -re, -im
        real.append(re)
        imag.append(im)
    right = jnp.concatenate([jnp.concatenate(real, axis=1), jnp.concatenate(imag, axis=1)], axis=0)
    out = matmul_deep(unradix_ref, split(right))
    for part in range(2):
        for j3 in range(3):
            out_ref[pl.ds(2 * j3 + part, 64, stride=CHUNK), :] = out[
                64 * part : 64 * part + 64, 128 * j3 : 128 * j3 + 128
            ]


def state_update_kernel(
    in_ref, damp_ref, state_ref, start_ref, twiddle_ref, untable_ref, tendency_ref, new_ref, z0, z1, z2
):
    sides = []
    for group in range(2):
        rows = []
        for half in range(2):
            for part in range(2):
                for j3 in range(3):
                    start = (32 * group + 16 * half) * CHUNK + 2 * j3 + part
                    rows.append(in_ref[pl.ds(start, 16, stride=CHUNK), :])
        damp = damp_ref[192 * group : 192 * group + 192, :]
        sides.append(jnp.concatenate(rows, axis=0) + damp)
    z0[...], z1[...], z2[...] = x_inverse(sides[0], sides[1], 1, untable_ref)
    twiddle = twiddle_ref[...]
    for block in range(4):
        rows = slice(8 * block, 8 * block + 8)
        tendency = real_synthesis(*modes_of(z0, z1, z2, 0, rows, twiddle))
        for a in range(16):
            columns = slice(128 * a, 128 * a + 128)
            tendency_ref[0, rows, columns] = tendency[a]
            new_ref[0, rows, columns] = 0.75 * start_ref[0, rows, columns] + 0.25 * (
                state_ref[0, rows, columns] + STEP_SIZE * tendency[a]
            )


VMEM = pl.BlockSpec(memory_space=pltpu.VMEM)
ANY = pl.BlockSpec(memory_space=pl.ANY)
MIB = 1024 * 1024


def call(kernel, outs, operands, scratch=(), fetched=False):
    if fetched:
        scratch_shapes = [pltpu.VMEM(operand.shape, operand.dtype) for operand in operands]
        scratch_shapes.append(pltpu.SemaphoreType.DMA((len(operands),)))
    else:
        scratch_shapes = [pltpu.VMEM(shape, F32) for shape in scratch]
    return pl.pallas_call(
        kernel,
        out_shape=[jax.ShapeDtypeStruct(shape, F32) for shape in outs],
        in_specs=[ANY if fetched else VMEM] * len(operands),
        out_specs=[VMEM] * len(outs),
        scratch_shapes=scratch_shapes,
        compiler_params=pltpu.CompilerParams(vmem_limit_bytes=(60 if fetched else 32) * MIB),
    )(*operands)


def row_exchange(chunks):
    length = chunks.shape[0]
    sent = chunks.reshape(64, 1, 2 * length)
    return lax.all_to_all(sent, "row", split_axis=0, concat_axis=0, tiled=True).reshape(length, 128)


def wide_exchange(chunks):
    length = chunks.shape[0]
    groups = [[(2 * z + core) * 64 + row for z in range(4) for row in range(64)] for core in range(2)]
    sent = chunks.reshape(WIDE, 1, length // 2)
    got = lax.all_to_all(
        sent, ("layer", "row"), split_axis=0, concat_axis=0, tiled=True, axis_index_groups=groups
    )
    return got.reshape(length, 128)


def pair_gather(spectrum):
    pairs = [[2 * z, 2 * z + 1] for z in range(4)]
    return lax.all_gather(spectrum, "layer", axis=0, tiled=False, axis_index_groups=pairs)


def per_device(state, start_state, to_modes, from_modes, deform):
    turn_x = jnp.asarray(x_twiddle())
    forward_x = jnp.asarray(x_forward_table(False))
    forward_apart = jnp.asarray(x_forward_table(True))
    inverse_x = jnp.asarray(x_inverse_table(False))
    inverse_ix = jnp.asarray(x_inverse_table(True))
    radix = jnp.asarray(y_radix_table())
    unradix = jnp.asarray(y_radix_inverse_table())
    turn_y = jnp.asarray(y_twiddle())
    lanes = jnp.asarray(y_lane_table())
    unlanes = jnp.asarray(y_lane_inverse_table())
    project = jnp.asarray(y_projection_table())
    mean = jnp.asarray(y_mean_table())
    facts = jnp.asarray(lane_facts())

    columns, scalars = call(
        state_kernel,
        [(2 * WIDE, 128), (136, 128)],
        [state, turn_x, forward_x, to_modes, from_modes, deform.reshape(1, 8)],
        fetched=True,
    )
    (spectrum,) = call(
        spectrum_kernel, [(WIDE, USED)], [wide_exchange(columns), radix, turn_y, lanes, facts]
    )
    (fields,) = call(
        stream_kernel,
        [(8 * WIDE, 128)],
        [scalars, pair_gather(spectrum), unradix, turn_y, unlanes, facts],
        scratch=[(2 * WIDE, 128)],
    )
    flux, damped = call(
        jacobian_kernel,
        [(64 * CHUNK, 128)] * 2,
        [wide_exchange(fields), turn_x, inverse_ix, forward_apart],
        scratch=[(512, 256)] * 3 + [(2, 9, ROWS, 128)],
    )
    (total,) = call(
        projection_kernel,
        [(64 * CHUNK, 128)],
        [row_exchange(flux), radix, unradix, turn_y, project, mean],
    )
    return tuple(
        call(
            state_update_kernel,
            [(1, ROWS, GRID)] * 2,
            [row_exchange(total), damped, state, start_state, turn_x, inverse_x],
            scratch=[(128, 256)] * 3,
        )
    )


def solution(mesh):
    in_specs = (P("layer", "row", None), P("layer", "row", None), P(), P(), P())
    out_specs = (P("layer", "row", None), P("layer", "row", None))
    return jax.shard_map(
        per_device, mesh=mesh, in_specs=in_specs, out_specs=out_specs, check_vma=False
    )
```

```python
import functools
import math

import jax
import jax.numpy as jnp
import ml_dtypes
import numpy as np
from jax import lax
from jax.experimental import pallas as pl
from jax.experimental.pallas import tpu as pltpu
from jax.sharding import PartitionSpec as P

GRID = 2048
KCUT = 672
ROWS = 32
HALF = 14
CHUNK = 6
KAP = 64
JP = 21
PIECE = 8 * JP
SPAN = 512
USED = 504
HYPER_RATE = 0.2
STEP_SIZE = 0.5
BF16 = jnp.bfloat16
F32 = jnp.float32


def halves(table):
    high = table.astype(ml_dtypes.bfloat16)
    low = (table - high.astype(np.float64)).astype(ml_dtypes.bfloat16)
    return np.stack([high, low])


def turn(numerator, denominator):
    angle = 2.0 * math.pi * (np.mod(numerator, denominator) / denominator)
    return np.cos(angle), np.sin(angle)


def x_forward_table():
    b = np.arange(128)
    table = np.zeros((2, 16, 8, 2, 128))
    for half in range(2):
        for tau in range(HALF):
            for j3 in range(3):
                c, s = turn((3 * tau + j3 - 42 * half) * b, 128)
                table[half, tau, j3, 0] = c
                table[half, tau, j3, 1] = s
                table[half, tau, 3 + j3, 0] = -s
                table[half, tau, 3 + j3, 1] = c
    return halves(table.reshape(2, 128, 256))


def x_inverse_table(times_i):
    b = np.arange(128)
    table = np.zeros((2, 2, 3, 16, 2, 128))
    for half in range(2):
        for tau in range(HALF):
            for j3 in range(3):
                c, s = turn((3 * tau + j3 - 42 * half) * b, 128)
                if times_i:
                    c, s = -s, c
                table[half, 0, j3, tau, 0] = c
                table[half, 0, j3, tau, 1] = s
                table[half, 1, j3, tau, 0] = -s
                table[half, 1, j3, tau, 1] = c
    return halves(table.reshape(192, 256) * (2.0 / (GRID * GRID)))


def x_twiddle():
    table = np.zeros((32, 128))
    c, s = turn(np.arange(9)[:, None] * np.arange(128)[None, :], GRID)
    table[0:9] = c
    table[16:25] = s
    return table.astype(np.float32)


def paired(table):
    high, low = halves(table)
    return np.concatenate([high, high, low], axis=1)


def y_radix_table():
    c, s = turn(np.arange(KAP)[:, None] * np.arange(64)[None, :] + 32 * np.arange(64)[None, :], 64)
    return paired(np.block([[c, s], [-s, c]]))


def y_radix_inverse_table():
    c, s = turn(np.arange(64)[:, None] * np.arange(KAP)[None, :] + 32 * np.arange(64)[:, None], 64)
    return paired(np.block([[c, -s], [s, c]]))


def y_twiddle():
    c, s = turn((np.arange(KAP)[:, None] - KCUT) * np.arange(ROWS)[None, :], GRID)
    return np.stack([np.tile(c, (1, 4)), np.tile(s, (1, 4))]).astype(np.float32)


def y_lane_table():
    c, s = turn(np.arange(ROWS)[:, None] * np.arange(JP)[None, :], ROWS)
    table = np.zeros((3, 2, 4, ROWS, 256))
    for j3 in range(3):
        for slot in range(4):
            re = 40 * j3 + slot * JP
            im = re + 4 * JP
            table[j3, 0, slot, :, re : re + JP] = c
            table[j3, 1, slot, :, re : re + JP] = s
            table[j3, 0, slot, :, im : im + JP] = -s
            table[j3, 1, slot, :, im : im + JP] = c
    return halves(table.reshape(3, 256, 256))


def y_lane_inverse_table():
    high, low = y_lane_table()
    return np.stack([np.swapaxes(high, 1, 2), np.swapaxes(low, 1, 2)])


def y_projection_table():
    difference = np.arange(ROWS)[None, :] - np.arange(ROWS)[:, None]
    c, s = turn(difference[:, :, None] * np.arange(JP)[None, None, :], ROWS)
    c, s = np.kron(np.eye(4), c.sum(-1)), np.kron(np.eye(4), s.sum(-1))
    return halves(np.block([[c, s], [-s, c]]))


def y_mean_table():
    return np.kron(np.eye(8), np.ones((ROWS, ROWS))).astype(ml_dtypes.bfloat16)


def lane_facts():
    lane = np.arange(SPAN)
    j3 = lane // PIECE
    slot = (lane % (4 * JP)) // JP
    facts = np.zeros((8, SPAN))
    facts[0] = 16 * j3
    facts[1] = slot
    facts[2] = 64 * (lane % JP) - KCUT
    facts[3] = slot == 0
    return facts.astype(np.float32)


def split(value):
    high = value.astype(BF16)
    low = (value - high.astype(F32)).astype(BF16)
    return high, low


def matmul(left, right, dims):
    def one(a, b):
        return lax.dot_general(a, b, (dims, ((), ())), preferred_element_type=F32)

    return one(left[0], right[0]) + (one(left[0], right[1]) + one(left[1], right[0]))


def matmul_deep(table, right):
    depth = right[0].shape[0]

    def one(a, b):
        return lax.dot_general(a, b, (NN, ((), ())), preferred_element_type=F32)

    both = jnp.concatenate(right, axis=0)
    return one(table[:, : 2 * depth], both) + one(table[:, 2 * depth :], right[0])


NN = ((1,), (0,))
NT = ((1,), (1,))
TN = ((0,), (0,))

C1 = math.cos(math.pi / 8)
C2 = math.cos(math.pi / 4)
C3 = math.cos(3 * math.pi / 8)


def real_analysis(x):
    s = [x[a] + x[a + 8] for a in range(8)]
    d = [x[a] - x[a + 8] for a in range(8)]
    e = [None] + [d[a] - d[8 - a] for a in range(1, 4)]
    f = [None] + [d[a] + d[8 - a] for a in range(1, 4)]
    e2, f2 = e[2] * C2, f[2] * C2
    plus, minus = d[0] + e2, d[0] - e2
    first, second = e[1] * C1 + e[3] * C3, e[1] * C3 - e[3] * C1
    third, fourth = f[1] * C3 + f[3] * C1, f[1] * C1 - f[3] * C3
    u, v = d[4] + f2, f2 - d[4]
    p = [s[a] + s[a + 4] for a in range(4)]
    q = [s[a] - s[a + 4] for a in range(4)]
    even, odd = p[0] + p[2], p[1] + p[3]
    hd, hs = (q[1] - q[3]) * C2, (q[1] + q[3]) * C2
    real = [
        even + odd,
        plus + first,
        q[0] + hd,
        minus + second,
        p[0] - p[2],
        minus - second,
        q[0] - hd,
        plus - first,
        even - odd,
    ]
    imag = [
        None,
        -(third + u),
        -(q[2] + hs),
        -(fourth + v),
        p[3] - p[1],
        v - fourth,
        q[2] - hs,
        u - third,
        None,
    ]
    return real, imag


def real_synthesis(real, imag):
    plus, first = real[1] + real[7], real[1] - real[7]
    minus, second = real[3] + real[5], real[3] - real[5]
    third, u = -(imag[1] + imag[7]), imag[7] - imag[1]
    fourth, v = -(imag[3] + imag[5]), imag[5] - imag[3]
    d = [None] * 8
    d[0], d[4] = plus + minus, u - v
    e = [None, first * C1 + second * C3, (plus - minus) * C2, first * C3 - second * C1]
    f = [None, third * C3 + fourth * C1, (u + v) * C2, third * C1 - fourth * C3]
    for a in range(1, 4):
        d[a], d[8 - a] = f[a] + e[a], f[a] - e[a]
    even, odd = real[0] + real[8], real[0] - real[8]
    p = [even + real[4], odd - imag[4], even - real[4], odd + imag[4]]
    hr, hi = (real[2] - real[6]) * C2, (imag[2] + imag[6]) * C2
    q = [real[2] + real[6], hr - hi, imag[6] - imag[2], -(hr + hi)]
    s = [p[a] + q[a] for a in range(4)] + [p[a] - q[a] for a in range(4)]
    return [s[a] + d[a] for a in range(8)] + [s[a] - d[a] for a in range(8)]


def regroup(blocks, wanted):
    block = lax.broadcasted_iota(jnp.int32, (1, 128), 1) // 32
    turned = [
        b if b is None or i == 0 else pltpu.roll(b, 32 * i, 1) for i, b in enumerate(blocks)
    ]
    results = []
    for p in wanted:
        total = None
        for i in range(4):
            part = jnp.zeros_like(turned[0]) if turned[i] is None else turned[i]
            total = part if total is None else jnp.where(block == (p + i) % 4, part, total)
        results.append(total if p == 0 else pltpu.roll(total, 128 - 32 * p, 1))
    return results


def turn_by(re, im, c, s):
    return re * c + im * s, im * c - re * s


def x_forward(real, imag, twiddle, table):
    pieces = []
    for k in range(9):
        if k == 0:
            pieces.append(jnp.concatenate([real[0], jnp.zeros_like(real[0])], axis=1))
            continue
        c, s = twiddle[k : k + 1], twiddle[16 + k : 17 + k]
        if k == 8:
            re, im = real[8] * c, -(real[8] * s)
        else:
            re, im = real[k] * c + imag[k] * s, imag[k] * c - real[k] * s
        pieces.append(jnp.concatenate([re, im], axis=1))
    shared = split(jnp.concatenate(pieces[1:8], axis=0))
    results = []
    for half, own in enumerate((pieces[0], pieces[8])):
        own = split(own)
        right = [jnp.concatenate([own[i], shared[i]], axis=0) for i in range(2)]
        results.append(matmul([table[0, half], table[1, half]], right, NT))
    return results


def x_inverse(left, right, table):
    fields = len(left)
    upper = [part[:96] for part in left]
    own = regroup(upper, [0])[0] if fields == 4 else upper[0]
    first = matmul(split(own), [table[i][:96] for i in range(2)], TN)
    whole = [table[i] for i in range(2)]
    sides = [split(jnp.concatenate(side, axis=1) if fields > 1 else side[0]) for side in (left, right)]
    return first, matmul(sides[0], whole, TN), matmul(sides[1], whole, TN)


def modes_of(first, second, rest, field, rows, twiddle):
    real, imag = [], []
    size = rows.stop - rows.start
    start = field * 32 + rows.start
    own = first[start : start + size]
    for k in range(9):
        c, s = twiddle[k : k + 1], twiddle[16 + k : 17 + k]
        start = field * 128 + 32 * (k % 4) + rows.start
        if k == 0:
            z = own
        elif k == 8:
            z = second[start : start + size] - own
        else:
            source = second if k < 4 else rest
            z = source[start : start + size]
        re, im = z[:, :128], z[:, 128:]
        if k == 0:
            real.append(re)
            imag.append(None)
        else:
            real.append(re * c - im * s)
            imag.append(None if k == 8 else re * s + im * c)
    return real, imag


def y_forward(pieces, radix, twiddle, lanes, facts):
    stacked = jnp.concatenate(
        [jnp.concatenate(pieces[0], axis=1), jnp.concatenate(pieces[1], axis=1)], axis=0
    )
    mixed = matmul_deep(radix, split(stacked))
    c, s = twiddle[0], twiddle[1]
    windows = []
    for j3 in range(3):
        re, im = mixed[:KAP, 128 * j3 : 128 * j3 + 128], mixed[KAP:, 128 * j3 : 128 * j3 + 128]
        turned = jnp.concatenate([re * c + im * s, im * c - re * s], axis=1)
        windows.append(matmul(split(turned), [lanes[0, j3], lanes[1, j3]], NN))
    first, second, third = windows
    spectrum = jnp.concatenate(
        [
            first[:, :128],
            first[:, 128:] + second[:, :128],
            second[:, 128:] + third[:, :128],
            third[:, 128:],
        ],
        axis=1,
    )
    wave_y = y_waves(facts)
    return jnp.where(wave_y > -KCUT, spectrum, 0.0)


def y_waves(facts):
    kap = lax.broadcasted_iota(jnp.int32, (KAP, 1), 0).astype(F32)
    return kap + facts[2:3]


def x_waves(facts, owner):
    group = owner // 32
    half = (owner % 32) // 16
    tau = owner % 16
    base = (4 * group + 16 * (3 * tau - 42 * half)).astype(F32)
    shift = (8 * half * (1 - group)).astype(F32)
    return facts[0:1] + facts[1:2] + base + shift * facts[3:4]


def y_inverse(spectra, radix, twiddle, lanes):
    count = len(spectra)
    stacked = split(jnp.concatenate(spectra, axis=0) if count > 1 else spectra[0])
    c, s = twiddle[0], twiddle[1]
    real, imag = [], []
    for j3 in range(3):
        window = [part[:, 128 * j3 : 128 * j3 + 256] for part in stacked]
        out = matmul(window, [lanes[0, j3], lanes[1, j3]], NN)
        for field in range(count):
            own = out[KAP * field : KAP * field + KAP]
            re, im = own[:, :128], own[:, 128:]
            real.append(re * c - im * s)
            imag.append(re * s + im * c)
    right = split(
        jnp.concatenate([jnp.concatenate(real, axis=1), jnp.concatenate(imag, axis=1)], axis=0)
    )
    out = matmul_deep(radix, right)
    fields = []
    for field in range(count):
        columns = [slice(128 * (count * j3 + field), 128 * (count * j3 + field) + 128) for j3 in range(3)]
        fields.append([[out[:64, own] for own in columns], [out[64:, own] for own in columns]])
    return fields


def store_x(out_ref, results):
    for half in range(2):
        for group in range(2):
            block = results[half][:, 128 * group : 128 * group + 128]
            for tau in range(16):
                start = (32 * group + 16 * half + tau) * CHUNK
                out_ref[start : start + CHUNK, :] = block[8 * tau : 8 * tau + CHUNK]


def load_pieces(ref):
    return [
        [ref[pl.ds(3 * part + j3, 64, stride=CHUNK), :] for j3 in range(3)] for part in range(2)
    ]


def store_pieces(ref, fields):
    stride = CHUNK * len(fields)
    for field, pieces in enumerate(fields):
        for part in range(2):
            for j3 in range(3):
                ref[pl.ds(CHUNK * field + 3 * part + j3, 64, stride=stride), :] = pieces[part][j3]


def load_x(ref, fields):
    stride = CHUNK * fields
    groups = []
    for group in range(2):
        columns = []
        for field in range(fields):
            rows = []
            for half in range(2):
                for part in range(CHUNK):
                    start = (32 * group + 16 * half) * stride + CHUNK * field + part
                    rows.append(ref[pl.ds(start, 16, stride=stride), :])
            columns.append(jnp.concatenate(rows, axis=0))
        groups.append(columns)
    return groups


def state_kernel(state_hbm, twiddle_hbm, table_hbm, out_ref, state_ref, twiddle_ref, table_ref, sems):
    pairs = ((state_hbm, state_ref), (twiddle_hbm, twiddle_ref), (table_hbm, table_ref))
    copies = [pltpu.make_async_copy(a, b, sems.at[i]) for i, (a, b) in enumerate(pairs)]
    for copy in copies:
        copy.start()
    copies[0].wait()
    x = [state_ref[0, :, 128 * a : 128 * a + 128] for a in range(16)]
    real, imag = real_analysis(x)
    copies[1].wait()
    copies[2].wait()
    store_x(out_ref, x_forward(real, imag, twiddle_ref[...], table_ref))


def weights_kernel(to_ref, from_ref, deform_ref, facts_ref, out_ref):
    facts = facts_ref[...]
    wave_x = x_waves(facts, lax.axis_index("row"))
    wave_y = y_waves(facts)
    square = (wave_x * wave_x + wave_y * wave_y)[:, :USED]
    layer = lax.axis_index("layer")
    modes = [from_ref[layer, m] * (-1.0 / (square + deform_ref[m])) for m in range(8)]
    for n in range(8):
        total = None
        for m in range(8):
            term = modes[m] * to_ref[m, n]
            total = term if total is None else total + term
        out_ref[n] = total


def spectrum_kernel(in_ref, radix_ref, turn_ref, lanes_ref, facts_ref, spec_ref, used_ref):
    facts = facts_ref[...]
    spectrum = y_forward(load_pieces(in_ref), radix_ref, turn_ref, lanes_ref, facts)
    spec_ref[...] = spectrum
    used_ref[...] = spectrum[:, :USED]


def stream_kernel(
    weights_ref, all_ref, spec_ref, unradix_ref, turn_ref, unlanes_ref, facts_ref, out_ref, stream_ref
):
    facts = facts_ref[...]
    wave_x = x_waves(facts, lax.axis_index("row"))
    wave_y = y_waves(facts)
    stream = None
    for n in range(8):
        term = weights_ref[n] * all_ref[n]
        stream = term if stream is None else stream + term
    stream_ref[:, SPAN - 128 :] = jnp.zeros((KAP, 128), F32)
    stream_ref[:, :USED] = stream
    stream = stream_ref[...]
    spectrum = spec_ref[...]
    along_y = wave_y * jnp.where(wave_x == 0.0, 0.5, 1.0)
    fields = [-along_y * stream, wave_x * stream, wave_x * spectrum, along_y * spectrum]
    store_pieces(out_ref, y_inverse(fields, unradix_ref, turn_ref, unlanes_ref))


def jacobian_kernel(in_ref, twiddle_ref, untable_ref, table_ref, out_ref, z0, z1, z2, jac):
    groups = load_x(in_ref, 4)
    z0[...], z1[...], z2[...] = x_inverse(groups[0], groups[1], untable_ref)
    twiddle = twiddle_ref[...]
    for block in range(4):
        rows = slice(8 * block, 8 * block + 8)

        def physical(field):
            return real_synthesis(*modes_of(z0, z1, z2, field, rows, twiddle))

        east, slope_x = physical(0), physical(2)
        product = [a * b for a, b in zip(east, slope_x)]
        north, slope_y = physical(1), physical(3)
        product = [p + a * b for p, a, b in zip(product, north, slope_y)]
        real, imag = real_analysis(product)
        for k in range(9):
            jac[0, k, rows, :] = real[k]
            if imag[k] is not None:
                jac[1, k, rows, :] = imag[k]
    real = [jac[0, k] for k in range(9)]
    imag = [None] + [jac[1, k] for k in range(1, 8)] + [None]
    store_x(out_ref, x_forward(real, imag, twiddle, table_ref))


def projection_kernel(
    in_ref, spec_ref, radix_ref, unradix_ref, turn_ref, project_ref, mean_ref, unlanes_ref, facts_ref, out_ref
):
    facts = facts_ref[...]
    wave_x = x_waves(facts, lax.axis_index("row"))
    wave_y = y_waves(facts)
    ratio = (wave_x * wave_x + wave_y * wave_y) * (1.0 / (KCUT * KCUT))
    ratio = ratio * ratio
    damped = split((HYPER_RATE * (ratio * ratio)) * spec_ref[...])

    pieces = load_pieces(in_ref)
    stacked = [jnp.concatenate(pieces[part], axis=1) for part in range(2)]
    mixed = matmul_deep(radix_ref, split(jnp.concatenate(stacked, axis=0)))
    c, s = turn_ref[0], turn_ref[1]
    turned = []
    for j3 in range(3):
        lanes = slice(128 * j3, 128 * j3 + 128)
        turned.append(jnp.concatenate(turn_by(mixed[:KAP, lanes], mixed[KAP:, lanes], c, s), axis=1))
    left = split(jnp.concatenate(turned, axis=0))
    out = matmul(left, project_ref, NN)
    first = lax.broadcasted_iota(jnp.int32, (16, 1), 0) == 0
    lane = lax.broadcasted_iota(jnp.int32, (1, 128), 1)
    real, imag = [], []
    for j3 in range(3):
        own = out[64 * j3 : 64 * j3 + 64]
        mean = sum(
            lax.dot_general(
                left[i][64 * j3 : 64 * j3 + 16],
                mean_ref[...],
                (NN, ((), ())),
                preferred_element_type=F32,
            )
            for i in range(2)
        )
        own = jnp.concatenate([own[:16] - jnp.where(first, mean, 0.0), own[16:]], axis=0)
        window = [part[:, 128 * j3 : 128 * j3 + 256] for part in damped]
        own = own + matmul(window, [unlanes_ref[i, j3] for i in range(2)], NN)
        re, im = turn_by(own[:, :128], own[:, 128:], c, -s)
        if j3 == 0:
            zero_wave = (lax.axis_index("row") == 0) & (lane < 32)
            weight = jnp.where(zero_wave, -0.5, -1.0)
            re, im = re * weight, im * weight
        else:
            re, im = -re, -im
        real.append(re)
        imag.append(im)
    right = jnp.concatenate([jnp.concatenate(real, axis=1), jnp.concatenate(imag, axis=1)], axis=0)
    out = matmul_deep(unradix_ref, split(right))
    columns = [slice(128 * j3, 128 * j3 + 128) for j3 in range(3)]
    store_pieces(out_ref, [[[out[:64, own] for own in columns], [out[64:, own] for own in columns]]])


def state_update_kernel(
    in_ref, state_ref, start_ref, twiddle_ref, untable_ref, tendency_ref, new_ref, z0, z1, z2
):
    groups = load_x(in_ref, 1)
    z0[...], z1[...], z2[...] = x_inverse(groups[0], groups[1], untable_ref)
    twiddle = twiddle_ref[...]
    for block in range(4):
        rows = slice(8 * block, 8 * block + 8)
        tendency = real_synthesis(*modes_of(z0, z1, z2, 0, rows, twiddle))
        for a in range(16):
            columns = slice(128 * a, 128 * a + 128)
            tendency_ref[0, rows, columns] = tendency[a]
            new_ref[0, rows, columns] = 0.75 * start_ref[0, rows, columns] + 0.25 * (
                state_ref[0, rows, columns] + STEP_SIZE * tendency[a]
            )


VMEM = pl.BlockSpec(memory_space=pltpu.VMEM)
SMEM = pl.BlockSpec(memory_space=pltpu.SMEM)
HBM = pl.BlockSpec(memory_space=pltpu.HBM)


def call(kernel, outs, operands, scalars=0, scratch=(), fetched=False, cost=None):
    if fetched:
        in_specs = [HBM] * len(operands)
        scratch_shapes = [pltpu.VMEM(operand.shape, operand.dtype) for operand in operands]
        scratch_shapes.append(pltpu.SemaphoreType.DMA((len(operands),)))
    else:
        in_specs = [SMEM] * scalars + [VMEM] * (len(operands) - scalars)
        scratch_shapes = [pltpu.VMEM(shape, F32) for shape in scratch]
    return pl.pallas_call(
        kernel,
        out_shape=[jax.ShapeDtypeStruct(shape, F32) for shape in outs],
        in_specs=in_specs,
        out_specs=[VMEM] * len(outs),
        scratch_shapes=scratch_shapes,
        compiler_params=pltpu.CompilerParams(vmem_limit_bytes=32 * 1024 * 1024),
        cost_estimate=cost,
    )(*operands)


def exchange(chunks, devices):
    length = chunks.shape[0]
    sent = chunks.reshape(devices, 1, length * 128 // devices)
    return lax.all_to_all(sent, "row", split_axis=0, concat_axis=0, tiled=True).reshape(length, 128)


def per_device(state, start_state, to_modes, from_modes, deform):
    devices = lax.axis_size("row")
    turn_x = jnp.asarray(x_twiddle())
    forward_x = jnp.asarray(x_forward_table())
    inverse_x = jnp.asarray(x_inverse_table(False))
    inverse_ix = jnp.asarray(x_inverse_table(True))
    radix = jnp.asarray(y_radix_table())
    unradix = jnp.asarray(y_radix_inverse_table())
    turn_y = jnp.asarray(y_twiddle())
    lanes = jnp.asarray(y_lane_table())
    unlanes = jnp.asarray(y_lane_inverse_table())
    project = jnp.asarray(y_projection_table())
    mean = jnp.asarray(y_mean_table())
    facts = jnp.asarray(lane_facts())

    one, four = (64 * CHUNK, 128), (256 * CHUNK, 128)
    (columns,) = call(state_kernel, [one], [state, turn_x, forward_x], fetched=True)
    columns = exchange(columns, devices)
    spectrum, used = call(
        spectrum_kernel, [(KAP, SPAN), (KAP, USED)], [columns, radix, turn_y, lanes, facts]
    )
    (weights,) = call(
        weights_kernel,
        [(8, KAP, USED)],
        [to_modes, from_modes, deform, facts],
        scalars=3,
        cost=pl.CostEstimate(flops=8_000_000, bytes_accessed=2_000_000, transcendentals=0),
    )
    gathered = lax.all_gather(used, "layer", axis=0, tiled=False)
    (fields,) = call(
        stream_kernel,
        [four],
        [weights, gathered, spectrum, unradix, turn_y, unlanes, facts],
        scratch=[(KAP, SPAN)],
    )
    fields = exchange(fields, devices)
    (flux,) = call(
        jacobian_kernel,
        [one],
        [fields, turn_x, inverse_ix, forward_x],
        scratch=[(128, 256), (512, 256), (512, 256), (2, 9, ROWS, 128)],
    )
    flux = exchange(flux, devices)
    (total,) = call(
        projection_kernel,
        [one],
        [flux, spectrum, radix, unradix, turn_y, project, mean, unlanes, facts],
    )
    total = exchange(total, devices)
    return tuple(
        call(
            state_update_kernel,
            [(1, ROWS, GRID)] * 2,
            [total, state, start_state, turn_x, inverse_x],
            scratch=[(128, 256)] * 3,
        )
    )


def solution(mesh):
    in_specs = (P("layer", "row", None), P("layer", "row", None), P(), P(), P())
    out_specs = (P("layer", "row", None), P("layer", "row", None))
    return jax.shard_map(
        per_device, mesh=mesh, in_specs=in_specs, out_specs=out_specs, check_vma=False
    )
```

```python
import functools
import math

import jax
import jax.numpy as jnp
import ml_dtypes
import numpy as np
from jax import lax
from jax.experimental import pallas as pl
from jax.experimental.pallas import tpu as pltpu
from jax.sharding import PartitionSpec as P

GRID = 2048
KCUT = 672
ROWS = 32
HALF = 14
CHUNK = 6
KAP = 64
JP = 21
PIECE = 8 * JP
SPAN = 512
USED = 504
HYPER_RATE = 0.2
STEP_SIZE = 0.5
BF16 = jnp.bfloat16
F32 = jnp.float32


def halves(table):
    high = table.astype(ml_dtypes.bfloat16)
    low = (table - high.astype(np.float64)).astype(ml_dtypes.bfloat16)
    return np.stack([high, low])


def turn(numerator, denominator):
    angle = 2.0 * math.pi * (np.mod(numerator, denominator) / denominator)
    return np.cos(angle), np.sin(angle)


def x_forward_table():
    b = np.arange(128)
    table = np.zeros((2, 16, 8, 2, 128))
    for half in range(2):
        for tau in range(HALF):
            for j3 in range(3):
                c, s = turn((3 * tau + j3 - 42 * half) * b, 128)
                table[half, tau, j3, 0] = c
                table[half, tau, j3, 1] = s
                table[half, tau, 3 + j3, 0] = -s
                table[half, tau, 3 + j3, 1] = c
    return halves(table.reshape(2, 128, 256))


def x_inverse_table(times_i):
    b = np.arange(128)
    table = np.zeros((2, 2, 3, 16, 2, 128))
    for half in range(2):
        for tau in range(HALF):
            for j3 in range(3):
                c, s = turn((3 * tau + j3 - 42 * half) * b, 128)
                if times_i:
                    c, s = -s, c
                table[half, 0, j3, tau, 0] = c
                table[half, 0, j3, tau, 1] = s
                table[half, 1, j3, tau, 0] = -s
                table[half, 1, j3, tau, 1] = c
    return halves(table.reshape(192, 256) * (2.0 / (GRID * GRID)))


def x_twiddle():
    table = np.zeros((32, 128))
    c, s = turn(np.arange(9)[:, None] * np.arange(128)[None, :], GRID)
    table[0:9] = c
    table[16:25] = s
    return table.astype(np.float32)


def paired(table):
    high, low = halves(table)
    return np.concatenate([high, high, low], axis=1)


def y_radix_table():
    c, s = turn(np.arange(KAP)[:, None] * np.arange(64)[None, :] + 32 * np.arange(64)[None, :], 64)
    return paired(np.block([[c, s], [-s, c]]))


def y_radix_inverse_table():
    c, s = turn(np.arange(64)[:, None] * np.arange(KAP)[None, :] + 32 * np.arange(64)[:, None], 64)
    return paired(np.block([[c, -s], [s, c]]))


def y_twiddle():
    c, s = turn((np.arange(KAP)[:, None] - KCUT) * np.arange(ROWS)[None, :], GRID)
    return np.stack([np.tile(c, (1, 4)), np.tile(s, (1, 4))]).astype(np.float32)


def y_lane_table():
    c, s = turn(np.arange(ROWS)[:, None] * np.arange(JP)[None, :], ROWS)
    table = np.zeros((3, 2, 4, ROWS, 256))
    for j3 in range(3):
        for slot in range(4):
            re = 40 * j3 + slot * JP
            im = re + 4 * JP
            table[j3, 0, slot, :, re : re + JP] = c
            table[j3, 1, slot, :, re : re + JP] = s
            table[j3, 0, slot, :, im : im + JP] = -s
            table[j3, 1, slot, :, im : im + JP] = c
    return halves(table.reshape(3, 256, 256))


def y_lane_inverse_table():
    high, low = y_lane_table()
    return np.stack([np.swapaxes(high, 1, 2), np.swapaxes(low, 1, 2)])


def y_projection_table():
    difference = np.arange(ROWS)[None, :] - np.arange(ROWS)[:, None]
    c, s = turn(difference[:, :, None] * np.arange(JP)[None, None, :], ROWS)
    c, s = np.kron(np.eye(4), c.sum(-1)), np.kron(np.eye(4), s.sum(-1))
    return halves(np.block([[c, s], [-s, c]]))


def y_mean_table():
    return np.kron(np.eye(8), np.ones((ROWS, ROWS))).astype(ml_dtypes.bfloat16)


def lane_facts():
    lane = np.arange(SPAN)
    j3 = lane // PIECE
    slot = (lane % (4 * JP)) // JP
    facts = np.zeros((8, SPAN))
    facts[0] = 16 * j3
    facts[1] = slot
    facts[2] = 64 * (lane % JP) - KCUT
    facts[3] = slot == 0
    return facts.astype(np.float32)


def split(value):
    high = value.astype(BF16)
    low = (value - high.astype(F32)).astype(BF16)
    return high, low


def matmul(left, right, dims):
    def one(a, b):
        return lax.dot_general(a, b, (dims, ((), ())), preferred_element_type=F32)

    return one(left[0], right[0]) + (one(left[0], right[1]) + one(left[1], right[0]))


def matmul_deep(table, right):
    depth = right[0].shape[0]

    def one(a, b):
        return lax.dot_general(a, b, (NN, ((), ())), preferred_element_type=F32)

    both = jnp.concatenate(right, axis=0)
    return one(table[:, : 2 * depth], both) + one(table[:, 2 * depth :], right[0])


NN = ((1,), (0,))
NT = ((1,), (1,))
TN = ((0,), (0,))

C1 = math.cos(math.pi / 8)
C2 = math.cos(math.pi / 4)
C3 = math.cos(3 * math.pi / 8)


def real_analysis(x):
    s = [x[a] + x[a + 8] for a in range(8)]
    d = [x[a] - x[a + 8] for a in range(8)]
    e = [None] + [d[a] - d[8 - a] for a in range(1, 4)]
    f = [None] + [d[a] + d[8 - a] for a in range(1, 4)]
    e2, f2 = e[2] * C2, f[2] * C2
    plus, minus = d[0] + e2, d[0] - e2
    first, second = e[1] * C1 + e[3] * C3, e[1] * C3 - e[3] * C1
    third, fourth = f[1] * C3 + f[3] * C1, f[1] * C1 - f[3] * C3
    u, v = d[4] + f2, f2 - d[4]
    p = [s[a] + s[a + 4] for a in range(4)]
    q = [s[a] - s[a + 4] for a in range(4)]
    even, odd = p[0] + p[2], p[1] + p[3]
    hd, hs = (q[1] - q[3]) * C2, (q[1] + q[3]) * C2
    real = [
        even + odd,
        plus + first,
        q[0] + hd,
        minus + second,
        p[0] - p[2],
        minus - second,
        q[0] - hd,
        plus - first,
        even - odd,
    ]
    imag = [
        None,
        -(third + u),
        -(q[2] + hs),
        -(fourth + v),
        p[3] - p[1],
        v - fourth,
        q[2] - hs,
        u - third,
        None,
    ]
    return real, imag


def real_synthesis(real, imag):
    plus, first = real[1] + real[7], real[1] - real[7]
    minus, second = real[3] + real[5], real[3] - real[5]
    third, u = -(imag[1] + imag[7]), imag[7] - imag[1]
    fourth, v = -(imag[3] + imag[5]), imag[5] - imag[3]
    d = [None] * 8
    d[0], d[4] = plus + minus, u - v
    e = [None, first * C1 + second * C3, (plus - minus) * C2, first * C3 - second * C1]
    f = [None, third * C3 + fourth * C1, (u + v) * C2, third * C1 - fourth * C3]
    for a in range(1, 4):
        d[a], d[8 - a] = f[a] + e[a], f[a] - e[a]
    even, odd = real[0] + real[8], real[0] - real[8]
    p = [even + real[4], odd - imag[4], even - real[4], odd + imag[4]]
    hr, hi = (real[2] - real[6]) * C2, (imag[2] + imag[6]) * C2
    q = [real[2] + real[6], hr - hi, imag[6] - imag[2], -(hr + hi)]
    s = [p[a] + q[a] for a in range(4)] + [p[a] - q[a] for a in range(4)]
    return [s[a] + d[a] for a in range(8)] + [s[a] - d[a] for a in range(8)]


def regroup(blocks, wanted):
    block = lax.broadcasted_iota(jnp.int32, (1, 128), 1) // 32
    turned = [
        b if b is None or i == 0 else pltpu.roll(b, 32 * i, 1) for i, b in enumerate(blocks)
    ]
    results = []
    for p in wanted:
        total = None
        for i in range(4):
            part = jnp.zeros_like(turned[0]) if turned[i] is None else turned[i]
            total = part if total is None else jnp.where(block == (p + i) % 4, part, total)
        results.append(total if p == 0 else pltpu.roll(total, 128 - 32 * p, 1))
    return results


def turn_by(re, im, c, s):
    return re * c + im * s, im * c - re * s


def x_forward(real, imag, twiddle, table):
    pieces = []
    for k in range(9):
        if k == 0:
            pieces.append(jnp.concatenate([real[0], jnp.zeros_like(real[0])], axis=1))
            continue
        c, s = twiddle[k : k + 1], twiddle[16 + k : 17 + k]
        if k == 8:
            re, im = real[8] * c, -(real[8] * s)
        else:
            re, im = real[k] * c + imag[k] * s, imag[k] * c - real[k] * s
        pieces.append(jnp.concatenate([re, im], axis=1))
    shared = split(jnp.concatenate(pieces[1:8], axis=0))
    results = []
    for half, own in enumerate((pieces[0], pieces[8])):
        own = split(own)
        right = [jnp.concatenate([own[i], shared[i]], axis=0) for i in range(2)]
        results.append(matmul([table[0, half], table[1, half]], right, NT))
    return results


def x_inverse(left, right, table):
    fields = len(left)
    upper = [part[:96] for part in left]
    own = regroup(upper, [0])[0] if fields == 4 else upper[0]
    first = matmul(split(own), [table[i][:96] for i in range(2)], TN)
    whole = [table[i] for i in range(2)]
    sides = [split(jnp.concatenate(side, axis=1) if fields > 1 else side[0]) for side in (left, right)]
    return first, matmul(sides[0], whole, TN), matmul(sides[1], whole, TN)


def modes_of(first, second, rest, field, rows, twiddle):
    real, imag = [], []
    size = rows.stop - rows.start
    start = field * 32 + rows.start
    own = first[start : start + size]
    for k in range(9):
        c, s = twiddle[k : k + 1], twiddle[16 + k : 17 + k]
        start = field * 128 + 32 * (k % 4) + rows.start
        if k == 0:
            z = own
        elif k == 8:
            z = second[start : start + size] - own
        else:
            source = second if k < 4 else rest
            z = source[start : start + size]
        re, im = z[:, :128], z[:, 128:]
        if k == 0:
            real.append(re)
            imag.append(None)
        else:
            real.append(re * c - im * s)
            imag.append(None if k == 8 else re * s + im * c)
    return real, imag


def y_forward(pieces, radix, twiddle, lanes, facts):
    stacked = jnp.concatenate(
        [jnp.concatenate(pieces[0], axis=1), jnp.concatenate(pieces[1], axis=1)], axis=0
    )
    mixed = matmul_deep(radix, split(stacked))
    c, s = twiddle[0], twiddle[1]
    windows = []
    for j3 in range(3):
        re, im = mixed[:KAP, 128 * j3 : 128 * j3 + 128], mixed[KAP:, 128 * j3 : 128 * j3 + 128]
        turned = jnp.concatenate([re * c + im * s, im * c - re * s], axis=1)
        windows.append(matmul(split(turned), [lanes[0, j3], lanes[1, j3]], NN))
    first, second, third = windows
    spectrum = jnp.concatenate(
        [
            first[:, :128],
            first[:, 128:] + second[:, :128],
            second[:, 128:] + third[:, :128],
            third[:, 128:],
        ],
        axis=1,
    )
    wave_y = y_waves(facts)
    return jnp.where(wave_y > -KCUT, spectrum, 0.0)


def y_waves(facts):
    kap = lax.broadcasted_iota(jnp.int32, (KAP, 1), 0).astype(F32)
    return kap + facts[2:3]


def x_waves(facts, owner):
    group = owner // 32
    half = (owner % 32) // 16
    tau = owner % 16
    base = (4 * group + 16 * (3 * tau - 42 * half)).astype(F32)
    shift = (8 * half * (1 - group)).astype(F32)
    return facts[0:1] + facts[1:2] + base + shift * facts[3:4]


def y_inverse(spectra, radix, twiddle, lanes):
    count = len(spectra)
    stacked = split(jnp.concatenate(spectra, axis=0) if count > 1 else spectra[0])
    c, s = twiddle[0], twiddle[1]
    real, imag = [], []
    for j3 in range(3):
        window = [part[:, 128 * j3 : 128 * j3 + 256] for part in stacked]
        out = matmul(window, [lanes[0, j3], lanes[1, j3]], NN)
        for field in range(count):
            own = out[KAP * field : KAP * field + KAP]
            re, im = own[:, :128], own[:, 128:]
            real.append(re * c - im * s)
            imag.append(re * s + im * c)
    right = split(
        jnp.concatenate([jnp.concatenate(real, axis=1), jnp.concatenate(imag, axis=1)], axis=0)
    )
    out = matmul_deep(radix, right)
    fields = []
    for field in range(count):
        columns = [slice(128 * (count * j3 + field), 128 * (count * j3 + field) + 128) for j3 in range(3)]
        fields.append([[out[:64, own] for own in columns], [out[64:, own] for own in columns]])
    return fields


def store_x(out_ref, results, halves_done=(0, 1)):
    for half in halves_done:
        for group in range(2):
            block = results[half][:, 128 * group : 128 * group + 128]
            for tau in range(16):
                start = (32 * group + 16 * half + tau) * CHUNK
                out_ref[start : start + CHUNK, :] = block[8 * tau : 8 * tau + CHUNK]


def load_pieces(ref):
    return [
        [ref[pl.ds(3 * part + j3, 64, stride=CHUNK), :] for j3 in range(3)] for part in range(2)
    ]


def store_pieces(ref, fields):
    stride = CHUNK * len(fields)
    for field, pieces in enumerate(fields):
        for part in range(2):
            for j3 in range(3):
                ref[pl.ds(CHUNK * field + 3 * part + j3, 64, stride=stride), :] = pieces[part][j3]


def load_x(ref, fields):
    stride = CHUNK * fields
    groups = []
    for group in range(2):
        columns = []
        for field in range(fields):
            rows = []
            for half in range(2):
                for part in range(CHUNK):
                    start = (32 * group + 16 * half) * stride + CHUNK * field + part
                    rows.append(ref[pl.ds(start, 16, stride=stride), :])
            columns.append(jnp.concatenate(rows, axis=0))
        groups.append(columns)
    return groups


def state_kernel(
    state_hbm, twiddle_hbm, table_hbm, out_hbm, state_ref, twiddle_ref, table_ref, out_ref, sems
):
    pairs = ((state_hbm, state_ref), (twiddle_hbm, twiddle_ref), (table_hbm, table_ref))
    copies = [pltpu.make_async_copy(a, b, sems.at[i]) for i, (a, b) in enumerate(pairs)]
    for copy in copies:
        copy.start()
    copies[0].wait()
    x = [state_ref[0, :, 128 * a : 128 * a + 128] for a in range(16)]
    real, imag = real_analysis(x)
    copies[1].wait()
    copies[2].wait()
    results = x_forward(real, imag, twiddle_ref[...], table_ref)
    sends = []
    for half in range(2):
        store_x(out_ref, results, (half,))
        for group in range(2):
            rows = pl.ds((32 * group + 16 * half) * CHUNK, 16 * CHUNK)
            sem = sems.at[3 + 2 * half + group]
            sends.append(pltpu.make_async_copy(out_ref.at[rows], out_hbm.at[rows], sem))
            sends[-1].start()
    for send in sends:
        send.wait()


def weights_kernel(to_ref, from_ref, deform_ref, facts_ref, out_ref):
    facts = facts_ref[...]
    wave_x = x_waves(facts, lax.axis_index("row"))
    wave_y = y_waves(facts)
    square = (wave_x * wave_x + wave_y * wave_y)[:, :USED]
    layer = lax.axis_index("layer")
    modes = [from_ref[layer, m] * (-1.0 / (square + deform_ref[m])) for m in range(8)]
    for n in range(8):
        total = None
        for m in range(8):
            term = modes[m] * to_ref[m, n]
            total = term if total is None else total + term
        out_ref[n] = total


def spectrum_kernel(in_ref, radix_ref, turn_ref, lanes_ref, facts_ref, spec_ref, used_ref):
    facts = facts_ref[...]
    spectrum = y_forward(load_pieces(in_ref), radix_ref, turn_ref, lanes_ref, facts)
    spec_ref[...] = spectrum
    used_ref[...] = spectrum[:, :USED]


def stream_kernel(
    weights_ref, all_ref, spec_ref, unradix_ref, turn_ref, unlanes_ref, facts_ref, out_ref, stream_ref
):
    facts = facts_ref[...]
    wave_x = x_waves(facts, lax.axis_index("row"))
    wave_y = y_waves(facts)
    stream = None
    for n in range(8):
        term = weights_ref[n] * all_ref[n]
        stream = term if stream is None else stream + term
    stream_ref[:, SPAN - 128 :] = jnp.zeros((KAP, 128), F32)
    stream_ref[:, :USED] = stream
    stream = stream_ref[...]
    spectrum = spec_ref[...]
    along_y = wave_y * jnp.where(wave_x == 0.0, 0.5, 1.0)
    fields = [-along_y * stream, wave_x * stream, wave_x * spectrum, along_y * spectrum]
    store_pieces(out_ref, y_inverse(fields, unradix_ref, turn_ref, unlanes_ref))


def jacobian_kernel(in_ref, twiddle_ref, untable_ref, table_ref, out_ref, z0, z1, z2, jac):
    groups = load_x(in_ref, 4)
    z0[...], z1[...], z2[...] = x_inverse(groups[0], groups[1], untable_ref)
    twiddle = twiddle_ref[...]
    for block in range(4):
        rows = slice(8 * block, 8 * block + 8)

        def physical(field):
            return real_synthesis(*modes_of(z0, z1, z2, field, rows, twiddle))

        east, slope_x = physical(0), physical(2)
        product = [a * b for a, b in zip(east, slope_x)]
        north, slope_y = physical(1), physical(3)
        product = [p + a * b for p, a, b in zip(product, north, slope_y)]
        real, imag = real_analysis(product)
        for k in range(9):
            jac[0, k, rows, :] = real[k]
            if imag[k] is not None:
                jac[1, k, rows, :] = imag[k]
    real = [jac[0, k] for k in range(9)]
    imag = [None] + [jac[1, k] for k in range(1, 8)] + [None]
    store_x(out_ref, x_forward(real, imag, twiddle, table_ref))


def projection_kernel(
    in_ref, spec_ref, radix_ref, unradix_ref, turn_ref, project_ref, mean_ref, unlanes_ref, facts_ref, out_ref
):
    facts = facts_ref[...]
    wave_x = x_waves(facts, lax.axis_index("row"))
    wave_y = y_waves(facts)
    ratio = (wave_x * wave_x + wave_y * wave_y) * (1.0 / (KCUT * KCUT))
    ratio = ratio * ratio
    damped = split((HYPER_RATE * (ratio * ratio)) * spec_ref[...])

    pieces = load_pieces(in_ref)
    stacked = [jnp.concatenate(pieces[part], axis=1) for part in range(2)]
    mixed = matmul_deep(radix_ref, split(jnp.concatenate(stacked, axis=0)))
    c, s = turn_ref[0], turn_ref[1]
    turned = []
    for j3 in range(3):
        lanes = slice(128 * j3, 128 * j3 + 128)
        turned.append(jnp.concatenate(turn_by(mixed[:KAP, lanes], mixed[KAP:, lanes], c, s), axis=1))
    left = split(jnp.concatenate(turned, axis=0))
    out = matmul(left, project_ref, NN)
    first = lax.broadcasted_iota(jnp.int32, (16, 1), 0) == 0
    lane = lax.broadcasted_iota(jnp.int32, (1, 128), 1)
    real, imag = [], []
    for j3 in range(3):
        own = out[64 * j3 : 64 * j3 + 64]
        mean = sum(
            lax.dot_general(
                left[i][64 * j3 : 64 * j3 + 16],
                mean_ref[...],
                (NN, ((), ())),
                preferred_element_type=F32,
            )
            for i in range(2)
        )
        own = jnp.concatenate([own[:16] - jnp.where(first, mean, 0.0), own[16:]], axis=0)
        window = [part[:, 128 * j3 : 128 * j3 + 256] for part in damped]
        own = own + matmul(window, [unlanes_ref[i, j3] for i in range(2)], NN)
        re, im = turn_by(own[:, :128], own[:, 128:], c, -s)
        if j3 == 0:
            zero_wave = (lax.axis_index("row") == 0) & (lane < 32)
            weight = jnp.where(zero_wave, -0.5, -1.0)
            re, im = re * weight, im * weight
        else:
            re, im = -re, -im
        real.append(re)
        imag.append(im)
    right = jnp.concatenate([jnp.concatenate(real, axis=1), jnp.concatenate(imag, axis=1)], axis=0)
    out = matmul_deep(unradix_ref, split(right))
    columns = [slice(128 * j3, 128 * j3 + 128) for j3 in range(3)]
    store_pieces(out_ref, [[[out[:64, own] for own in columns], [out[64:, own] for own in columns]]])


def state_update_kernel(
    in_ref,
    state_ref,
    start_ref,
    twiddle_ref,
    untable_ref,
    tendency_hbm,
    new_hbm,
    z0,
    z1,
    z2,
    tendency_ref,
    new_ref,
    sems,
):
    groups = load_x(in_ref, 1)
    z0[...], z1[...], z2[...] = x_inverse(groups[0], groups[1], untable_ref)
    twiddle = twiddle_ref[...]
    sends = []
    for block in range(4):
        rows = slice(8 * block, 8 * block + 8)
        tendency = real_synthesis(*modes_of(z0, z1, z2, 0, rows, twiddle))
        for a in range(16):
            columns = slice(128 * a, 128 * a + 128)
            tendency_ref[0, rows, columns] = tendency[a]
            new_ref[0, rows, columns] = 0.75 * start_ref[0, rows, columns] + 0.25 * (
                state_ref[0, rows, columns] + STEP_SIZE * tendency[a]
            )
        for i, (near, far) in enumerate(((tendency_ref, tendency_hbm), (new_ref, new_hbm))):
            own = (slice(None), pl.ds(8 * block, 8))
            sends.append(pltpu.make_async_copy(near.at[own], far.at[own], sems.at[2 * block + i]))
            sends[-1].start()
    for send in sends:
        send.wait()


VMEM = pl.BlockSpec(memory_space=pltpu.VMEM)
SMEM = pl.BlockSpec(memory_space=pltpu.SMEM)
ANY = pl.BlockSpec(memory_space=pl.ANY)
MIB = 1024 * 1024


def call(kernel, outs, operands, scalars=0, scratch=(), far_in=False, far_out=False, copies=0, cost=None):
    scratch_shapes = [pltpu.VMEM(operand.shape, operand.dtype) for operand in operands] if far_in else []
    scratch_shapes += [pltpu.VMEM(shape, F32) for shape in scratch]
    scratch_shapes += [pltpu.VMEM(shape, F32) for shape in outs] if far_out else []
    scratch_shapes += [pltpu.SemaphoreType.DMA((copies,))] if copies else []
    near = [SMEM] * scalars + [VMEM] * (len(operands) - scalars)
    return pl.pallas_call(
        kernel,
        out_shape=[jax.ShapeDtypeStruct(shape, F32) for shape in outs],
        in_specs=[ANY] * len(operands) if far_in else near,
        out_specs=[ANY if far_out else VMEM] * len(outs),
        scratch_shapes=scratch_shapes,
        compiler_params=pltpu.CompilerParams(vmem_limit_bytes=(60 if far_in else 32) * MIB),
        cost_estimate=cost,
    )(*operands)


def exchange(chunks, devices):
    length = chunks.shape[0]
    sent = chunks.reshape(devices, 1, length * 128 // devices)
    return lax.all_to_all(sent, "row", split_axis=0, concat_axis=0, tiled=True).reshape(length, 128)


def per_device(state, start_state, to_modes, from_modes, deform):
    devices = lax.axis_size("row")
    turn_x = jnp.asarray(x_twiddle())
    forward_x = jnp.asarray(x_forward_table())
    inverse_x = jnp.asarray(x_inverse_table(False))
    inverse_ix = jnp.asarray(x_inverse_table(True))
    radix = jnp.asarray(y_radix_table())
    unradix = jnp.asarray(y_radix_inverse_table())
    turn_y = jnp.asarray(y_twiddle())
    lanes = jnp.asarray(y_lane_table())
    unlanes = jnp.asarray(y_lane_inverse_table())
    project = jnp.asarray(y_projection_table())
    mean = jnp.asarray(y_mean_table())
    facts = jnp.asarray(lane_facts())

    one, four = (64 * CHUNK, 128), (256 * CHUNK, 128)
    (columns,) = call(state_kernel, [one], [state, turn_x, forward_x], far_in=True, far_out=True, copies=7)
    columns = exchange(columns, devices)
    spectrum, used = call(
        spectrum_kernel, [(KAP, SPAN), (KAP, USED)], [columns, radix, turn_y, lanes, facts]
    )
    (weights,) = call(
        weights_kernel,
        [(8, KAP, USED)],
        [to_modes, from_modes, deform, facts],
        scalars=3,
        cost=pl.CostEstimate(flops=8_000_000, bytes_accessed=2_000_000, transcendentals=0),
    )
    gathered = lax.all_gather(used, "layer", axis=0, tiled=False)
    (fields,) = call(
        stream_kernel,
        [four],
        [weights, gathered, spectrum, unradix, turn_y, unlanes, facts],
        scratch=[(KAP, SPAN)],
    )
    fields = exchange(fields, devices)
    (flux,) = call(
        jacobian_kernel,
        [one],
        [fields, turn_x, inverse_ix, forward_x],
        scratch=[(128, 256), (512, 256), (512, 256), (2, 9, ROWS, 128)],
    )
    flux = exchange(flux, devices)
    (total,) = call(
        projection_kernel,
        [one],
        [flux, spectrum, radix, unradix, turn_y, project, mean, unlanes, facts],
    )
    total = exchange(total, devices)
    return tuple(
        call(
            state_update_kernel,
            [(1, ROWS, GRID)] * 2,
            [total, state, start_state, turn_x, inverse_x],
            scratch=[(128, 256)] * 3,
            far_out=True,
            copies=8,
        )
    )


def solution(mesh):
    in_specs = (P("layer", "row", None), P("layer", "row", None), P(), P(), P())
    out_specs = (P("layer", "row", None), P("layer", "row", None))
    return jax.shard_map(
        per_device, mesh=mesh, in_specs=in_specs, out_specs=out_specs, check_vma=False
    )
```

```python
import functools
import math

import jax
import jax.numpy as jnp
import ml_dtypes
import numpy as np
from jax import lax
from jax.experimental import pallas as pl
from jax.experimental.pallas import tpu as pltpu
from jax.sharding import PartitionSpec as P

GRID = 2048
KCUT = 672
ROWS = 32
MINE = 21
CHUNK = 6
KAP = 64
JP = 11
SPAN = 512
USED = MINE * 2 * JP
TILES = ((0, 0), (1, 0), (1, 1), (2, 1), (2, 2), (3, 2), (4, 2), (4, 3), (5, 3))
WINDOW = (0, 0, 1, 2, 2, 2)
HYPER_RATE = 0.2
STEP_SIZE = 0.5
BF16 = jnp.bfloat16
F32 = jnp.float32


def halves(table):
    high = table.astype(ml_dtypes.bfloat16)
    low = (table - high.astype(np.float64)).astype(ml_dtypes.bfloat16)
    return np.stack([high, low])


def turn(numerator, denominator):
    angle = 2.0 * math.pi * (np.mod(numerator, denominator) / denominator)
    return np.cos(angle), np.sin(angle)


def column_j(h, i):
    return 21 * h + i - 84 * (h // 2)


def x_forward_table():
    b = np.arange(128)
    table = np.zeros((2, 4, 2, 2, 8, 2, 128))
    for h in range(4):
        for i in range(MINE):
            c, s = turn(column_j(h, i) * b, 128)
            own = table[h // 2, i % 4, h % 2, :, i // 4]
            own[0, 0], own[0, 1], own[1, 0], own[1, 1] = c, s, -s, c
    return halves(table.reshape(2, 128, 256))


def x_inverse_table(by_chunk, times_i):
    b = np.arange(128)
    table = np.zeros((4, 4, 2, 6, 2, 128)) if by_chunk else np.zeros((4, 2, MINE, 2, 128))
    for h in range(4):
        for i in range(MINE):
            c, s = turn(column_j(h, i) * b, 128)
            if times_i:
                c, s = -s, c
            own = table[i % 4, h, :, i // 4] if by_chunk else table[h, :, i]
            own[0, 0], own[0, 1], own[1, 0], own[1, 1] = c, s, -s, c
    table = table.reshape(-1, 256) * (2.0 / (GRID * GRID))
    return halves(table if by_chunk else np.pad(table, ((0, 8), (0, 0))))


def x_twiddle():
    table = np.zeros((32, 128))
    c, s = turn(np.arange(9)[:, None] * np.arange(128)[None, :], GRID)
    table[0:9] = c
    table[16:25] = s
    return table.astype(np.float32)


def y_radix_table():
    c, s = turn(np.arange(KAP)[:, None] * np.arange(64)[None, :], 64)
    high, low = halves(np.concatenate([c, -s], axis=0))
    return np.concatenate([high, high, low], axis=1)


def y_radix_inverse_table():
    c, s = turn(np.arange(64)[:, None] * np.arange(KAP)[None, :], 64)
    high, low = halves(np.concatenate([c, -s], axis=1))
    return np.concatenate([high, high, low], axis=1)


def y_twiddle():
    c, s = turn(np.arange(KAP)[:, None] * np.arange(ROWS)[None, :], GRID)
    return np.stack([np.tile(c, (1, 4)), np.tile(s, (1, 4))]).astype(np.float32)


def lanes_of(jr):
    c, s = turn(np.arange(ROWS)[:, None] * np.arange(JP)[None, :], ROWS)
    table = np.zeros((2, 4, ROWS, SPAN))
    for jb in range(4):
        i = 4 * jr + jb
        if i < MINE:
            re = slice(2 * JP * i, 2 * JP * i + JP)
            im = slice(2 * JP * i + JP, 2 * JP * i + 2 * JP)
            table[0, jb, :, re], table[1, jb, :, re] = c, s
            table[0, jb, :, im], table[1, jb, :, im] = -s, c
    return table.reshape(256, SPAN)


def y_lane_table():
    return halves(np.stack([lanes_of(jr)[:, 128 * tile : 128 * tile + 128] for jr, tile in TILES]))


def y_lane_inverse_table(times_i):
    tables = []
    for jr in range(6):
        table = 2.0 * lanes_of(jr)[:, 128 * WINDOW[jr] : 128 * WINDOW[jr] + 256].T
        if times_i:
            table = np.concatenate([-table[:, 128:], table[:, :128]], axis=1)
        tables.append(table)
    return halves(np.stack(tables))


def y_projection_table():
    difference = np.arange(ROWS)[None, :] - np.arange(ROWS)[:, None]
    tables = []
    for count in (JP, JP - 1):
        c, s = turn(difference[:, :, None] * np.arange(count)[None, None, :], ROWS)
        c, s = np.kron(np.eye(4), 2 * c.sum(-1)), np.kron(np.eye(4), 2 * s.sum(-1))
        tables.append(np.block([[c, s], [-s, c]]))
    return halves(np.stack(tables))


def y_mean_table():
    return np.kron(np.eye(8), np.ones((ROWS, ROWS))).astype(ml_dtypes.bfloat16)


def lane_facts():
    lane = np.arange(SPAN)
    facts = np.zeros((8, SPAN))
    facts[0] = 16 * (lane // (2 * JP))
    facts[1] = 64 * (lane % JP)
    return facts.astype(np.float32)


def split(value):
    high = value.astype(BF16)
    low = (value - high.astype(F32)).astype(BF16)
    return high, low


def matmul(left, right, dims):
    def one(a, b):
        return lax.dot_general(a, b, (dims, ((), ())), preferred_element_type=F32)

    return one(left[0], right[0]) + (one(left[0], right[1]) + one(left[1], right[0]))


def matmul_deep(table, right):
    depth = right[0].shape[0]

    def one(a, b):
        return lax.dot_general(a, b, (NN, ((), ())), preferred_element_type=F32)

    both = jnp.concatenate(right, axis=0)
    return one(table[:, : 2 * depth], both) + one(table[:, 2 * depth :], right[0])


NN = ((1,), (0,))
NT = ((1,), (1,))
TN = ((0,), (0,))

C1 = math.cos(math.pi / 8)
C2 = math.cos(math.pi / 4)
C3 = math.cos(3 * math.pi / 8)


def real_analysis(x):
    s = [x[a] + x[a + 8] for a in range(8)]
    d = [x[a] - x[a + 8] for a in range(8)]
    e = [None] + [d[a] - d[8 - a] for a in range(1, 4)]
    f = [None] + [d[a] + d[8 - a] for a in range(1, 4)]
    e2, f2 = e[2] * C2, f[2] * C2
    plus, minus = d[0] + e2, d[0] - e2
    first, second = e[1] * C1 + e[3] * C3, e[1] * C3 - e[3] * C1
    third, fourth = f[1] * C3 + f[3] * C1, f[1] * C1 - f[3] * C3
    u, v = d[4] + f2, f2 - d[4]
    p = [s[a] + s[a + 4] for a in range(4)]
    q = [s[a] - s[a + 4] for a in range(4)]
    even, odd = p[0] + p[2], p[1] + p[3]
    hd, hs = (q[1] - q[3]) * C2, (q[1] + q[3]) * C2
    real = [
        even + odd,
        plus + first,
        q[0] + hd,
        minus + second,
        p[0] - p[2],
        minus - second,
        q[0] - hd,
        plus - first,
        even - odd,
    ]
    imag = [
        None,
        -(third + u),
        -(q[2] + hs),
        -(fourth + v),
        p[3] - p[1],
        v - fourth,
        q[2] - hs,
        u - third,
        None,
    ]
    return real, imag


def real_synthesis(real, imag):
    plus, first = real[1] + real[7], real[1] - real[7]
    minus, second = real[3] + real[5], real[3] - real[5]
    third, u = -(imag[1] + imag[7]), imag[7] - imag[1]
    fourth, v = -(imag[3] + imag[5]), imag[5] - imag[3]
    d = [None] * 8
    d[0], d[4] = plus + minus, u - v
    e = [None, first * C1 + second * C3, (plus - minus) * C2, first * C3 - second * C1]
    f = [None, third * C3 + fourth * C1, (u + v) * C2, third * C1 - fourth * C3]
    for a in range(1, 4):
        d[a], d[8 - a] = f[a] + e[a], f[a] - e[a]
    even, odd = real[0] + real[8], real[0] - real[8]
    p = [even + real[4], odd - imag[4], even - real[4], odd + imag[4]]
    hr, hi = (real[2] - real[6]) * C2, (imag[2] + imag[6]) * C2
    q = [real[2] + real[6], hr - hi, imag[6] - imag[2], -(hr + hi)]
    s = [p[a] + q[a] for a in range(4)] + [p[a] - q[a] for a in range(4)]
    return [s[a] + d[a] for a in range(8)] + [s[a] - d[a] for a in range(8)]


def regroup(blocks, wanted):
    block = lax.broadcasted_iota(jnp.int32, (1, 128), 1) // 32
    turned = [
        b if b is None or i == 0 else pltpu.roll(b, 32 * i, 1) for i, b in enumerate(blocks)
    ]
    results = []
    for p in wanted:
        total = None
        for i in range(4):
            part = jnp.zeros_like(turned[0]) if turned[i] is None else turned[i]
            total = part if total is None else jnp.where(block == (p + i) % 4, part, total)
        results.append(total if p == 0 else pltpu.roll(total, 128 - 32 * p, 1))
    return results


def turn_by(re, im, c, s):
    return re * c + im * s, im * c - re * s


def x_forward(real, imag, twiddle, table):
    pieces = []
    for k in range(9):
        if k == 0:
            pieces.append(jnp.concatenate([real[0], jnp.zeros_like(real[0])], axis=1))
            continue
        c, s = twiddle[k : k + 1], twiddle[16 + k : 17 + k]
        if k == 8:
            re, im = real[8] * c, -(real[8] * s)
        else:
            re, im = real[k] * c + imag[k] * s, imag[k] * c - real[k] * s
        pieces.append(jnp.concatenate([re, im], axis=1))
    shared = split(jnp.concatenate(pieces[1:8], axis=0))
    results = []
    for half, own in enumerate((pieces[0], pieces[8])):
        own = split(own)
        right = [jnp.concatenate([own[i], shared[i]], axis=0) for i in range(2)]
        results.append(matmul([table[0, half], table[1, half]], right, NT))
    return results


def modes_of(source, twiddle):
    real, imag = [], []
    for k in range(9):
        c, s = twiddle[k : k + 1], twiddle[16 + k : 17 + k]
        z = source(k)
        re, im = z[:, :128], z[:, 128:]
        if k == 0:
            real.append(re)
            imag.append(None)
        else:
            real.append(re * c - im * s)
            imag.append(None if k == 8 else re * s + im * c)
    return real, imag


def y_turned(in_ref, radix, twiddle):
    columns = [in_ref[pl.ds(jr, 64, stride=CHUNK), :] for jr in range(6)]
    high, low = split(jnp.concatenate(columns, axis=1))
    mixed = lax.dot_general(
        radix[...],
        jnp.concatenate([high, low, high], axis=0),
        (NN, ((), ())),
        preferred_element_type=F32,
    )
    results = []
    for jr in range(6):
        lanes = slice(128 * jr, 128 * jr + 128)
        re, im = turn_by(mixed[:KAP, lanes], mixed[KAP:, lanes], twiddle[0], twiddle[1])
        results.append(jnp.concatenate([re, im], axis=1))
    return results


def y_returned(pairs, radix, twiddle):
    turned = [turn_by(pair[:, :128], pair[:, 128:], twiddle[0], -twiddle[1]) for pair in pairs]
    right = [jnp.concatenate([pair[part] for pair in turned], axis=1) for part in range(2)]
    return matmul_deep(radix, split(jnp.concatenate(right, axis=0)))


def y_waves(facts):
    kap = lax.broadcasted_iota(jnp.int32, (KAP, 1), 0).astype(F32)
    return kap + facts[1:2]


def x_waves(facts, owner):
    slot = owner // 8
    h = (owner % 8) // 2
    eight = jnp.where(slot == 0, 8 * (h // 2), 0)
    return facts[0:1] + (slot + eight + 16 * (21 * h - 84 * (h // 2))).astype(F32)


def half_of_zero(wave):
    return jnp.where(wave == 0.0, 0.5, 1.0)


def store_x(out_ref, results, group):
    for half in range(2):
        lanes = slice(128 * group, 128 * group + 128)
        blocks = [results[half][32 * jb : 32 * jb + 32, lanes] for jb in range(4)]
        for slot, block in enumerate(regroup(blocks, range(4))):
            for own in range(4):
                start = (8 * (4 * group + slot) + 4 * half + own) * CHUNK
                out_ref[start : start + CHUNK, :] = block[8 * own : 8 * own + CHUNK]


def state_kernel(
    state_hbm, twiddle_hbm, table_hbm, out_hbm, state_ref, twiddle_ref, table_ref, out_ref, sems
):
    pairs = ((state_hbm, state_ref), (twiddle_hbm, twiddle_ref), (table_hbm, table_ref))
    copies = [pltpu.make_async_copy(a, b, sems.at[i]) for i, (a, b) in enumerate(pairs)]
    for copy in copies:
        copy.start()
    copies[0].wait()
    x = [state_ref[0, :, 128 * a : 128 * a + 128] for a in range(16)]
    real, imag = real_analysis(x)
    copies[1].wait()
    copies[2].wait()
    results = x_forward(real, imag, twiddle_ref[...], table_ref)
    sends = []
    for group in range(2):
        store_x(out_ref, results, group)
        rows = pl.ds(32 * group * CHUNK, 32 * CHUNK)
        sends.append(pltpu.make_async_copy(out_ref.at[rows], out_hbm.at[rows], sems.at[3 + group]))
        sends[-1].start()
    for send in sends:
        send.wait()


def weights_kernel(to_ref, from_ref, deform_ref, facts_ref, out_ref):
    facts = facts_ref[...]
    wave_x = x_waves(facts, lax.axis_index("row"))
    wave_y = y_waves(facts)
    square = (wave_x * wave_x + wave_y * wave_y)[:, :USED]
    layer = lax.axis_index("layer")
    modes = [from_ref[layer, m] * (-1.0 / (square + deform_ref[m])) for m in range(8)]
    for n in range(8):
        total = None
        for m in range(8):
            term = modes[m] * to_ref[m, n]
            total = term if total is None else total + term
        out_ref[n] = total


def spectrum_kernel(in_ref, radix_ref, turn_ref, lanes_ref, facts_ref, spec_ref, used_ref):
    turned = [split(pair) for pair in y_turned(in_ref, radix_ref, turn_ref)]
    wave_y = y_waves(facts_ref[...])
    for tile in range(4):
        total = None
        for index, (jr, own) in enumerate(TILES):
            if own == tile:
                part = matmul(turned[jr], [lanes_ref[0, index], lanes_ref[1, index]], NN)
                total = part if total is None else total + part
        lanes = slice(128 * tile, 128 * tile + 128)
        total = jnp.where(wave_y[:, lanes] < KCUT, total, 0.0)
        spec_ref[:, lanes] = total
        used = min(USED - 128 * tile, 128)
        used_ref[:, 128 * tile : 128 * tile + used] = total[:, :used]


def stream_kernel(
    weights_ref,
    all_ref,
    spec_ref,
    unradix_ref,
    turn_ref,
    unlanes_ref,
    unlanes_i_ref,
    facts_ref,
    out_ref,
    stream_ref,
):
    facts = facts_ref[...]
    wave_x = x_waves(facts, lax.axis_index("row"))
    wave_y = y_waves(facts)
    stream = None
    for n in range(8):
        term = weights_ref[n] * all_ref[n]
        stream = term if stream is None else stream + term
    stream_ref[:, SPAN - 128 :] = jnp.zeros((KAP, 128), F32)
    stream_ref[:, :USED] = stream
    stream = stream_ref[...]
    spectrum = spec_ref[...]
    along_y = wave_y * half_of_zero(wave_x)
    along_x = wave_x * half_of_zero(wave_y)
    both_y = split(jnp.concatenate([-along_y * stream, along_y * spectrum], axis=0))
    both_x = split(jnp.concatenate([along_x * stream, along_x * spectrum], axis=0))
    pairs = []
    for jr in range(6):
        lanes = slice(128 * WINDOW[jr], 128 * WINDOW[jr] + 256)
        for both, table in ((both_y, unlanes_i_ref), (both_x, unlanes_ref)):
            out = matmul([part[:, lanes] for part in both], [table[0, jr], table[1, jr]], NN)
            pairs += [out[:KAP], out[KAP:]]
    out = y_returned(pairs, unradix_ref, turn_ref)
    for jr in range(6):
        blocks = [out[:, 128 * (4 * jr + f) : 128 * (4 * jr + f) + 128] for f in range(4)]
        count = min(MINE - 4 * jr, 4)
        for jb, block in enumerate(regroup(blocks, range(count))):
            out_ref[pl.ds(4 * jr + jb, 64, stride=MINE), :] = block


def jacobian_kernel(
    in_ref, twiddle_ref, untable_ref, untable_i_ref, table_ref, out_ref, first0, first1, whole0, whole1, jac
):
    depth = 8 * MINE
    lane = lax.broadcasted_iota(jnp.int32, (1, 128), 1)
    row = lax.broadcasted_iota(jnp.int32, (depth, 1), 0)
    slots = [in_ref[depth * slot : depth * slot + depth, :] for slot in range(8)]
    spare = jnp.zeros((8, 128), F32)
    lower, upper = [], []
    for a, b in zip(slots[0::2], slots[1::2]):
        pair = [jnp.where(lane < 64, a, pltpu.roll(b, 64, 1)), jnp.where(lane < 64, pltpu.roll(a, 64, 1), b)]
        lower.append(jnp.concatenate([pair[0], spare], axis=0))
        upper.append(jnp.concatenate([pair[1], spare], axis=0))
    own = jnp.concatenate([jnp.where(row < depth // 2, slots[0], 0.0), spare], axis=0)
    own = split(own)
    tables = [[ref[0], ref[1]] for ref in (untable_ref, untable_i_ref)]
    first0[...] = matmul(own, tables[0], TN)
    first1[...] = matmul(own, tables[1], TN)
    whole0[...] = matmul(split(jnp.concatenate(lower, axis=1)), tables[0], TN)
    whole1[...] = matmul(split(jnp.concatenate(upper, axis=1)), tables[1], TN)
    twiddle = twiddle_ref[...]
    for block in range(4):
        rows = slice(8 * block, 8 * block + 8)

        def physical(field):
            first, whole = ((first0, whole0), (first1, whole1))[field // 2]

            def source(k):
                start = 32 * field + rows.start
                if k == 0:
                    return first[start : start + 8, :]
                start = 32 * (field % 2) + 64 * (k % 8) + rows.start
                z = whole[start : start + 8, :]
                return z if k < 8 else z - source(0)

            return real_synthesis(*modes_of(source, twiddle))

        east, slope_x = physical(0), physical(3)
        product = [a * b for a, b in zip(east, slope_x)]
        north, slope_y = physical(2), physical(1)
        product = [p + a * b for p, a, b in zip(product, north, slope_y)]
        real, imag = real_analysis(product)
        for k in range(9):
            jac[0, k, rows, :] = real[k]
            if imag[k] is not None:
                jac[1, k, rows, :] = imag[k]
    real = [jac[0, k] for k in range(9)]
    imag = [None] + [jac[1, k] for k in range(1, 8)] + [None]
    results = x_forward(real, imag, twiddle, table_ref)
    for group in range(2):
        store_x(out_ref, results, group)


def projection_kernel(
    in_ref, spec_ref, radix_ref, unradix_ref, turn_ref, project_ref, mean_ref, unlanes_ref, facts_ref, out_ref
):
    facts = facts_ref[...]
    wave_x = x_waves(facts, lax.axis_index("row"))
    wave_y = y_waves(facts)
    ratio = (wave_x * wave_x + wave_y * wave_y) * (1.0 / (KCUT * KCUT))
    ratio = ratio * ratio
    damped = split(((HYPER_RATE * (ratio * ratio)) * half_of_zero(wave_y)) * spec_ref[...])
    left = [split(pair) for pair in y_turned(in_ref, radix_ref, turn_ref)]
    sides = []
    for side in range(2):
        rows = slice(32 * side, 32 * side + 32)
        stacked = [jnp.concatenate([pair[i][rows] for pair in left], axis=0) for i in range(2)]
        sides.append(matmul(stacked, [project_ref[i, side] for i in range(2)], NN))
    first = lax.broadcasted_iota(jnp.int32, (16, 1), 0) == 0
    lane = lax.broadcasted_iota(jnp.int32, (1, 256), 1)
    zero_wave = (lax.axis_index("row") < 2) & (lane % 128 < 32)
    pairs = []
    for jr in range(6):
        mean = sum(
            lax.dot_general(
                left[jr][i][:16], mean_ref[...], (NN, ((), ())), preferred_element_type=F32
            )
            for i in range(2)
        )
        low, high = [side[32 * jr : 32 * jr + 32] for side in sides]
        low = jnp.concatenate([low[:16] - jnp.where(first, mean, 0.0), low[16:]], axis=0)
        window = [part[:, 128 * WINDOW[jr] : 128 * WINDOW[jr] + 256] for part in damped]
        damping = matmul(window, [unlanes_ref[i, jr] for i in range(2)], NN)
        total = jnp.concatenate([low, high], axis=0) + damping
        pairs.append(total * jnp.where(zero_wave, -0.5, -1.0) if jr == 0 else -total)
    out = y_returned(pairs, unradix_ref, turn_ref)
    for jr in range(6):
        out_ref[pl.ds(jr, 64, stride=CHUNK), :] = out[:, 128 * jr : 128 * jr + 128]


def state_update_kernel(
    in_ref,
    state_ref,
    start_ref,
    twiddle_ref,
    untable_ref,
    tendency_hbm,
    new_hbm,
    first,
    whole,
    tendency_ref,
    new_ref,
    sems,
):
    depth = 8 * CHUNK
    table = [untable_ref[0], untable_ref[1]]
    for group in range(2):
        blocks = [in_ref[depth * slot : depth * slot + depth, :] for slot in range(4 * group, 4 * group + 4)]
        side = jnp.concatenate(regroup(blocks, range(4)), axis=0)
        whole[128 * group : 128 * group + 128, :] = matmul(split(side), table, TN)
        if group == 0:
            row = lax.broadcasted_iota(jnp.int32, (4 * depth, 1), 0)
            own = jnp.where(row % depth < depth // 2, side, 0.0)
            first[...] = matmul(split(own), table, TN)
    twiddle = twiddle_ref[...]
    sends = []
    for block in range(4):
        rows = slice(8 * block, 8 * block + 8)

        def source(k):
            if k == 0:
                return first[rows, :]
            start = 32 * (k % 8) + rows.start
            z = whole[start : start + 8, :]
            return z if k < 8 else z - source(0)

        tendency = real_synthesis(*modes_of(source, twiddle))
        for a in range(16):
            columns = slice(128 * a, 128 * a + 128)
            tendency_ref[0, rows, columns] = tendency[a]
            new_ref[0, rows, columns] = 0.75 * start_ref[0, rows, columns] + 0.25 * (
                state_ref[0, rows, columns] + STEP_SIZE * tendency[a]
            )
        for i, (near, far) in enumerate(((tendency_ref, tendency_hbm), (new_ref, new_hbm))):
            own = (slice(None), pl.ds(8 * block, 8))
            sends.append(pltpu.make_async_copy(near.at[own], far.at[own], sems.at[2 * block + i]))
            sends[-1].start()
    for send in sends:
        send.wait()


VMEM = pl.BlockSpec(memory_space=pltpu.VMEM)
SMEM = pl.BlockSpec(memory_space=pltpu.SMEM)
ANY = pl.BlockSpec(memory_space=pl.ANY)
MIB = 1024 * 1024


def call(kernel, outs, operands, scalars=0, scratch=(), far_in=False, far_out=False, copies=0, cost=None):
    scratch_shapes = [pltpu.VMEM(operand.shape, operand.dtype) for operand in operands] if far_in else []
    scratch_shapes += [pltpu.VMEM(shape, F32) for shape in scratch]
    scratch_shapes += [pltpu.VMEM(shape, F32) for shape in outs] if far_out else []
    scratch_shapes += [pltpu.SemaphoreType.DMA((copies,))] if copies else []
    near = [SMEM] * scalars + [VMEM] * (len(operands) - scalars)
    return pl.pallas_call(
        kernel,
        out_shape=[jax.ShapeDtypeStruct(shape, F32) for shape in outs],
        in_specs=[ANY] * len(operands) if far_in else near,
        out_specs=[ANY if far_out else VMEM] * len(outs),
        scratch_shapes=scratch_shapes,
        compiler_params=pltpu.CompilerParams(vmem_limit_bytes=(60 if far_in else 32) * MIB),
        cost_estimate=cost,
    )(*operands)


def exchange(chunks, devices):
    length = chunks.shape[0]
    sent = chunks.reshape(devices, 1, length * 128 // devices)
    return lax.all_to_all(sent, "row", split_axis=0, concat_axis=0, tiled=True).reshape(length, 128)


def per_device(state, start_state, to_modes, from_modes, deform):
    devices = lax.axis_size("row")
    turn_x = jnp.asarray(x_twiddle())
    forward_x = jnp.asarray(x_forward_table())
    inverse_x = jnp.asarray(x_inverse_table(False, False))
    inverse_ix = jnp.asarray(x_inverse_table(False, True))
    inverse_chunk = jnp.asarray(x_inverse_table(True, False))
    radix = jnp.asarray(y_radix_table())
    unradix = jnp.asarray(y_radix_inverse_table())
    turn_y = jnp.asarray(y_twiddle())
    lanes = jnp.asarray(y_lane_table())
    unlanes = jnp.asarray(y_lane_inverse_table(False))
    unlanes_i = jnp.asarray(y_lane_inverse_table(True))
    project = jnp.asarray(y_projection_table())
    mean = jnp.asarray(y_mean_table())
    facts = jnp.asarray(lane_facts())

    one, four = (64 * CHUNK, 128), (64 * MINE, 128)
    (columns,) = call(state_kernel, [one], [state, turn_x, forward_x], far_in=True, far_out=True, copies=5)
    columns = exchange(columns, devices)
    spectrum, used = call(
        spectrum_kernel, [(KAP, SPAN), (KAP, USED)], [columns, radix, turn_y, lanes, facts]
    )
    (weights,) = call(
        weights_kernel,
        [(8, KAP, USED)],
        [to_modes, from_modes, deform, facts],
        scalars=3,
        cost=pl.CostEstimate(flops=8_000_000, bytes_accessed=2_000_000, transcendentals=0),
    )
    gathered = lax.all_gather(used, "layer", axis=0, tiled=False)
    (fields,) = call(
        stream_kernel,
        [four],
        [weights, gathered, spectrum, unradix, turn_y, unlanes, unlanes_i, facts],
        scratch=[(KAP, SPAN)],
    )
    fields = exchange(fields, devices)
    (flux,) = call(
        jacobian_kernel,
        [one],
        [fields, turn_x, inverse_x, inverse_ix, forward_x],
        scratch=[(128, 256)] * 2 + [(512, 256)] * 2 + [(2, 9, ROWS, 128)],
    )
    flux = exchange(flux, devices)
    (total,) = call(
        projection_kernel,
        [one],
        [flux, spectrum, radix, unradix, turn_y, project, mean, unlanes, facts],
    )
    total = exchange(total, devices)
    return tuple(
        call(
            state_update_kernel,
            [(1, ROWS, GRID)] * 2,
            [total, state, start_state, turn_x, inverse_chunk],
            scratch=[(128, 256), (256, 256)],
            far_out=True,
            copies=8,
        )
    )


def solution(mesh):
    in_specs = (P("layer", "row", None), P("layer", "row", None), P(), P(), P())
    out_specs = (P("layer", "row", None), P("layer", "row", None))
    return jax.shard_map(
        per_device, mesh=mesh, in_specs=in_specs, out_specs=out_specs, check_vma=False
    )
```

```python
import functools
import math

import jax
import jax.numpy as jnp
import ml_dtypes
import numpy as np
from jax import lax
from jax.experimental import pallas as pl
from jax.experimental.pallas import tpu as pltpu
from jax.sharding import PartitionSpec as P

GRID = 2048
KCUT = 672
ROWS = 32
MINE = 21
CHUNK = 6
KAP = 64
JP = 11
PIECE = 4 * 2 * JP
USED = MINE * 2 * JP
HYPER_RATE = 0.2
STEP_SIZE = 0.5
BF16 = jnp.bfloat16
F32 = jnp.float32


def halves(table):
    high = table.astype(ml_dtypes.bfloat16)
    low = (table - high.astype(np.float64)).astype(ml_dtypes.bfloat16)
    return np.stack([high, low])


def turn(numerator, denominator):
    angle = 2.0 * math.pi * (np.mod(numerator, denominator) / denominator)
    return np.cos(angle), np.sin(angle)


def column_j(h, i):
    return 21 * h + i - 84 * (h // 2)


def x_forward_table():
    b = np.arange(128)
    table = np.zeros((2, 4, 2, 2, 8, 2, 128))
    for h in range(4):
        for i in range(MINE):
            c, s = turn(column_j(h, i) * b, 128)
            own = table[h // 2, i % 4, h % 2, :, i // 4]
            own[0, 0], own[0, 1], own[1, 0], own[1, 1] = c, s, -s, c
    return halves(table.reshape(2, 128, 256))


def x_inverse_table(by_chunk):
    b = np.arange(128)
    table = np.zeros((4, 4, 2, 6, 2, 128)) if by_chunk else np.zeros((4, 2, MINE, 2, 128))
    for h in range(4):
        for i in range(MINE):
            c, s = turn(column_j(h, i) * b, 128)
            own = table[i % 4, h, :, i // 4] if by_chunk else table[h, :, i]
            own[0, 0], own[0, 1], own[1, 0], own[1, 1] = c, s, -s, c
    table = table.reshape(-1, 256) * (2.0 / (GRID * GRID))
    return halves(table if by_chunk else np.pad(table, ((0, 8), (0, 0))))


def x_twiddle():
    table = np.zeros((32, 128))
    c, s = turn(np.arange(9)[:, None] * np.arange(128)[None, :], GRID)
    table[0:9] = c
    table[16:25] = s
    return table.astype(np.float32)


def y_radix_table():
    c, s = turn(np.arange(KAP)[:, None] * np.arange(64)[None, :], 64)
    high, low = halves(np.concatenate([c, -s], axis=0))
    return np.concatenate([high, high, low], axis=1)


def y_radix_inverse_table():
    c, s = turn(np.arange(64)[:, None] * np.arange(KAP)[None, :], 64)
    high, low = halves(np.concatenate([c, -s], axis=1))
    return np.concatenate([high, high, low], axis=1)


def y_twiddle():
    c, s = turn(np.arange(KAP)[:, None] * np.arange(ROWS)[None, :], GRID)
    return np.stack([np.tile(c, (1, 4)), np.tile(s, (1, 4))]).astype(np.float32)


def lanes_of():
    c, s = turn(np.arange(ROWS)[:, None] * np.arange(JP)[None, :], ROWS)
    table = np.zeros((2, 4, ROWS, 128))
    for jb in range(4):
        re = slice(2 * JP * jb, 2 * JP * jb + JP)
        im = slice(2 * JP * jb + JP, 2 * JP * jb + 2 * JP)
        table[0, jb, :, re], table[1, jb, :, re] = c, s
        table[0, jb, :, im], table[1, jb, :, im] = -s, c
    return table.reshape(256, 128)


def y_lane_table():
    return halves(lanes_of())


def y_lane_inverse_table():
    high, low = halves(2.0 * lanes_of().T)
    return np.concatenate([high, high, low], axis=0)


def y_projection_table():
    difference = np.arange(ROWS)[None, :] - np.arange(ROWS)[:, None]
    tables = []
    for count in (JP, JP - 1):
        c, s = turn(difference[:, :, None] * np.arange(count)[None, None, :], ROWS)
        c, s = np.kron(np.eye(4), 2 * c.sum(-1)), np.kron(np.eye(4), 2 * s.sum(-1))
        tables.append(np.block([[c, s], [-s, c]]))
    return halves(np.stack(tables))


def y_mean_table():
    return np.kron(np.eye(8), np.ones((ROWS, ROWS))).astype(ml_dtypes.bfloat16)


def lane_facts(packed):
    lane = np.arange(512 if packed else 128)
    facts = np.zeros((8, lane.size))
    facts[0] = 16 * (lane // (2 * JP))
    facts[1] = 64 * (lane % JP)
    return facts.astype(np.float32)


def split(value):
    high = value.astype(BF16)
    low = (value - high.astype(F32)).astype(BF16)
    return high, low


def matmul(left, right, dims):
    def one(a, b):
        return lax.dot_general(a, b, (dims, ((), ())), preferred_element_type=F32)

    return one(left[0], right[0]) + (one(left[0], right[1]) + one(left[1], right[0]))


def matmul_deep(table, right):
    depth = right[0].shape[0]

    def one(a, b):
        return lax.dot_general(a, b, (NN, ((), ())), preferred_element_type=F32)

    both = jnp.concatenate(right, axis=0)
    return one(table[:, : 2 * depth], both) + one(table[:, 2 * depth :], right[0])


def matmul_wide(left, table):
    depth = left[0].shape[1]

    def one(a, b):
        return lax.dot_general(a, b, (NN, ((), ())), preferred_element_type=F32)

    both = jnp.concatenate(left, axis=1)
    return one(both, table[: 2 * depth]) + one(left[0], table[2 * depth :])


NN = ((1,), (0,))
NT = ((1,), (1,))
TN = ((0,), (0,))

C1 = math.cos(math.pi / 8)
C2 = math.cos(math.pi / 4)
C3 = math.cos(3 * math.pi / 8)


def real_analysis(x):
    s = [x[a] + x[a + 8] for a in range(8)]
    d = [x[a] - x[a + 8] for a in range(8)]
    e = [None] + [d[a] - d[8 - a] for a in range(1, 4)]
    f = [None] + [d[a] + d[8 - a] for a in range(1, 4)]
    e2, f2 = e[2] * C2, f[2] * C2
    plus, minus = d[0] + e2, d[0] - e2
    first, second = e[1] * C1 + e[3] * C3, e[1] * C3 - e[3] * C1
    third, fourth = f[1] * C3 + f[3] * C1, f[1] * C1 - f[3] * C3
    u, v = d[4] + f2, f2 - d[4]
    p = [s[a] + s[a + 4] for a in range(4)]
    q = [s[a] - s[a + 4] for a in range(4)]
    even, odd = p[0] + p[2], p[1] + p[3]
    hd, hs = (q[1] - q[3]) * C2, (q[1] + q[3]) * C2
    real = [
        even + odd,
        plus + first,
        q[0] + hd,
        minus + second,
        p[0] - p[2],
        minus - second,
        q[0] - hd,
        plus - first,
        even - odd,
    ]
    imag = [
        None,
        -(third + u),
        -(q[2] + hs),
        -(fourth + v),
        p[3] - p[1],
        v - fourth,
        q[2] - hs,
        u - third,
        None,
    ]
    return real, imag


def real_synthesis(real, imag):
    plus, first = real[1] + real[7], real[1] - real[7]
    minus, second = real[3] + real[5], real[3] - real[5]
    third, u = -(imag[1] + imag[7]), imag[7] - imag[1]
    fourth, v = -(imag[3] + imag[5]), imag[5] - imag[3]
    d = [None] * 8
    d[0], d[4] = plus + minus, u - v
    e = [None, first * C1 + second * C3, (plus - minus) * C2, first * C3 - second * C1]
    f = [None, third * C3 + fourth * C1, (u + v) * C2, third * C1 - fourth * C3]
    for a in range(1, 4):
        d[a], d[8 - a] = f[a] + e[a], f[a] - e[a]
    even, odd = real[0] + real[8], real[0] - real[8]
    p = [even + real[4], odd - imag[4], even - real[4], odd + imag[4]]
    hr, hi = (real[2] - real[6]) * C2, (imag[2] + imag[6]) * C2
    q = [real[2] + real[6], hr - hi, imag[6] - imag[2], -(hr + hi)]
    s = [p[a] + q[a] for a in range(4)] + [p[a] - q[a] for a in range(4)]
    return [s[a] + d[a] for a in range(8)] + [s[a] - d[a] for a in range(8)]


def regroup(blocks, wanted):
    block = lax.broadcasted_iota(jnp.int32, (1, 128), 1) // 32
    turned = [
        b if b is None or i == 0 else pltpu.roll(b, 32 * i, 1) for i, b in enumerate(blocks)
    ]
    results = []
    for p in wanted:
        total = None
        for i in range(4):
            part = jnp.zeros_like(turned[0]) if turned[i] is None else turned[i]
            total = part if total is None else jnp.where(block == (p + i) % 4, part, total)
        results.append(total if p == 0 else pltpu.roll(total, 128 - 32 * p, 1))
    return results


def turn_by(re, im, c, s):
    return re * c + im * s, im * c - re * s


def x_forward(real, imag, twiddle, table):
    pieces = []
    for k in range(9):
        if k == 0:
            pieces.append(jnp.concatenate([real[0], jnp.zeros_like(real[0])], axis=1))
            continue
        c, s = twiddle[k : k + 1], twiddle[16 + k : 17 + k]
        if k == 8:
            re, im = real[8] * c, -(real[8] * s)
        else:
            re, im = real[k] * c + imag[k] * s, imag[k] * c - real[k] * s
        pieces.append(jnp.concatenate([re, im], axis=1))
    shared = split(jnp.concatenate(pieces[1:8], axis=0))
    results = []
    for half, own in enumerate((pieces[0], pieces[8])):
        own = split(own)
        right = [jnp.concatenate([own[i], shared[i]], axis=0) for i in range(2)]
        results.append(matmul([table[0, half], table[1, half]], right, NT))
    return results


def modes_of(source, twiddle, turned=False):
    real, imag = [], []
    for k in range(9):
        c, s = twiddle[k : k + 1], twiddle[16 + k : 17 + k]
        z = source(k)
        re, im = z[:, :128], z[:, 128:]
        if k == 0:
            real.append(im if turned else re)
            imag.append(None)
            continue
        real.append(im * c + re * s if turned else re * c - im * s)
        if k == 8:
            imag.append(None)
        else:
            imag.append(im * s - re * c if turned else re * s + im * c)
    return real, imag


def y_turned(in_ref, radix, twiddle):
    columns = [in_ref[pl.ds(jr, 64, stride=CHUNK), :] for jr in range(6)]
    high, low = split(jnp.concatenate(columns, axis=1))
    mixed = lax.dot_general(
        radix[...],
        jnp.concatenate([high, low, high], axis=0),
        (NN, ((), ())),
        preferred_element_type=F32,
    )
    results = []
    for jr in range(6):
        lanes = slice(128 * jr, 128 * jr + 128)
        re, im = turn_by(mixed[:KAP, lanes], mixed[KAP:, lanes], twiddle[0], twiddle[1])
        results.append(jnp.concatenate([re, im], axis=1))
    return results


def y_returned(pairs, radix, twiddle):
    c, s = twiddle[0], twiddle[1]
    real, imag = [], []
    for pair, turned in pairs:
        re, im = pair[:, :128], pair[:, 128:]
        real.append(im * c + re * s if turned else re * c - im * s)
        imag.append(im * s - re * c if turned else re * s + im * c)
    right = jnp.concatenate([jnp.concatenate(real, axis=1), jnp.concatenate(imag, axis=1)], axis=0)
    return matmul_deep(radix, split(right))


def pack(tiles):
    lane = lax.broadcasted_iota(jnp.int32, (1, 128), 1)
    packed = [None] * 4
    for jr, tile in enumerate(tiles):
        index, offset = divmod(PIECE * jr, 128)
        moved = pltpu.roll(tile, offset, 1) if offset else tile
        parts = [(index, moved)]
        if offset + PIECE > 128:
            parts = [(index, jnp.where(lane >= offset, moved, 0.0))]
            parts.append((index + 1, jnp.where(lane < offset, moved, 0.0)))
        for own, part in parts:
            if own < 4:
                packed[own] = part if packed[own] is None else packed[own] + part
    return packed


def unpack(packed):
    lane = lax.broadcasted_iota(jnp.int32, (1, 128), 1)
    tiles = []
    for jr in range(6):
        index, offset = divmod(PIECE * jr, 128)
        tile = packed[:, 128 * index : 128 * index + 128]
        if offset + PIECE > 128:
            later = packed[:, 128 * index + 128 : 128 * index + 256] if index < 3 else 0.0
            tile = jnp.where(lane >= offset, tile, later)
        tiles.append(pltpu.roll(tile, 128 - offset, 1) if offset else tile)
    return tiles


def y_waves(facts):
    kap = lax.broadcasted_iota(jnp.int32, (KAP, 1), 0).astype(F32)
    return kap + facts[1:2]


def x_waves(facts, owner):
    slot = owner // 8
    h = (owner % 8) // 2
    eight = jnp.where(slot == 0, 8 * (h // 2), 0)
    return facts[0:1] + (slot + eight + 16 * (21 * h - 84 * (h // 2))).astype(F32)


def half_of_zero(wave):
    return jnp.where(wave == 0.0, 0.5, 1.0)


def store_x(out_ref, results, group):
    for half in range(2):
        lanes = slice(128 * group, 128 * group + 128)
        blocks = [results[half][32 * jb : 32 * jb + 32, lanes] for jb in range(4)]
        for slot, block in enumerate(regroup(blocks, range(4))):
            for own in range(4):
                start = (8 * (4 * group + slot) + 4 * half + own) * CHUNK
                out_ref[start : start + CHUNK, :] = block[8 * own : 8 * own + CHUNK]


def state_kernel(
    state_hbm, twiddle_hbm, table_hbm, out_hbm, state_ref, twiddle_ref, table_ref, out_ref, sems
):
    pairs = ((state_hbm, state_ref), (twiddle_hbm, twiddle_ref), (table_hbm, table_ref))
    copies = [pltpu.make_async_copy(a, b, sems.at[i]) for i, (a, b) in enumerate(pairs)]
    for copy in copies:
        copy.start()
    copies[0].wait()
    x = [state_ref[0, :, 128 * a : 128 * a + 128] for a in range(16)]
    real, imag = real_analysis(x)
    copies[1].wait()
    copies[2].wait()
    results = x_forward(real, imag, twiddle_ref[...], table_ref)
    sends = []
    for group in range(2):
        store_x(out_ref, results, group)
        rows = pl.ds(32 * group * CHUNK, 32 * CHUNK)
        sends.append(pltpu.make_async_copy(out_ref.at[rows], out_hbm.at[rows], sems.at[3 + group]))
        sends[-1].start()
    for send in sends:
        send.wait()


def weights_kernel(to_ref, from_ref, deform_ref, facts_ref, out_ref):
    facts = facts_ref[...]
    wave_x = x_waves(facts, lax.axis_index("row"))
    wave_y = y_waves(facts)
    square = (wave_x * wave_x + wave_y * wave_y)[:, :USED]
    layer = lax.axis_index("layer")
    modes = [from_ref[layer, m] * (-1.0 / (square + deform_ref[m])) for m in range(8)]
    for n in range(8):
        total = None
        for m in range(8):
            term = modes[m] * to_ref[m, n]
            total = term if total is None else total + term
        out_ref[n] = total


def spectrum_kernel(in_ref, radix_ref, turn_ref, lanes_ref, facts_ref, spec_ref, used_ref):
    turned = split(jnp.concatenate(y_turned(in_ref, radix_ref, turn_ref), axis=0))
    spectrum = matmul(turned, lanes_ref, NN)
    kept = y_waves(facts_ref[...]) < KCUT
    tiles = [jnp.where(kept, spectrum[KAP * jr : KAP * jr + KAP], 0.0) for jr in range(6)]
    spec_ref[...] = jnp.concatenate(tiles, axis=0)
    for index, tile in enumerate(pack(tiles)):
        used = min(USED - 128 * index, 128)
        used_ref[:, 128 * index : 128 * index + used] = tile[:, :used]


def stream_kernel(
    weights_ref, all_ref, spec_ref, unradix_ref, turn_ref, unlanes_ref, facts_ref, out_ref, stream_ref
):
    stream = None
    for n in range(8):
        term = weights_ref[n] * all_ref[n]
        stream = term if stream is None else stream + term
    stream_ref[:, 384:] = jnp.zeros((KAP, 128), F32)
    stream_ref[:, :USED] = stream
    facts = facts_ref[...]
    wave_y = y_waves(facts)
    once = half_of_zero(wave_y)
    pieces = []
    for jr, tile in enumerate(unpack(stream_ref[...])):
        wave_x = x_waves(facts, lax.axis_index("row")) + 64 * jr
        along_y, along_x = wave_y * half_of_zero(wave_x), wave_x * once
        own = spec_ref[KAP * jr : KAP * jr + KAP, :]
        pieces += [along_y * tile, -along_y * own, along_x * tile, along_x * own]
    out = matmul_wide(split(jnp.concatenate(pieces, axis=0)), unlanes_ref)
    pairs = [(out[KAP * i : KAP * i + KAP], i % 4 < 2) for i in range(24)]
    out = y_returned(pairs, unradix_ref, turn_ref)
    for jr in range(6):
        blocks = [out[:, 128 * (4 * jr + f) : 128 * (4 * jr + f) + 128] for f in range(4)]
        count = min(MINE - 4 * jr, 4)
        for jb, block in enumerate(regroup(blocks, range(count))):
            out_ref[pl.ds(4 * jr + jb, 64, stride=MINE), :] = block


def jacobian_kernel(in_ref, twiddle_ref, untable_ref, table_ref, out_ref, first_ref, whole_ref, jac):
    depth = 8 * MINE
    row = lax.broadcasted_iota(jnp.int32, (depth, 1), 0)
    spare = jnp.zeros((8, 4 * 128), F32)
    table = [untable_ref[0], untable_ref[1]]
    for part in range(2):
        slots = [
            in_ref[depth * slot : depth * slot + depth, :] for slot in range(4 * part, 4 * part + 4)
        ]
        side = jnp.concatenate([jnp.concatenate(slots, axis=1), spare], axis=0)
        whole_ref[512 * part : 512 * part + 512, :] = matmul(split(side), table, TN)
        if part == 0:
            own = jnp.concatenate([jnp.where(row < depth // 2, slots[0], 0.0), spare[:, :128]], axis=0)
            first_ref[...] = matmul(split(own), table, TN)
    twiddle = twiddle_ref[...]
    for block in range(4):
        rows = slice(8 * block, 8 * block + 8)

        def physical(field):
            def source(k):
                start = 32 * field + rows.start
                if k == 0:
                    return first_ref[start : start + 8, :]
                start += 128 * (k % 8)
                z = whole_ref[start : start + 8, :]
                return z if k < 8 else z - source(0)

            return real_synthesis(*modes_of(source, twiddle, field > 1))

        east, slope_x = physical(0), physical(3)
        product = [a * b for a, b in zip(east, slope_x)]
        north, slope_y = physical(2), physical(1)
        product = [p + a * b for p, a, b in zip(product, north, slope_y)]
        real, imag = real_analysis(product)
        for k in range(9):
            jac[0, k, rows, :] = real[k]
            if imag[k] is not None:
                jac[1, k, rows, :] = imag[k]
    real = [jac[0, k] for k in range(9)]
    imag = [None] + [jac[1, k] for k in range(1, 8)] + [None]
    results = x_forward(real, imag, twiddle, table_ref)
    for group in range(2):
        store_x(out_ref, results, group)


def projection_kernel(
    in_ref, spec_ref, radix_ref, unradix_ref, turn_ref, project_ref, mean_ref, unlanes_ref, facts_ref, out_ref
):
    facts = facts_ref[...]
    wave_y = y_waves(facts)
    once = half_of_zero(wave_y)
    damped = []
    for jr in range(6):
        wave_x = x_waves(facts, lax.axis_index("row")) + 64 * jr
        ratio = (wave_x * wave_x + wave_y * wave_y) * (1.0 / (KCUT * KCUT))
        ratio = ratio * ratio
        damped.append(((HYPER_RATE * (ratio * ratio)) * once) * spec_ref[KAP * jr : KAP * jr + KAP, :])
    damping = matmul_wide(split(jnp.concatenate(damped, axis=0)), unlanes_ref)
    left = [split(pair) for pair in y_turned(in_ref, radix_ref, turn_ref)]
    sides = []
    for side in range(2):
        rows = slice(32 * side, 32 * side + 32)
        stacked = [jnp.concatenate([pair[i][rows] for pair in left], axis=0) for i in range(2)]
        sides.append(matmul(stacked, [project_ref[i, side] for i in range(2)], NN))
    heads = [jnp.concatenate([pair[i][:16] for pair in left], axis=0) for i in range(2)]
    mean = sum(
        lax.dot_general(head, mean_ref[...], (NN, ((), ())), preferred_element_type=F32)
        for head in heads
    )
    first = lax.broadcasted_iota(jnp.int32, (16, 1), 0) == 0
    lane = lax.broadcasted_iota(jnp.int32, (1, 256), 1)
    zero_wave = (lax.axis_index("row") < 2) & (lane % 128 < 32)
    pairs = []
    for jr in range(6):
        low, high = [side[32 * jr : 32 * jr + 32] for side in sides]
        own = jnp.where(first, mean[16 * jr : 16 * jr + 16], 0.0)
        flux = jnp.concatenate([low[:16] - own, low[16:], high], axis=0)
        total = flux - damping[KAP * jr : KAP * jr + KAP]
        pairs.append((total * jnp.where(zero_wave, 0.5, 1.0) if jr == 0 else total, False))
    out = y_returned(pairs, unradix_ref, turn_ref)
    for jr in range(6):
        out_ref[pl.ds(jr, 64, stride=CHUNK), :] = out[:, 128 * jr : 128 * jr + 128]


def state_update_kernel(
    in_ref,
    state_ref,
    start_ref,
    twiddle_ref,
    untable_ref,
    tendency_hbm,
    new_hbm,
    first,
    whole,
    tendency_ref,
    new_ref,
    sems,
):
    depth = 8 * CHUNK
    table = [untable_ref[0], untable_ref[1]]
    for group in range(2):
        blocks = [in_ref[depth * slot : depth * slot + depth, :] for slot in range(4 * group, 4 * group + 4)]
        side = jnp.concatenate(regroup(blocks, range(4)), axis=0)
        whole[128 * group : 128 * group + 128, :] = matmul(split(side), table, TN)
        if group == 0:
            row = lax.broadcasted_iota(jnp.int32, (4 * depth, 1), 0)
            own = jnp.where(row % depth < depth // 2, side, 0.0)
            first[...] = matmul(split(own), table, TN)
    twiddle = twiddle_ref[...]
    sends = []
    for block in range(4):
        rows = slice(8 * block, 8 * block + 8)

        def source(k):
            if k == 0:
                return first[rows, :]
            start = 32 * (k % 8) + rows.start
            z = whole[start : start + 8, :]
            return z if k < 8 else z - source(0)

        tendency = real_synthesis(*modes_of(source, twiddle))
        for a in range(16):
            columns = slice(128 * a, 128 * a + 128)
            tendency_ref[0, rows, columns] = tendency[a]
            new_ref[0, rows, columns] = 0.75 * start_ref[0, rows, columns] + 0.25 * (
                state_ref[0, rows, columns] + STEP_SIZE * tendency[a]
            )
        for i, (near, far) in enumerate(((tendency_ref, tendency_hbm), (new_ref, new_hbm))):
            own = (slice(None), pl.ds(8 * block, 8))
            sends.append(pltpu.make_async_copy(near.at[own], far.at[own], sems.at[2 * block + i]))
            sends[-1].start()
    for send in sends:
        send.wait()


VMEM = pl.BlockSpec(memory_space=pltpu.VMEM)
SMEM = pl.BlockSpec(memory_space=pltpu.SMEM)
ANY = pl.BlockSpec(memory_space=pl.ANY)
MIB = 1024 * 1024


def call(kernel, outs, operands, scalars=0, scratch=(), far_in=False, far_out=False, copies=0, cost=None):
    scratch_shapes = [pltpu.VMEM(operand.shape, operand.dtype) for operand in operands] if far_in else []
    scratch_shapes += [pltpu.VMEM(shape, F32) for shape in scratch]
    scratch_shapes += [pltpu.VMEM(shape, F32) for shape in outs] if far_out else []
    scratch_shapes += [pltpu.SemaphoreType.DMA((copies,))] if copies else []
    near = [SMEM] * scalars + [VMEM] * (len(operands) - scalars)
    return pl.pallas_call(
        kernel,
        out_shape=[jax.ShapeDtypeStruct(shape, F32) for shape in outs],
        in_specs=[ANY] * len(operands) if far_in else near,
        out_specs=[ANY if far_out else VMEM] * len(outs),
        scratch_shapes=scratch_shapes,
        compiler_params=pltpu.CompilerParams(vmem_limit_bytes=(60 if far_in else 32) * MIB),
        cost_estimate=cost,
    )(*operands)


def exchange(chunks, devices):
    length = chunks.shape[0]
    sent = chunks.reshape(devices, 1, length * 128 // devices)
    return lax.all_to_all(sent, "row", split_axis=0, concat_axis=0, tiled=True).reshape(length, 128)


def per_device(state, start_state, to_modes, from_modes, deform):
    devices = lax.axis_size("row")
    turn_x = jnp.asarray(x_twiddle())
    forward_x = jnp.asarray(x_forward_table())
    inverse_x = jnp.asarray(x_inverse_table(False))
    inverse_chunk = jnp.asarray(x_inverse_table(True))
    radix = jnp.asarray(y_radix_table())
    unradix = jnp.asarray(y_radix_inverse_table())
    turn_y = jnp.asarray(y_twiddle())
    lanes = jnp.asarray(y_lane_table())
    unlanes = jnp.asarray(y_lane_inverse_table())
    project = jnp.asarray(y_projection_table())
    mean = jnp.asarray(y_mean_table())
    facts = jnp.asarray(lane_facts(False))
    packed_facts = jnp.asarray(lane_facts(True))

    one, four = (64 * CHUNK, 128), (64 * MINE, 128)
    (columns,) = call(state_kernel, [one], [state, turn_x, forward_x], far_in=True, far_out=True, copies=5)
    columns = exchange(columns, devices)
    spectrum, used = call(
        spectrum_kernel, [(6 * KAP, 128), (KAP, USED)], [columns, radix, turn_y, lanes, facts]
    )
    (weights,) = call(
        weights_kernel,
        [(8, KAP, USED)],
        [to_modes, from_modes, deform, packed_facts],
        scalars=3,
        cost=pl.CostEstimate(flops=8_000_000, bytes_accessed=2_000_000, transcendentals=0),
    )
    gathered = lax.all_gather(used, "layer", axis=0, tiled=False)
    (fields,) = call(
        stream_kernel,
        [four],
        [weights, gathered, spectrum, unradix, turn_y, unlanes, facts],
        scratch=[(KAP, 512)],
    )
    fields = exchange(fields, devices)
    (flux,) = call(
        jacobian_kernel,
        [one],
        [fields, turn_x, inverse_x, forward_x],
        scratch=[(128, 256), (1024, 256), (2, 9, ROWS, 128)],
    )
    flux = exchange(flux, devices)
    (total,) = call(
        projection_kernel,
        [one],
        [flux, spectrum, radix, unradix, turn_y, project, mean, unlanes, facts],
    )
    total = exchange(total, devices)
    return tuple(
        call(
            state_update_kernel,
            [(1, ROWS, GRID)] * 2,
            [total, state, start_state, turn_x, inverse_chunk],
            scratch=[(128, 256), (256, 256)],
            far_out=True,
            copies=8,
        )
    )


def solution(mesh):
    in_specs = (P("layer", "row", None), P("layer", "row", None), P(), P(), P())
    out_specs = (P("layer", "row", None), P("layer", "row", None))
    return jax.shard_map(
        per_device, mesh=mesh, in_specs=in_specs, out_specs=out_specs, check_vma=False
    )
```

```python
import functools
import math

import jax
import jax.numpy as jnp
import ml_dtypes
import numpy as np
from jax import lax
from jax.experimental import pallas as pl
from jax.experimental.pallas import tpu as pltpu
from jax.sharding import PartitionSpec as P

GRID = 2048
KCUT = 672
ROWS = 32
MINE = 21
CHUNK = 6
KAP = 64
JP = 11
PIECE = 4 * 2 * JP
USED = MINE * 2 * JP
HYPER_RATE = 0.2
STEP_SIZE = 0.5
BF16 = jnp.bfloat16
F32 = jnp.float32


def halves(table):
    high = table.astype(ml_dtypes.bfloat16)
    low = (table - high.astype(np.float64)).astype(ml_dtypes.bfloat16)
    return np.stack([high, low])


def turn(numerator, denominator):
    angle = 2.0 * math.pi * (np.mod(numerator, denominator) / denominator)
    return np.cos(angle), np.sin(angle)


def column_j(h, i):
    return 21 * h + i - 84 * (h // 2)


def x_forward_table():
    b = np.arange(128)
    table = np.zeros((2, 4, 2, 2, 6, 2, 128))
    for h in range(4):
        for i in range(MINE):
            c, s = turn(column_j(h, i) * b, 128)
            own = table[h // 2, i % 4, h % 2, :, i // 4]
            own[0, 0], own[0, 1], own[1, 0], own[1, 1] = c, s, -s, c
    return np.concatenate(list(halves(table.reshape(2, 96, 256))), axis=1)


def x_inverse_table(by_chunk):
    b = np.arange(128)
    table = np.zeros((4, 4, 2, 6, 2, 128)) if by_chunk else np.zeros((4, 2, MINE, 2, 128))
    for h in range(4):
        for i in range(MINE):
            c, s = turn(column_j(h, i) * b, 128)
            own = table[i % 4, h, :, i // 4] if by_chunk else table[h, :, i]
            own[0, 0], own[0, 1], own[1, 0], own[1, 1] = c, s, -s, c
    table = table.reshape(-1, 256) * (2.0 / (GRID * GRID))
    return halves(table if by_chunk else np.pad(table, ((0, 8), (0, 0))))


def x_twiddle():
    table = np.zeros((32, 128))
    c, s = turn(np.arange(9)[:, None] * np.arange(128)[None, :], GRID)
    table[0:9] = c
    table[16:25] = s
    return table.astype(np.float32)


def y_radix_table():
    c, s = turn(np.arange(KAP)[:, None] * np.arange(64)[None, :], 64)
    high, low = halves(np.concatenate([c, -s], axis=0))
    return np.concatenate([high, high, low], axis=1)


def y_radix_inverse_table():
    c, s = turn(np.arange(64)[:, None] * np.arange(KAP)[None, :], 64)
    high, low = halves(np.concatenate([c, -s], axis=1))
    return np.block([[high, high], [low, np.zeros_like(low)]])


def y_twiddle():
    c, s = turn(np.arange(KAP)[:, None] * np.arange(ROWS)[None, :], GRID)
    return np.stack([np.tile(c, (1, 4)), np.tile(s, (1, 4))]).astype(np.float32)


def lanes_of():
    c, s = turn(np.arange(ROWS)[:, None] * np.arange(JP)[None, :], ROWS)
    table = np.zeros((2, 4, ROWS, 128))
    for jb in range(4):
        re = slice(2 * JP * jb, 2 * JP * jb + JP)
        im = slice(2 * JP * jb + JP, 2 * JP * jb + 2 * JP)
        table[0, jb, :, re], table[1, jb, :, re] = c, s
        table[0, jb, :, im], table[1, jb, :, im] = -s, c
    return table.reshape(256, 128)


def y_lane_table():
    return np.concatenate(list(halves(lanes_of())), axis=1)


def y_lane_inverse_table():
    high, low = halves(2.0 * lanes_of().T)
    return np.concatenate([high, high, low], axis=0)


def y_projection_table():
    difference = np.arange(ROWS)[None, :] - np.arange(ROWS)[:, None]
    tables = []
    for count in (JP, JP - 1):
        c, s = turn(difference[:, :, None] * np.arange(count)[None, None, :], ROWS)
        c, s = np.kron(np.eye(4), 2 * c.sum(-1)), np.kron(np.eye(4), 2 * s.sum(-1))
        tables.append(np.block([[c, s], [-s, c]]))
    return halves(np.stack(tables))


def y_mean_table():
    return np.kron(np.eye(8), np.ones((ROWS, ROWS))).astype(ml_dtypes.bfloat16)


def lane_facts(packed):
    lane = np.arange(512 if packed else 128)
    facts = np.zeros((8, lane.size))
    facts[0] = 16 * (lane // (2 * JP))
    facts[1] = 64 * (lane % JP)
    return facts.astype(np.float32)


def split(value):
    high = value.astype(BF16)
    low = (value - high.astype(F32)).astype(BF16)
    return high, low


def dot(a, b, dims):
    return lax.dot_general(a, b, (dims, ((), ())), preferred_element_type=F32)


def matmul(left, right, dims):
    return dot(left[0], right[0], dims) + (dot(left[0], right[1], dims) + dot(left[1], right[0], dims))


def matmul_tall(table, right):
    out = dot(table[...], jnp.concatenate(right, axis=0), NN)
    size = table.shape[0] // 2
    return out[:size] + out[size:]


def matmul_wide(left, table):
    depth = left[0].shape[1]
    both = jnp.concatenate(left, axis=1)
    return dot(both, table[: 2 * depth], NN) + dot(left[0], table[2 * depth :], NN)


def matmul_beside(left, table):
    size = table.shape[1] // 2
    out = dot(left[0], table[...], NN)
    return out[:, :size] + (out[:, size:] + dot(left[1], table[:, :size], NN))


NN = ((1,), (0,))
NT = ((1,), (1,))
TN = ((0,), (0,))

C1 = math.cos(math.pi / 8)
C2 = math.cos(math.pi / 4)
C3 = math.cos(3 * math.pi / 8)


def real_analysis(x):
    s = [x[a] + x[a + 8] for a in range(8)]
    d = [x[a] - x[a + 8] for a in range(8)]
    e = [None] + [d[a] - d[8 - a] for a in range(1, 4)]
    f = [None] + [d[a] + d[8 - a] for a in range(1, 4)]
    e2, f2 = e[2] * C2, f[2] * C2
    plus, minus = d[0] + e2, d[0] - e2
    first, second = e[1] * C1 + e[3] * C3, e[1] * C3 - e[3] * C1
    third, fourth = f[1] * C3 + f[3] * C1, f[1] * C1 - f[3] * C3
    u, v = d[4] + f2, f2 - d[4]
    p = [s[a] + s[a + 4] for a in range(4)]
    q = [s[a] - s[a + 4] for a in range(4)]
    even, odd = p[0] + p[2], p[1] + p[3]
    hd, hs = (q[1] - q[3]) * C2, (q[1] + q[3]) * C2
    real = [
        even + odd,
        plus + first,
        q[0] + hd,
        minus + second,
        p[0] - p[2],
        minus - second,
        q[0] - hd,
        plus - first,
        even - odd,
    ]
    imag = [
        None,
        -(third + u),
        -(q[2] + hs),
        -(fourth + v),
        p[3] - p[1],
        v - fourth,
        q[2] - hs,
        u - third,
        None,
    ]
    return real, imag


def real_synthesis(real, imag):
    plus, first = real[1] + real[7], real[1] - real[7]
    minus, second = real[3] + real[5], real[3] - real[5]
    third, u = -(imag[1] + imag[7]), imag[7] - imag[1]
    fourth, v = -(imag[3] + imag[5]), imag[5] - imag[3]
    d = [None] * 8
    d[0], d[4] = plus + minus, u - v
    e = [None, first * C1 + second * C3, (plus - minus) * C2, first * C3 - second * C1]
    f = [None, third * C3 + fourth * C1, (u + v) * C2, third * C1 - fourth * C3]
    for a in range(1, 4):
        d[a], d[8 - a] = f[a] + e[a], f[a] - e[a]
    even, odd = real[0] + real[8], real[0] - real[8]
    p = [even + real[4], odd - imag[4], even - real[4], odd + imag[4]]
    hr, hi = (real[2] - real[6]) * C2, (imag[2] + imag[6]) * C2
    q = [real[2] + real[6], hr - hi, imag[6] - imag[2], -(hr + hi)]
    s = [p[a] + q[a] for a in range(4)] + [p[a] - q[a] for a in range(4)]
    return [s[a] + d[a] for a in range(8)] + [s[a] - d[a] for a in range(8)]


def regroup(blocks, wanted):
    block = lax.broadcasted_iota(jnp.int32, (1, 128), 1) // 32
    turned = [
        b if b is None or i == 0 else pltpu.roll(b, 32 * i, 1) for i, b in enumerate(blocks)
    ]
    results = []
    for p in wanted:
        total = None
        for i in range(4):
            part = jnp.zeros_like(turned[0]) if turned[i] is None else turned[i]
            total = part if total is None else jnp.where(block == (p + i) % 4, part, total)
        results.append(total if p == 0 else pltpu.roll(total, 128 - 32 * p, 1))
    return results


def turn_by(re, im, c, s):
    return re * c + im * s, im * c - re * s


def x_forward(real, imag, twiddle, table):
    pieces = []
    for k in range(9):
        if k == 0:
            pieces.append(jnp.concatenate([real[0], jnp.zeros_like(real[0])], axis=1))
            continue
        c, s = twiddle[k : k + 1], twiddle[16 + k : 17 + k]
        if k == 8:
            re, im = real[8] * c, -(real[8] * s)
        else:
            re, im = real[k] * c + imag[k] * s, imag[k] * c - real[k] * s
        pieces.append(jnp.concatenate([re, im], axis=1))
    shared = split(jnp.concatenate(pieces[1:8], axis=0))
    results = []
    for half, own in enumerate((pieces[0], pieces[8])):
        own = split(own)
        right = [jnp.concatenate([own[i], shared[i]], axis=0) for i in range(2)]
        out = dot(table[half], right[0], NT)
        results.append(out[:96] + (out[96:] + dot(table[half, :96], right[1], NT)))
    return results


def modes_of(source, twiddle, turned=False):
    real, imag = [], []
    for k in range(9):
        c, s = twiddle[k : k + 1], twiddle[16 + k : 17 + k]
        z = source(k)
        re, im = z[:, :128], z[:, 128:]
        if k == 0:
            real.append(im if turned else re)
            imag.append(None)
            continue
        real.append(im * c + re * s if turned else re * c - im * s)
        if k == 8:
            imag.append(None)
        else:
            imag.append(im * s - re * c if turned else re * s + im * c)
    return real, imag


def y_turned(in_ref, radix, twiddle):
    columns = [in_ref[pl.ds(jr, 64, stride=CHUNK), :] for jr in range(6)]
    high, low = split(jnp.concatenate(columns, axis=1))
    mixed = dot(radix[...], jnp.concatenate([high, low, high], axis=0), NN)
    results = []
    for jr in range(6):
        lanes = slice(128 * jr, 128 * jr + 128)
        re, im = turn_by(mixed[:KAP, lanes], mixed[KAP:, lanes], twiddle[0], twiddle[1])
        results.append(jnp.concatenate([re, im], axis=1))
    return results


def y_returned(pairs, radix, twiddle):
    c, s = twiddle[0], twiddle[1]
    real, imag = [], []
    for pair, turned in pairs:
        re, im = pair[:, :128], pair[:, 128:]
        real.append(im * c + re * s if turned else re * c - im * s)
        imag.append(im * s - re * c if turned else re * s + im * c)
    right = jnp.concatenate([jnp.concatenate(real, axis=1), jnp.concatenate(imag, axis=1)], axis=0)
    return matmul_tall(radix, split(right))


def pack(tiles):
    lane = lax.broadcasted_iota(jnp.int32, (1, 128), 1)
    packed = [None] * 4
    for jr, tile in enumerate(tiles):
        index, offset = divmod(PIECE * jr, 128)
        moved = pltpu.roll(tile, offset, 1) if offset else tile
        parts = [(index, moved)]
        if offset + PIECE > 128:
            parts = [(index, jnp.where(lane >= offset, moved, 0.0))]
            parts.append((index + 1, jnp.where(lane < offset, moved, 0.0)))
        for own, part in parts:
            if own < 4:
                packed[own] = part if packed[own] is None else packed[own] + part
    return packed


def unpack(packed):
    lane = lax.broadcasted_iota(jnp.int32, (1, 128), 1)
    tiles = []
    for jr in range(6):
        index, offset = divmod(PIECE * jr, 128)
        tile = packed[:, 128 * index : 128 * index + 128]
        if offset + PIECE > 128:
            later = packed[:, 128 * index + 128 : 128 * index + 256] if index < 3 else 0.0
            tile = jnp.where(lane >= offset, tile, later)
        tiles.append(pltpu.roll(tile, 128 - offset, 1) if offset else tile)
    return tiles


def y_waves(facts):
    kap = lax.broadcasted_iota(jnp.int32, (KAP, 1), 0).astype(F32)
    return kap + facts[1:2]


def x_waves(facts, owner):
    slot = owner // 8
    h = (owner % 8) // 2
    eight = jnp.where(slot == 0, 8 * (h // 2), 0)
    return facts[0:1] + (slot + eight + 16 * (21 * h - 84 * (h // 2))).astype(F32)


def half_of_zero(wave):
    return jnp.where(wave == 0.0, 0.5, 1.0)


def store_x(out_ref, results, group):
    for half in range(2):
        lanes = slice(128 * group, 128 * group + 128)
        blocks = [results[half][24 * jb : 24 * jb + 24, lanes] for jb in range(4)]
        for slot, block in enumerate(regroup(blocks, range(4))):
            start = (8 * (4 * group + slot) + 4 * half) * CHUNK
            out_ref[start : start + 4 * CHUNK, :] = block


def state_kernel(
    state_hbm, twiddle_hbm, table_hbm, out_hbm, state_ref, twiddle_ref, table_ref, out_ref, sems
):
    pairs = ((state_hbm, state_ref), (twiddle_hbm, twiddle_ref), (table_hbm, table_ref))
    copies = [pltpu.make_async_copy(a, b, sems.at[i]) for i, (a, b) in enumerate(pairs)]
    for copy in copies:
        copy.start()
    copies[0].wait()
    x = [state_ref[0, :, 128 * a : 128 * a + 128] for a in range(16)]
    real, imag = real_analysis(x)
    copies[1].wait()
    copies[2].wait()
    results = x_forward(real, imag, twiddle_ref[...], table_ref)
    sends = []
    for group in range(2):
        store_x(out_ref, results, group)
        rows = pl.ds(32 * group * CHUNK, 32 * CHUNK)
        sends.append(pltpu.make_async_copy(out_ref.at[rows], out_hbm.at[rows], sems.at[3 + group]))
        sends[-1].start()
    for send in sends:
        send.wait()


def weights_kernel(to_ref, from_ref, deform_ref, facts_ref, out_ref):
    facts = facts_ref[...]
    wave_x = x_waves(facts, lax.axis_index("row"))
    wave_y = y_waves(facts)
    square = (wave_x * wave_x + wave_y * wave_y)[:, :USED]
    layer = lax.axis_index("layer")
    modes = [from_ref[layer, m] * (-1.0 / (square + deform_ref[m])) for m in range(8)]
    for n in range(8):
        total = None
        for m in range(8):
            term = modes[m] * to_ref[m, n]
            total = term if total is None else total + term
        out_ref[n] = total


def spectrum_kernel(in_ref, radix_ref, turn_ref, lanes_ref, facts_ref, spec_ref, used_ref):
    turned = split(jnp.concatenate(y_turned(in_ref, radix_ref, turn_ref), axis=0))
    spectrum = matmul_beside(turned, lanes_ref)
    kept = y_waves(facts_ref[...]) < KCUT
    tiles = [jnp.where(kept, spectrum[KAP * jr : KAP * jr + KAP], 0.0) for jr in range(6)]
    spec_ref[...] = jnp.concatenate(tiles, axis=0)
    for index, tile in enumerate(pack(tiles)):
        used = min(USED - 128 * index, 128)
        used_ref[:, 128 * index : 128 * index + used] = tile[:, :used]


def stream_kernel(
    weights_ref, all_ref, spec_ref, unradix_ref, turn_ref, unlanes_ref, facts_ref, out_ref, stream_ref
):
    stream = None
    for n in range(8):
        term = weights_ref[n] * all_ref[n]
        stream = term if stream is None else stream + term
    stream_ref[:, 384:] = jnp.zeros((KAP, 128), F32)
    stream_ref[:, :USED] = stream
    facts = facts_ref[...]
    wave_y = y_waves(facts)
    once = half_of_zero(wave_y)
    pieces = []
    for jr, tile in enumerate(unpack(stream_ref[...])):
        wave_x = x_waves(facts, lax.axis_index("row")) + 64 * jr
        along_y, along_x = wave_y * half_of_zero(wave_x), wave_x * once
        own = spec_ref[KAP * jr : KAP * jr + KAP, :]
        pieces += [along_y * tile, -along_y * own, along_x * tile, along_x * own]
    out = matmul_wide(split(jnp.concatenate(pieces, axis=0)), unlanes_ref)
    pairs = [(out[KAP * i : KAP * i + KAP], i % 4 < 2) for i in range(24)]
    out = y_returned(pairs, unradix_ref, turn_ref)
    for jr in range(6):
        blocks = [out[:, 128 * (4 * jr + f) : 128 * (4 * jr + f) + 128] for f in range(4)]
        count = min(MINE - 4 * jr, 4)
        for jb, block in enumerate(regroup(blocks, range(count))):
            out_ref[pl.ds(4 * jr + jb, 64, stride=MINE), :] = block


def jacobian_kernel(in_ref, twiddle_ref, untable_ref, table_ref, out_ref, first_ref, whole_ref, jac):
    depth = 8 * MINE
    row = lax.broadcasted_iota(jnp.int32, (depth, 1), 0)
    spare = jnp.zeros((8, 4 * 128), F32)
    table = [untable_ref[0], untable_ref[1]]
    for part in range(2):
        slots = [
            in_ref[depth * slot : depth * slot + depth, :] for slot in range(4 * part, 4 * part + 4)
        ]
        side = jnp.concatenate([jnp.concatenate(slots, axis=1), spare], axis=0)
        whole_ref[512 * part : 512 * part + 512, :] = matmul(split(side), table, TN)
        if part == 0:
            own = jnp.concatenate([jnp.where(row < depth // 2, slots[0], 0.0), spare[:, :128]], axis=0)
            first_ref[...] = matmul(split(own), table, TN)
    twiddle = twiddle_ref[...]
    for block in range(4):
        rows = slice(8 * block, 8 * block + 8)

        def physical(field):
            def source(k):
                start = 32 * field + rows.start
                if k == 0:
                    return first_ref[start : start + 8, :]
                start += 128 * (k % 8)
                z = whole_ref[start : start + 8, :]
                return z if k < 8 else z - source(0)

            return real_synthesis(*modes_of(source, twiddle, field > 1))

        east, slope_x = physical(0), physical(3)
        product = [a * b for a, b in zip(east, slope_x)]
        north, slope_y = physical(2), physical(1)
        product = [p + a * b for p, a, b in zip(product, north, slope_y)]
        real, imag = real_analysis(product)
        for k in range(9):
            jac[0, k, rows, :] = real[k]
            if imag[k] is not None:
                jac[1, k, rows, :] = imag[k]
    real = [jac[0, k] for k in range(9)]
    imag = [None] + [jac[1, k] for k in range(1, 8)] + [None]
    results = x_forward(real, imag, twiddle, table_ref)
    for group in range(2):
        store_x(out_ref, results, group)


def projection_kernel(
    in_ref, spec_ref, radix_ref, unradix_ref, turn_ref, project_ref, mean_ref, unlanes_ref, facts_ref, out_ref
):
    facts = facts_ref[...]
    wave_y = y_waves(facts)
    once = half_of_zero(wave_y)
    damped = []
    for jr in range(6):
        wave_x = x_waves(facts, lax.axis_index("row")) + 64 * jr
        ratio = (wave_x * wave_x + wave_y * wave_y) * (1.0 / (KCUT * KCUT))
        ratio = ratio * ratio
        damped.append(((HYPER_RATE * (ratio * ratio)) * once) * spec_ref[KAP * jr : KAP * jr + KAP, :])
    damping = matmul_wide(split(jnp.concatenate(damped, axis=0)), unlanes_ref)
    left = [split(pair) for pair in y_turned(in_ref, radix_ref, turn_ref)]
    sides = []
    for side in range(2):
        rows = slice(32 * side, 32 * side + 32)
        stacked = [jnp.concatenate([pair[i][rows] for pair in left], axis=0) for i in range(2)]
        sides.append(matmul(stacked, [project_ref[i, side] for i in range(2)], NN))
    heads = [jnp.concatenate([pair[i][:16] for pair in left], axis=0) for i in range(2)]
    mean = dot(heads[0], mean_ref[...], NN) + dot(heads[1], mean_ref[...], NN)
    first = lax.broadcasted_iota(jnp.int32, (16, 1), 0) == 0
    lane = lax.broadcasted_iota(jnp.int32, (1, 256), 1)
    zero_wave = (lax.axis_index("row") < 2) & (lane % 128 < 32)
    pairs = []
    for jr in range(6):
        low, high = [side[32 * jr : 32 * jr + 32] for side in sides]
        own = jnp.where(first, mean[16 * jr : 16 * jr + 16], 0.0)
        flux = jnp.concatenate([low[:16] - own, low[16:], high], axis=0)
        total = flux - damping[KAP * jr : KAP * jr + KAP]
        pairs.append((total * jnp.where(zero_wave, 0.5, 1.0) if jr == 0 else total, False))
    out = y_returned(pairs, unradix_ref, turn_ref)
    for jr in range(6):
        out_ref[pl.ds(jr, 64, stride=CHUNK), :] = out[:, 128 * jr : 128 * jr + 128]


def state_update_kernel(
    in_ref,
    state_ref,
    start_ref,
    twiddle_ref,
    untable_ref,
    tendency_hbm,
    new_hbm,
    first,
    whole,
    tendency_ref,
    new_ref,
    sems,
):
    depth = 8 * CHUNK
    table = [untable_ref[0], untable_ref[1]]
    for group in range(2):
        blocks = [in_ref[depth * slot : depth * slot + depth, :] for slot in range(4 * group, 4 * group + 4)]
        side = jnp.concatenate(regroup(blocks, range(4)), axis=0)
        whole[128 * group : 128 * group + 128, :] = matmul(split(side), table, TN)
        if group == 0:
            row = lax.broadcasted_iota(jnp.int32, (4 * depth, 1), 0)
            own = jnp.where(row % depth < depth // 2, side, 0.0)
            first[...] = matmul(split(own), table, TN)
    twiddle = twiddle_ref[...]
    sends = []
    for block in range(4):
        rows = slice(8 * block, 8 * block + 8)

        def source(k):
            if k == 0:
                return first[rows, :]
            start = 32 * (k % 8) + rows.start
            z = whole[start : start + 8, :]
            return z if k < 8 else z - source(0)

        tendency = real_synthesis(*modes_of(source, twiddle))
        for a in range(16):
            columns = slice(128 * a, 128 * a + 128)
            tendency_ref[0, rows, columns] = tendency[a]
            new_ref[0, rows, columns] = 0.75 * start_ref[0, rows, columns] + 0.25 * (
                state_ref[0, rows, columns] + STEP_SIZE * tendency[a]
            )
        for i, (near, far) in enumerate(((tendency_ref, tendency_hbm), (new_ref, new_hbm))):
            own = (slice(None), pl.ds(8 * block, 8))
            sends.append(pltpu.make_async_copy(near.at[own], far.at[own], sems.at[2 * block + i]))
            sends[-1].start()
    for send in sends:
        send.wait()


VMEM = pl.BlockSpec(memory_space=pltpu.VMEM)
SMEM = pl.BlockSpec(memory_space=pltpu.SMEM)
ANY = pl.BlockSpec(memory_space=pl.ANY)
MIB = 1024 * 1024


def call(kernel, outs, operands, scalars=0, scratch=(), far_in=False, far_out=False, copies=0, cost=None):
    scratch_shapes = [pltpu.VMEM(operand.shape, operand.dtype) for operand in operands] if far_in else []
    scratch_shapes += [pltpu.VMEM(shape, F32) for shape in scratch]
    scratch_shapes += [pltpu.VMEM(shape, F32) for shape in outs] if far_out else []
    scratch_shapes += [pltpu.SemaphoreType.DMA((copies,))] if copies else []
    near = [SMEM] * scalars + [VMEM] * (len(operands) - scalars)
    return pl.pallas_call(
        kernel,
        out_shape=[jax.ShapeDtypeStruct(shape, F32) for shape in outs],
        in_specs=[ANY] * len(operands) if far_in else near,
        out_specs=[ANY if far_out else VMEM] * len(outs),
        scratch_shapes=scratch_shapes,
        compiler_params=pltpu.CompilerParams(vmem_limit_bytes=(60 if far_in else 32) * MIB),
        cost_estimate=cost,
    )(*operands)


def exchange(chunks, devices):
    length = chunks.shape[0]
    sent = chunks.reshape(devices, 1, length * 128 // devices)
    return lax.all_to_all(sent, "row", split_axis=0, concat_axis=0, tiled=True).reshape(length, 128)


def per_device(state, start_state, to_modes, from_modes, deform):
    devices = lax.axis_size("row")
    turn_x = jnp.asarray(x_twiddle())
    forward_x = jnp.asarray(x_forward_table())
    inverse_x = jnp.asarray(x_inverse_table(False))
    inverse_chunk = jnp.asarray(x_inverse_table(True))
    radix = jnp.asarray(y_radix_table())
    unradix = jnp.asarray(y_radix_inverse_table())
    turn_y = jnp.asarray(y_twiddle())
    lanes = jnp.asarray(y_lane_table())
    unlanes = jnp.asarray(y_lane_inverse_table())
    project = jnp.asarray(y_projection_table())
    mean = jnp.asarray(y_mean_table())
    facts = jnp.asarray(lane_facts(False))
    packed_facts = jnp.asarray(lane_facts(True))

    one, four = (64 * CHUNK, 128), (64 * MINE, 128)
    (columns,) = call(state_kernel, [one], [state, turn_x, forward_x], far_in=True, far_out=True, copies=5)
    columns = exchange(columns, devices)
    spectrum, used = call(
        spectrum_kernel, [(6 * KAP, 128), (KAP, USED)], [columns, radix, turn_y, lanes, facts]
    )
    (weights,) = call(
        weights_kernel,
        [(8, KAP, USED)],
        [to_modes, from_modes, deform, packed_facts],
        scalars=3,
        cost=pl.CostEstimate(flops=8_000_000, bytes_accessed=2_000_000, transcendentals=0),
    )
    gathered = lax.all_gather(used, "layer", axis=0, tiled=False)
    (fields,) = call(
        stream_kernel,
        [four],
        [weights, gathered, spectrum, unradix, turn_y, unlanes, facts],
        scratch=[(KAP, 512)],
    )
    fields = exchange(fields, devices)
    (flux,) = call(
        jacobian_kernel,
        [one],
        [fields, turn_x, inverse_x, forward_x],
        scratch=[(128, 256), (1024, 256), (2, 9, ROWS, 128)],
    )
    flux = exchange(flux, devices)
    (total,) = call(
        projection_kernel,
        [one],
        [flux, spectrum, radix, unradix, turn_y, project, mean, unlanes, facts],
    )
    total = exchange(total, devices)
    return tuple(
        call(
            state_update_kernel,
            [(1, ROWS, GRID)] * 2,
            [total, state, start_state, turn_x, inverse_chunk],
            scratch=[(128, 256), (256, 256)],
            far_out=True,
            copies=8,
        )
    )


def solution(mesh):
    in_specs = (P("layer", "row", None), P("layer", "row", None), P(), P(), P())
    out_specs = (P("layer", "row", None), P("layer", "row", None))
    return jax.shard_map(
        per_device, mesh=mesh, in_specs=in_specs, out_specs=out_specs, check_vma=False
    )
```

```python
import functools
import math

import jax
import jax.numpy as jnp
import ml_dtypes
import numpy as np
from jax import lax
from jax.experimental import pallas as pl
from jax.experimental.pallas import tpu as pltpu
from jax.sharding import PartitionSpec as P

GRID = 2048
KCUT = 672
ROWS = 32
MINE = 21
CHUNK = 6
KAP = 64
JP = 11
PIECE = 4 * 2 * JP
USED = 8 * MINE * 2 * JP
TILES = -(-USED // 128)
HYPER_RATE = 0.2
STEP_SIZE = 0.5
BF16 = jnp.bfloat16
F32 = jnp.float32


def halves(table):
    high = table.astype(ml_dtypes.bfloat16)
    low = (table - high.astype(np.float64)).astype(ml_dtypes.bfloat16)
    return np.stack([high, low])


def turn(numerator, denominator):
    angle = 2.0 * math.pi * (np.mod(numerator, denominator) / denominator)
    return np.cos(angle), np.sin(angle)


def column_j(h, i):
    return 21 * h + i - 84 * (h // 2)


def x_forward_table():
    b = np.arange(128)
    table = np.zeros((2, 4, 2, 2, 6, 2, 128))
    for h in range(4):
        for i in range(MINE):
            c, s = turn(column_j(h, i) * b, 128)
            own = table[h // 2, i % 4, h % 2, :, i // 4]
            own[0, 0], own[0, 1], own[1, 0], own[1, 1] = c, s, -s, c
    return np.concatenate(list(halves(table.reshape(2, 96, 256))), axis=1)


def x_inverse_table(by_chunk):
    b = np.arange(128)
    table = np.zeros((4, 4, 2, 6, 2, 128)) if by_chunk else np.zeros((4, 2, MINE, 2, 128))
    for h in range(4):
        for i in range(MINE):
            c, s = turn(column_j(h, i) * b, 128)
            own = table[i % 4, h, :, i // 4] if by_chunk else table[h, :, i]
            own[0, 0], own[0, 1], own[1, 0], own[1, 1] = c, s, -s, c
    table = table.reshape(-1, 256) * (2.0 / (GRID * GRID))
    return halves(table if by_chunk else np.pad(table, ((0, 8), (0, 0))))


def x_twiddle():
    table = np.zeros((32, 128))
    c, s = turn(np.arange(9)[:, None] * np.arange(128)[None, :], GRID)
    table[0:9] = c
    table[16:25] = s
    return table.astype(np.float32)


def y_radix_table():
    c, s = turn(np.arange(KAP)[:, None] * np.arange(64)[None, :], 64)
    high, low = halves(np.concatenate([c, -s], axis=0))
    return np.concatenate([high, high, low], axis=1)


def y_radix_inverse_table():
    c, s = turn(np.arange(64)[:, None] * np.arange(KAP)[None, :], 64)
    high, low = halves(np.concatenate([c, -s], axis=1))
    return np.block([[high, high], [low, np.zeros_like(low)]])


def y_twiddle():
    c, s = turn(np.arange(KAP)[:, None] * np.arange(ROWS)[None, :], GRID)
    return np.stack([np.tile(c, (1, 4)), np.tile(s, (1, 4))]).astype(np.float32)


def lanes_of():
    c, s = turn(np.arange(ROWS)[:, None] * np.arange(JP)[None, :], ROWS)
    table = np.zeros((2, 4, ROWS, 128))
    for jb in range(4):
        re = slice(2 * JP * jb, 2 * JP * jb + JP)
        im = slice(2 * JP * jb + JP, 2 * JP * jb + 2 * JP)
        table[0, jb, :, re], table[1, jb, :, re] = c, s
        table[0, jb, :, im], table[1, jb, :, im] = -s, c
    return table.reshape(256, 128)


def y_lane_table():
    return np.concatenate(list(halves(lanes_of())), axis=1)


def y_lane_inverse_table():
    high, low = halves(2.0 * lanes_of().T)
    return np.concatenate([high, high, low], axis=0)


def y_projection_table():
    difference = np.arange(ROWS)[None, :] - np.arange(ROWS)[:, None]
    tables = []
    for count in (JP, JP - 1):
        c, s = turn(difference[:, :, None] * np.arange(count)[None, None, :], ROWS)
        c, s = np.kron(np.eye(4), 2 * c.sum(-1)), np.kron(np.eye(4), 2 * s.sum(-1))
        tables.append(np.block([[c, s], [-s, c]]))
    return halves(np.stack(tables))


def y_mean_table():
    return np.kron(np.eye(8), np.ones((ROWS, ROWS))).astype(ml_dtypes.bfloat16)


def lane_facts():
    lane = np.arange(128)
    facts = np.zeros((8, 128))
    facts[0] = 16 * (lane // (2 * JP))
    facts[1] = 64 * (lane % JP)
    return facts.astype(np.float32)


def packed_facts():
    lane = np.arange(USED)
    own = lane % (USED // 8)
    facts = np.zeros((8, USED))
    facts[0] = 16 * (own // (2 * JP))
    facts[1] = 64 * (own % JP) + 8 * (lane // (USED // 8))
    return facts.astype(np.float32)


def split(value):
    high = value.astype(BF16)
    low = (value - high.astype(F32)).astype(BF16)
    return high, low


def dot(a, b, dims):
    return lax.dot_general(a, b, (dims, ((), ())), preferred_element_type=F32)


def matmul(left, right, dims):
    return dot(left[0], right[0], dims) + (dot(left[0], right[1], dims) + dot(left[1], right[0], dims))


def matmul_tall(table, right):
    out = dot(table[...], jnp.concatenate(right, axis=0), NN)
    size = table.shape[0] // 2
    return out[:size] + out[size:]


def matmul_wide(left, table):
    depth = left[0].shape[1]
    both = jnp.concatenate(left, axis=1)
    return dot(both, table[: 2 * depth], NN) + dot(left[0], table[2 * depth :], NN)


def matmul_beside(left, table):
    size = table.shape[1] // 2
    out = dot(left[0], table[...], NN)
    return out[:, :size] + (out[:, size:] + dot(left[1], table[:, :size], NN))


NN = ((1,), (0,))
NT = ((1,), (1,))
TN = ((0,), (0,))

C1 = math.cos(math.pi / 8)
C2 = math.cos(math.pi / 4)
C3 = math.cos(3 * math.pi / 8)


def real_analysis(x):
    s = [x[a] + x[a + 8] for a in range(8)]
    d = [x[a] - x[a + 8] for a in range(8)]
    e = [None] + [d[a] - d[8 - a] for a in range(1, 4)]
    f = [None] + [d[a] + d[8 - a] for a in range(1, 4)]
    e2, f2 = e[2] * C2, f[2] * C2
    plus, minus = d[0] + e2, d[0] - e2
    first, second = e[1] * C1 + e[3] * C3, e[1] * C3 - e[3] * C1
    third, fourth = f[1] * C3 + f[3] * C1, f[1] * C1 - f[3] * C3
    u, v = d[4] + f2, f2 - d[4]
    p = [s[a] + s[a + 4] for a in range(4)]
    q = [s[a] - s[a + 4] for a in range(4)]
    even, odd = p[0] + p[2], p[1] + p[3]
    hd, hs = (q[1] - q[3]) * C2, (q[1] + q[3]) * C2
    real = [
        even + odd,
        plus + first,
        q[0] + hd,
        minus + second,
        p[0] - p[2],
        minus - second,
        q[0] - hd,
        plus - first,
        even - odd,
    ]
    imag = [
        None,
        -(third + u),
        -(q[2] + hs),
        -(fourth + v),
        p[3] - p[1],
        v - fourth,
        q[2] - hs,
        u - third,
        None,
    ]
    return real, imag


def real_synthesis(real, imag):
    plus, first = real[1] + real[7], real[1] - real[7]
    minus, second = real[3] + real[5], real[3] - real[5]
    third, u = -(imag[1] + imag[7]), imag[7] - imag[1]
    fourth, v = -(imag[3] + imag[5]), imag[5] - imag[3]
    d = [None] * 8
    d[0], d[4] = plus + minus, u - v
    e = [None, first * C1 + second * C3, (plus - minus) * C2, first * C3 - second * C1]
    f = [None, third * C3 + fourth * C1, (u + v) * C2, third * C1 - fourth * C3]
    for a in range(1, 4):
        d[a], d[8 - a] = f[a] + e[a], f[a] - e[a]
    even, odd = real[0] + real[8], real[0] - real[8]
    p = [even + real[4], odd - imag[4], even - real[4], odd + imag[4]]
    hr, hi = (real[2] - real[6]) * C2, (imag[2] + imag[6]) * C2
    q = [real[2] + real[6], hr - hi, imag[6] - imag[2], -(hr + hi)]
    s = [p[a] + q[a] for a in range(4)] + [p[a] - q[a] for a in range(4)]
    return [s[a] + d[a] for a in range(8)] + [s[a] - d[a] for a in range(8)]


def regroup(blocks, wanted):
    block = lax.broadcasted_iota(jnp.int32, (1, 128), 1) // 32
    turned = [
        b if b is None or i == 0 else pltpu.roll(b, 32 * i, 1) for i, b in enumerate(blocks)
    ]
    results = []
    for p in wanted:
        total = None
        for i in range(4):
            part = jnp.zeros_like(turned[0]) if turned[i] is None else turned[i]
            total = part if total is None else jnp.where(block == (p + i) % 4, part, total)
        results.append(total if p == 0 else pltpu.roll(total, 128 - 32 * p, 1))
    return results


def turn_by(re, im, c, s):
    return re * c + im * s, im * c - re * s


def x_forward(real, imag, twiddle, table):
    pieces = []
    for k in range(9):
        if k == 0:
            pieces.append(jnp.concatenate([real[0], jnp.zeros_like(real[0])], axis=1))
            continue
        c, s = twiddle[k : k + 1], twiddle[16 + k : 17 + k]
        if k == 8:
            re, im = real[8] * c, -(real[8] * s)
        else:
            re, im = real[k] * c + imag[k] * s, imag[k] * c - real[k] * s
        pieces.append(jnp.concatenate([re, im], axis=1))
    shared = split(jnp.concatenate(pieces[1:8], axis=0))
    results = []
    for half, own in enumerate((pieces[0], pieces[8])):
        own = split(own)
        right = [jnp.concatenate([own[i], shared[i]], axis=0) for i in range(2)]
        out = dot(table[half], right[0], NT)
        results.append(out[:96] + (out[96:] + dot(table[half, :96], right[1], NT)))
    return results


def modes_of(source, twiddle, turned=False):
    real, imag = [], []
    for k in range(9):
        c, s = twiddle[k : k + 1], twiddle[16 + k : 17 + k]
        z = source(k)
        re, im = z[:, :128], z[:, 128:]
        if k == 0:
            real.append(im if turned else re)
            imag.append(None)
            continue
        real.append(im * c + re * s if turned else re * c - im * s)
        if k == 8:
            imag.append(None)
        else:
            imag.append(im * s - re * c if turned else re * s + im * c)
    return real, imag


def y_turned(in_ref, radix, twiddle):
    columns = [in_ref[pl.ds(jr, 64, stride=CHUNK), :] for jr in range(6)]
    high, low = split(jnp.concatenate(columns, axis=1))
    mixed = dot(radix[...], jnp.concatenate([high, low, high], axis=0), NN)
    results = []
    for jr in range(6):
        lanes = slice(128 * jr, 128 * jr + 128)
        re, im = turn_by(mixed[:KAP, lanes], mixed[KAP:, lanes], twiddle[0], twiddle[1])
        results.append(jnp.concatenate([re, im], axis=1))
    return results


def y_returned(pairs, radix, twiddle):
    c, s = twiddle[0], twiddle[1]
    real, imag = [], []
    for pair, turned in pairs:
        re, im = pair[:, :128], pair[:, 128:]
        real.append(im * c + re * s if turned else re * c - im * s)
        imag.append(im * s - re * c if turned else re * s + im * c)
    right = jnp.concatenate([jnp.concatenate(real, axis=1), jnp.concatenate(imag, axis=1)], axis=0)
    return matmul_tall(radix, split(right))


def pieces_of():
    for rows in range(8):
        for jr in range(6):
            index, offset = divmod(rows * (USED // 8) + PIECE * jr, 128)
            yield rows, jr, index, offset, PIECE if jr < 5 else 2 * JP


def pack(tiles):
    lane = lax.broadcasted_iota(jnp.int32, (1, 128), 1)
    packed = [None] * TILES
    for rows, jr, index, offset, used in pieces_of():
        moved = tiles[jr][8 * rows : 8 * rows + 8]
        moved = pltpu.roll(moved, offset, 1) if offset else moved
        parts = [(index, moved)]
        if offset + used > 128:
            parts = [(index, jnp.where(lane >= offset, moved, 0.0))]
            parts.append((index + 1, jnp.where(lane < offset, moved, 0.0)))
        for own, part in parts:
            packed[own] = part if packed[own] is None else packed[own] + part
    return packed


def unpack(packed):
    lane = lax.broadcasted_iota(jnp.int32, (1, 128), 1)
    tiles = [[] for _ in range(6)]
    for rows, jr, index, offset, used in pieces_of():
        tile = packed[:, 128 * index : 128 * index + 128]
        if offset + used > 128:
            tile = jnp.where(lane >= offset, tile, packed[:, 128 * index + 128 : 128 * index + 256])
        tiles[jr].append(pltpu.roll(tile, 128 - offset, 1) if offset else tile)
    return [jnp.concatenate(tile, axis=0) for tile in tiles]


def y_waves(facts, count=KAP):
    row = lax.broadcasted_iota(jnp.int32, (count, 1), 0).astype(F32)
    return row + facts[1:2]


def x_waves(facts, owner):
    slot = owner // 8
    h = (owner % 8) // 2
    eight = jnp.where(slot == 0, 8 * (h // 2), 0)
    return facts[0:1] + (slot + eight + 16 * (21 * h - 84 * (h // 2))).astype(F32)


def half_of_zero(wave):
    return jnp.where(wave == 0.0, 0.5, 1.0)


def store_x(out_ref, results, group):
    for half in range(2):
        lanes = slice(128 * group, 128 * group + 128)
        blocks = [results[half][24 * jb : 24 * jb + 24, lanes] for jb in range(4)]
        for slot, block in enumerate(regroup(blocks, range(4))):
            start = (8 * (4 * group + slot) + 4 * half) * CHUNK
            out_ref[start : start + 4 * CHUNK, :] = block


def state_kernel(
    state_hbm, twiddle_hbm, table_hbm, out_hbm, state_ref, twiddle_ref, table_ref, out_ref, sems
):
    pairs = ((state_hbm, state_ref), (twiddle_hbm, twiddle_ref), (table_hbm, table_ref))
    copies = [pltpu.make_async_copy(a, b, sems.at[i]) for i, (a, b) in enumerate(pairs)]
    for copy in copies:
        copy.start()
    copies[0].wait()
    x = [state_ref[0, :, 128 * a : 128 * a + 128] for a in range(16)]
    real, imag = real_analysis(x)
    copies[1].wait()
    copies[2].wait()
    results = x_forward(real, imag, twiddle_ref[...], table_ref)
    sends = []
    for group in range(2):
        store_x(out_ref, results, group)
        rows = pl.ds(32 * group * CHUNK, 32 * CHUNK)
        sends.append(pltpu.make_async_copy(out_ref.at[rows], out_hbm.at[rows], sems.at[3 + group]))
        sends[-1].start()
    for send in sends:
        send.wait()


def weights_kernel(to_ref, from_ref, deform_ref, facts_ref, out_ref):
    facts = facts_ref[...]
    wave_x = x_waves(facts, lax.axis_index("row"))
    wave_y = y_waves(facts, 8)
    square = wave_x * wave_x + wave_y * wave_y
    layer = lax.axis_index("layer")
    modes = [from_ref[layer, m] * (-1.0 / (square + deform_ref[m])) for m in range(8)]
    for n in range(8):
        total = None
        for m in range(8):
            term = modes[m] * to_ref[m, n]
            total = term if total is None else total + term
        out_ref[n] = total


def spectrum_kernel(in_ref, radix_ref, turn_ref, lanes_ref, facts_ref, spec_ref, used_ref):
    turned = split(jnp.concatenate(y_turned(in_ref, radix_ref, turn_ref), axis=0))
    spectrum = matmul_beside(turned, lanes_ref)
    kept = y_waves(facts_ref[...]) < KCUT
    tiles = [jnp.where(kept, spectrum[KAP * jr : KAP * jr + KAP], 0.0) for jr in range(6)]
    spec_ref[...] = jnp.concatenate(tiles, axis=0)
    for index, tile in enumerate(pack(tiles)):
        lanes = slice(128 * index, min(USED, 128 * index + 128))
        used_ref[:, lanes] = tile[:, : lanes.stop - lanes.start]


def stream_kernel(
    weights_ref, all_ref, spec_ref, unradix_ref, turn_ref, unlanes_ref, facts_ref, out_ref, stream_ref
):
    stream = None
    for n in range(8):
        term = weights_ref[n] * all_ref[n]
        stream = term if stream is None else stream + term
    stream_ref[:, 128 * TILES - 128 :] = jnp.zeros((8, 128), F32)
    stream_ref[:, :USED] = stream
    facts = facts_ref[...]
    wave_y = y_waves(facts)
    once = half_of_zero(wave_y)
    pieces = []
    for jr, tile in enumerate(unpack(stream_ref[...])):
        wave_x = x_waves(facts, lax.axis_index("row")) + 64 * jr
        along_y, along_x = wave_y * half_of_zero(wave_x), wave_x * once
        own = spec_ref[KAP * jr : KAP * jr + KAP, :]
        pieces += [along_y * tile, -along_y * own, along_x * tile, along_x * own]
    out = matmul_wide(split(jnp.concatenate(pieces, axis=0)), unlanes_ref)
    pairs = [(out[KAP * i : KAP * i + KAP], i % 4 < 2) for i in range(24)]
    out = y_returned(pairs, unradix_ref, turn_ref)
    for jr in range(6):
        blocks = [out[:, 128 * (4 * jr + f) : 128 * (4 * jr + f) + 128] for f in range(4)]
        count = min(MINE - 4 * jr, 4)
        for jb, block in enumerate(regroup(blocks, range(count))):
            out_ref[pl.ds(4 * jr + jb, 64, stride=MINE), :] = block


def jacobian_kernel(in_ref, twiddle_ref, untable_ref, table_ref, out_ref, first_ref, whole_ref, jac):
    depth = 8 * MINE
    row = lax.broadcasted_iota(jnp.int32, (depth, 1), 0)
    spare = jnp.zeros((8, 4 * 128), F32)
    table = [untable_ref[0], untable_ref[1]]
    for part in range(2):
        slots = [
            in_ref[depth * slot : depth * slot + depth, :] for slot in range(4 * part, 4 * part + 4)
        ]
        side = jnp.concatenate([jnp.concatenate(slots, axis=1), spare], axis=0)
        whole_ref[512 * part : 512 * part + 512, :] = matmul(split(side), table, TN)
        if part == 0:
            own = jnp.concatenate([jnp.where(row < depth // 2, slots[0], 0.0), spare[:, :128]], axis=0)
            first_ref[...] = matmul(split(own), table, TN)
    twiddle = twiddle_ref[...]
    for block in range(4):
        rows = slice(8 * block, 8 * block + 8)

        def physical(field):
            def source(k):
                start = 32 * field + rows.start
                if k == 0:
                    return first_ref[start : start + 8, :]
                start += 128 * (k % 8)
                z = whole_ref[start : start + 8, :]
                return z if k < 8 else z - source(0)

            return real_synthesis(*modes_of(source, twiddle, field > 1))

        east, slope_x = physical(0), physical(3)
        product = [a * b for a, b in zip(east, slope_x)]
        north, slope_y = physical(2), physical(1)
        product = [p + a * b for p, a, b in zip(product, north, slope_y)]
        real, imag = real_analysis(product)
        for k in range(9):
            jac[0, k, rows, :] = real[k]
            if imag[k] is not None:
                jac[1, k, rows, :] = imag[k]
    real = [jac[0, k] for k in range(9)]
    imag = [None] + [jac[1, k] for k in range(1, 8)] + [None]
    results = x_forward(real, imag, twiddle, table_ref)
    for group in range(2):
        store_x(out_ref, results, group)


def projection_kernel(
    in_ref, spec_ref, radix_ref, unradix_ref, turn_ref, project_ref, mean_ref, unlanes_ref, facts_ref, out_ref
):
    facts = facts_ref[...]
    wave_y = y_waves(facts)
    once = half_of_zero(wave_y)
    damped = []
    for jr in range(6):
        wave_x = x_waves(facts, lax.axis_index("row")) + 64 * jr
        ratio = (wave_x * wave_x + wave_y * wave_y) * (1.0 / (KCUT * KCUT))
        ratio = ratio * ratio
        damped.append(((HYPER_RATE * (ratio * ratio)) * once) * spec_ref[KAP * jr : KAP * jr + KAP, :])
    damping = matmul_wide(split(jnp.concatenate(damped, axis=0)), unlanes_ref)
    left = [split(pair) for pair in y_turned(in_ref, radix_ref, turn_ref)]
    sides = []
    for side in range(2):
        rows = slice(32 * side, 32 * side + 32)
        stacked = [jnp.concatenate([pair[i][rows] for pair in left], axis=0) for i in range(2)]
        sides.append(matmul(stacked, [project_ref[i, side] for i in range(2)], NN))
    heads = [jnp.concatenate([pair[i][:16] for pair in left], axis=0) for i in range(2)]
    mean = dot(heads[0], mean_ref[...], NN) + dot(heads[1], mean_ref[...], NN)
    first = lax.broadcasted_iota(jnp.int32, (16, 1), 0) == 0
    lane = lax.broadcasted_iota(jnp.int32, (1, 256), 1)
    zero_wave = (lax.axis_index("row") < 2) & (lane % 128 < 32)
    pairs = []
    for jr in range(6):
        low, high = [side[32 * jr : 32 * jr + 32] for side in sides]
        own = jnp.where(first, mean[16 * jr : 16 * jr + 16], 0.0)
        flux = jnp.concatenate([low[:16] - own, low[16:], high], axis=0)
        total = flux - damping[KAP * jr : KAP * jr + KAP]
        pairs.append((total * jnp.where(zero_wave, 0.5, 1.0) if jr == 0 else total, False))
    out = y_returned(pairs, unradix_ref, turn_ref)
    for jr in range(6):
        out_ref[pl.ds(jr, 64, stride=CHUNK), :] = out[:, 128 * jr : 128 * jr + 128]


def state_update_kernel(
    in_ref,
    state_ref,
    start_ref,
    twiddle_ref,
    untable_ref,
    tendency_hbm,
    new_hbm,
    first,
    whole,
    tendency_ref,
    new_ref,
    sems,
):
    depth = 8 * CHUNK
    table = [untable_ref[0], untable_ref[1]]
    for group in range(2):
        blocks = [in_ref[depth * slot : depth * slot + depth, :] for slot in range(4 * group, 4 * group + 4)]
        side = jnp.concatenate(regroup(blocks, range(4)), axis=0)
        whole[128 * group : 128 * group + 128, :] = matmul(split(side), table, TN)
        if group == 0:
            row = lax.broadcasted_iota(jnp.int32, (4 * depth, 1), 0)
            own = jnp.where(row % depth < depth // 2, side, 0.0)
            first[...] = matmul(split(own), table, TN)
    twiddle = twiddle_ref[...]
    sends = []
    for block in range(4):
        rows = slice(8 * block, 8 * block + 8)

        def source(k):
            if k == 0:
                return first[rows, :]
            start = 32 * (k % 8) + rows.start
            z = whole[start : start + 8, :]
            return z if k < 8 else z - source(0)

        tendency = real_synthesis(*modes_of(source, twiddle))
        for a in range(16):
            columns = slice(128 * a, 128 * a + 128)
            tendency_ref[0, rows, columns] = tendency[a]
            new_ref[0, rows, columns] = 0.75 * start_ref[0, rows, columns] + 0.25 * (
                state_ref[0, rows, columns] + STEP_SIZE * tendency[a]
            )
        for i, (near, far) in enumerate(((tendency_ref, tendency_hbm), (new_ref, new_hbm))):
            own = (slice(None), pl.ds(8 * block, 8))
            sends.append(pltpu.make_async_copy(near.at[own], far.at[own], sems.at[2 * block + i]))
            sends[-1].start()
    for send in sends:
        send.wait()


VMEM = pl.BlockSpec(memory_space=pltpu.VMEM)
SMEM = pl.BlockSpec(memory_space=pltpu.SMEM)
ANY = pl.BlockSpec(memory_space=pl.ANY)
MIB = 1024 * 1024


def call(kernel, outs, operands, scalars=0, scratch=(), far_in=False, far_out=False, copies=0, cost=None):
    scratch_shapes = [pltpu.VMEM(operand.shape, operand.dtype) for operand in operands] if far_in else []
    scratch_shapes += [pltpu.VMEM(shape, F32) for shape in scratch]
    scratch_shapes += [pltpu.VMEM(shape, F32) for shape in outs] if far_out else []
    scratch_shapes += [pltpu.SemaphoreType.DMA((copies,))] if copies else []
    near = [SMEM] * scalars + [VMEM] * (len(operands) - scalars)
    return pl.pallas_call(
        kernel,
        out_shape=[jax.ShapeDtypeStruct(shape, F32) for shape in outs],
        in_specs=[ANY] * len(operands) if far_in else near,
        out_specs=[ANY if far_out else VMEM] * len(outs),
        scratch_shapes=scratch_shapes,
        compiler_params=pltpu.CompilerParams(vmem_limit_bytes=(60 if far_in else 32) * MIB),
        cost_estimate=cost,
    )(*operands)


def exchange(chunks, devices):
    length = chunks.shape[0]
    sent = chunks.reshape(devices, 1, length * 128 // devices)
    return lax.all_to_all(sent, "row", split_axis=0, concat_axis=0, tiled=True).reshape(length, 128)


def per_device(state, start_state, to_modes, from_modes, deform):
    devices = lax.axis_size("row")
    turn_x = jnp.asarray(x_twiddle())
    forward_x = jnp.asarray(x_forward_table())
    inverse_x = jnp.asarray(x_inverse_table(False))
    inverse_chunk = jnp.asarray(x_inverse_table(True))
    radix = jnp.asarray(y_radix_table())
    unradix = jnp.asarray(y_radix_inverse_table())
    turn_y = jnp.asarray(y_twiddle())
    lanes = jnp.asarray(y_lane_table())
    unlanes = jnp.asarray(y_lane_inverse_table())
    project = jnp.asarray(y_projection_table())
    mean = jnp.asarray(y_mean_table())
    facts = jnp.asarray(lane_facts())

    one, four = (64 * CHUNK, 128), (64 * MINE, 128)
    (columns,) = call(state_kernel, [one], [state, turn_x, forward_x], far_in=True, far_out=True, copies=5)
    columns = exchange(columns, devices)
    spectrum, used = call(
        spectrum_kernel, [(6 * KAP, 128), (8, USED)], [columns, radix, turn_y, lanes, facts]
    )
    (weights,) = call(
        weights_kernel,
        [(8, 8, USED)],
        [to_modes, from_modes, deform, jnp.asarray(packed_facts())],
        scalars=3,
        cost=pl.CostEstimate(flops=8_000_000, bytes_accessed=2_000_000, transcendentals=0),
    )
    gathered = lax.all_gather(used, "layer", axis=0, tiled=False)
    (fields,) = call(
        stream_kernel,
        [four],
        [weights, gathered, spectrum, unradix, turn_y, unlanes, facts],
        scratch=[(8, 128 * TILES)],
    )
    fields = exchange(fields, devices)
    (flux,) = call(
        jacobian_kernel,
        [one],
        [fields, turn_x, inverse_x, forward_x],
        scratch=[(128, 256), (1024, 256), (2, 9, ROWS, 128)],
    )
    flux = exchange(flux, devices)
    (total,) = call(
        projection_kernel,
        [one],
        [flux, spectrum, radix, unradix, turn_y, project, mean, unlanes, facts],
    )
    total = exchange(total, devices)
    return tuple(
        call(
            state_update_kernel,
            [(1, ROWS, GRID)] * 2,
            [total, state, start_state, turn_x, inverse_chunk],
            scratch=[(128, 256), (256, 256)],
            far_out=True,
            copies=8,
        )
    )


def solution(mesh):
    in_specs = (P("layer", "row", None), P("layer", "row", None), P(), P(), P())
    out_specs = (P("layer", "row", None), P("layer", "row", None))
    return jax.shard_map(
        per_device, mesh=mesh, in_specs=in_specs, out_specs=out_specs, check_vma=False
    )
```

```python
import functools
import math

import jax
import jax.numpy as jnp
import ml_dtypes
import numpy as np
from jax import lax
from jax.experimental import pallas as pl
from jax.experimental.pallas import tpu as pltpu
from jax.sharding import PartitionSpec as P

GRID = 2048
KCUT = 672
ROWS = 32
MINE = 21
CHUNK = 6
KAP = 64
JP = 11
PIECE = 4 * 2 * JP
USED = 8 * MINE * 2 * JP
TILES = -(-USED // 128)
HYPER_RATE = 0.2
STEP_SIZE = 0.5
BF16 = jnp.bfloat16
F32 = jnp.float32


def halves(table):
    high = table.astype(ml_dtypes.bfloat16)
    low = (table - high.astype(np.float64)).astype(ml_dtypes.bfloat16)
    return np.stack([high, low])


def turn(numerator, denominator):
    angle = 2.0 * math.pi * (np.mod(numerator, denominator) / denominator)
    return np.cos(angle), np.sin(angle)


def column_j(h, i):
    return 21 * h + i - 84 * (h // 2)


def x_forward_table():
    b = np.arange(128)
    table = np.zeros((2, 4, 2, 2, 6, 2, 128))
    for h in range(4):
        for i in range(MINE):
            c, s = turn(column_j(h, i) * b, 128)
            own = table[h // 2, i % 4, h % 2, :, i // 4]
            own[0, 0], own[0, 1], own[1, 0], own[1, 1] = c, s, -s, c
    return np.concatenate(list(halves(table.reshape(2, 96, 256))), axis=1)


def x_inverse_table(by_chunk):
    b = np.arange(128)
    table = np.zeros((4, 4, 2, 6, 2, 128)) if by_chunk else np.zeros((4, 2, MINE, 2, 128))
    for h in range(4):
        for i in range(MINE):
            c, s = turn(column_j(h, i) * b, 128)
            own = table[i % 4, h, :, i // 4] if by_chunk else table[h, :, i]
            own[0, 0], own[0, 1], own[1, 0], own[1, 1] = c, s, -s, c
    table = table.reshape(-1, 256) * (2.0 / (GRID * GRID))
    return halves(table if by_chunk else np.pad(table, ((0, 8), (0, 0))))


def x_twiddle():
    table = np.zeros((32, 128))
    c, s = turn(np.arange(9)[:, None] * np.arange(128)[None, :], GRID)
    table[0:9] = c
    table[16:25] = s
    return table.astype(np.float32)


def y_radix_table():
    c, s = turn(np.arange(KAP)[:, None] * np.arange(64)[None, :], 64)
    high, low = halves(np.concatenate([c, -s], axis=0))
    return np.concatenate([high, high, low], axis=1)


def y_radix_inverse_table():
    c, s = turn(np.arange(64)[:, None] * np.arange(KAP)[None, :], 64)
    high, low = halves(np.concatenate([c, -s], axis=1))
    return np.block([[high, high], [low, np.zeros_like(low)]])


def y_twiddle():
    c, s = turn(np.arange(KAP)[:, None] * np.arange(ROWS)[None, :], GRID)
    return np.stack([np.tile(c, (1, 4)), np.tile(s, (1, 4))]).astype(np.float32)


def lanes_of():
    c, s = turn(np.arange(ROWS)[:, None] * np.arange(JP)[None, :], ROWS)
    table = np.zeros((2, 4, ROWS, 128))
    for jb in range(4):
        re = slice(2 * JP * jb, 2 * JP * jb + JP)
        im = slice(2 * JP * jb + JP, 2 * JP * jb + 2 * JP)
        table[0, jb, :, re], table[1, jb, :, re] = c, s
        table[0, jb, :, im], table[1, jb, :, im] = -s, c
    return table.reshape(256, 128)


def y_lane_table():
    return np.concatenate(list(halves(lanes_of())), axis=1)


def y_lane_inverse_table():
    high, low = halves(2.0 * lanes_of().T)
    return np.concatenate([high, high, low], axis=0)


def y_projection_table():
    difference = np.arange(ROWS)[None, :] - np.arange(ROWS)[:, None]
    tables = []
    for count in (JP, JP - 1):
        c, s = turn(difference[:, :, None] * np.arange(count)[None, None, :], ROWS)
        c, s = np.kron(np.eye(4), 2 * c.sum(-1)), np.kron(np.eye(4), 2 * s.sum(-1))
        tables.append(np.block([[c, s], [-s, c]]))
    return halves(np.stack(tables))


def y_mean_table():
    return np.kron(np.eye(8), np.ones((ROWS, ROWS))).astype(ml_dtypes.bfloat16)


def lane_facts():
    lane = np.arange(128)
    facts = np.zeros((8, 128))
    facts[0] = 16 * (lane // (2 * JP))
    facts[1] = 64 * (lane % JP)
    return facts.astype(np.float32)


def packed_facts():
    lane = np.arange(USED)
    own = lane % (USED // 8)
    facts = np.zeros((8, USED))
    facts[0] = 16 * (own // (2 * JP))
    facts[1] = 64 * (own % JP) + 8 * (lane // (USED // 8))
    return facts.astype(np.float32)


def split(value):
    high = value.astype(BF16)
    low = (value - high.astype(F32)).astype(BF16)
    return high, low


def dot(a, b, dims):
    return lax.dot_general(a, b, (dims, ((), ())), preferred_element_type=F32)


def matmul(left, right, dims):
    return dot(left[0], right[0], dims) + (dot(left[0], right[1], dims) + dot(left[1], right[0], dims))


def matmul_tall(table, right):
    out = dot(table[...], jnp.concatenate(right, axis=0), NN)
    size = table.shape[0] // 2
    return out[:size] + out[size:]


def matmul_wide(left, table):
    depth = left[0].shape[1]
    both = jnp.concatenate(left, axis=1)
    return dot(both, table[: 2 * depth], NN) + dot(left[0], table[2 * depth :], NN)


def matmul_beside(left, table):
    size = table.shape[1] // 2
    out = dot(left[0], table[...], NN)
    return out[:, :size] + (out[:, size:] + dot(left[1], table[:, :size], NN))


NN = ((1,), (0,))
NT = ((1,), (1,))
TN = ((0,), (0,))

C1 = math.cos(math.pi / 8)
C2 = math.cos(math.pi / 4)
C3 = math.cos(3 * math.pi / 8)


def real_analysis(x):
    s = [x[a] + x[a + 8] for a in range(8)]
    d = [x[a] - x[a + 8] for a in range(8)]
    e = [None] + [d[a] - d[8 - a] for a in range(1, 4)]
    f = [None] + [d[a] + d[8 - a] for a in range(1, 4)]
    e2, f2 = e[2] * C2, f[2] * C2
    plus, minus = d[0] + e2, d[0] - e2
    first, second = e[1] * C1 + e[3] * C3, e[1] * C3 - e[3] * C1
    third, fourth = f[1] * C3 + f[3] * C1, f[1] * C1 - f[3] * C3
    u, v = d[4] + f2, f2 - d[4]
    p = [s[a] + s[a + 4] for a in range(4)]
    q = [s[a] - s[a + 4] for a in range(4)]
    even, odd = p[0] + p[2], p[1] + p[3]
    hd, hs = (q[1] - q[3]) * C2, (q[1] + q[3]) * C2
    real = [
        even + odd,
        plus + first,
        q[0] + hd,
        minus + second,
        p[0] - p[2],
        minus - second,
        q[0] - hd,
        plus - first,
        even - odd,
    ]
    imag = [
        None,
        -(third + u),
        -(q[2] + hs),
        -(fourth + v),
        p[3] - p[1],
        v - fourth,
        q[2] - hs,
        u - third,
        None,
    ]
    return real, imag


def real_synthesis(real, imag):
    plus, first = real[1] + real[7], real[1] - real[7]
    minus, second = real[3] + real[5], real[3] - real[5]
    third, u = -(imag[1] + imag[7]), imag[7] - imag[1]
    fourth, v = -(imag[3] + imag[5]), imag[5] - imag[3]
    d = [None] * 8
    d[0], d[4] = plus + minus, u - v
    e = [None, first * C1 + second * C3, (plus - minus) * C2, first * C3 - second * C1]
    f = [None, third * C3 + fourth * C1, (u + v) * C2, third * C1 - fourth * C3]
    for a in range(1, 4):
        d[a], d[8 - a] = f[a] + e[a], f[a] - e[a]
    even, odd = real[0] + real[8], real[0] - real[8]
    p = [even + real[4], odd - imag[4], even - real[4], odd + imag[4]]
    hr, hi = (real[2] - real[6]) * C2, (imag[2] + imag[6]) * C2
    q = [real[2] + real[6], hr - hi, imag[6] - imag[2], -(hr + hi)]
    s = [p[a] + q[a] for a in range(4)] + [p[a] - q[a] for a in range(4)]
    return [s[a] + d[a] for a in range(8)] + [s[a] - d[a] for a in range(8)]


def regroup(blocks, wanted):
    block = lax.broadcasted_iota(jnp.int32, (1, 128), 1) // 32
    turned = [
        b if b is None or i == 0 else pltpu.roll(b, 32 * i, 1) for i, b in enumerate(blocks)
    ]
    results = []
    for p in wanted:
        total = None
        for i in range(4):
            part = jnp.zeros_like(turned[0]) if turned[i] is None else turned[i]
            total = part if total is None else jnp.where(block == (p + i) % 4, part, total)
        results.append(total if p == 0 else pltpu.roll(total, 128 - 32 * p, 1))
    return results


def turn_by(re, im, c, s):
    return re * c + im * s, im * c - re * s


def x_forward(real, imag, twiddle, table):
    pieces = []
    for k in range(9):
        if k == 0:
            pieces.append(jnp.concatenate([real[0], jnp.zeros_like(real[0])], axis=1))
            continue
        c, s = twiddle[k : k + 1], twiddle[16 + k : 17 + k]
        if k == 8:
            re, im = real[8] * c, -(real[8] * s)
        else:
            re, im = real[k] * c + imag[k] * s, imag[k] * c - real[k] * s
        pieces.append(jnp.concatenate([re, im], axis=1))
    shared = split(jnp.concatenate(pieces[1:8], axis=0))
    results = []
    for half, own in enumerate((pieces[0], pieces[8])):
        own = split(own)
        right = [jnp.concatenate([own[i], shared[i]], axis=0) for i in range(2)]
        out = dot(table[half], right[0], NT)
        results.append(out[:96] + (out[96:] + dot(table[half, :96], right[1], NT)))
    return results


def modes_of(source, twiddle, turned=False):
    real, imag = [], []
    for k in range(9):
        c, s = twiddle[k : k + 1], twiddle[16 + k : 17 + k]
        z = source(k)
        re, im = z[:, :128], z[:, 128:]
        if k == 0:
            real.append(im if turned else re)
            imag.append(None)
            continue
        real.append(im * c + re * s if turned else re * c - im * s)
        if k == 8:
            imag.append(None)
        else:
            imag.append(im * s - re * c if turned else re * s + im * c)
    return real, imag


def y_turned(in_ref, radix, twiddle):
    columns = [in_ref[pl.ds(jr, 64, stride=CHUNK), :] for jr in range(6)]
    high, low = split(jnp.concatenate(columns, axis=1))
    mixed = dot(radix[...], jnp.concatenate([high, low, high], axis=0), NN)
    results = []
    for jr in range(6):
        lanes = slice(128 * jr, 128 * jr + 128)
        re, im = turn_by(mixed[:KAP, lanes], mixed[KAP:, lanes], twiddle[0], twiddle[1])
        results.append(jnp.concatenate([re, im], axis=1))
    return results


def y_returned(pairs, radix, twiddle):
    lane = lax.broadcasted_iota(jnp.int32, (1, 128), 1)
    c, s = twiddle[0], twiddle[1]
    real, imag = [], []
    for pair, turned in pairs:
        re, im = pair[:, :128], pair[:, 128:]
        if turned in (0, 4):
            real.append(im * c + re * s if turned else re * c - im * s)
            imag.append(im * s - re * c if turned else re * s + im * c)
            continue
        early = lane < 32 * turned
        re, im = jnp.where(early, im, re), jnp.where(early, -re, im)
        real.append(re * c - im * s)
        imag.append(re * s + im * c)
    right = jnp.concatenate([jnp.concatenate(real, axis=1), jnp.concatenate(imag, axis=1)], axis=0)
    return matmul_tall(radix, split(right))


def pieces_of():
    for rows in range(8):
        for jr in range(6):
            index, offset = divmod(rows * (USED // 8) + PIECE * jr, 128)
            yield rows, jr, index, offset, PIECE if jr < 5 else 2 * JP


def pack(tiles):
    lane = lax.broadcasted_iota(jnp.int32, (1, 128), 1)
    packed = [None] * TILES
    for rows, jr, index, offset, used in pieces_of():
        moved = tiles[jr][8 * rows : 8 * rows + 8]
        moved = pltpu.roll(moved, offset, 1) if offset else moved
        parts = [(index, moved)]
        if offset + used > 128:
            parts = [(index, jnp.where(lane >= offset, moved, 0.0))]
            parts.append((index + 1, jnp.where(lane < offset, moved, 0.0)))
        for own, part in parts:
            packed[own] = part if packed[own] is None else packed[own] + part
    return packed


def unpack(packed):
    lane = lax.broadcasted_iota(jnp.int32, (1, 128), 1)
    tiles = [[] for _ in range(6)]
    for rows, jr, index, offset, used in pieces_of():
        tile = packed[:, 128 * index : 128 * index + 128]
        if offset + used > 128:
            tile = jnp.where(lane >= offset, tile, packed[:, 128 * index + 128 : 128 * index + 256])
        tiles[jr].append(pltpu.roll(tile, 128 - offset, 1) if offset else tile)
    return [jnp.concatenate(tile, axis=0) for tile in tiles]


def y_waves(facts, count=KAP):
    row = lax.broadcasted_iota(jnp.int32, (count, 1), 0).astype(F32)
    return row + facts[1:2]


def x_waves(facts, owner):
    slot = owner // 8
    h = (owner % 8) // 2
    eight = jnp.where(slot == 0, 8 * (h // 2), 0)
    return facts[0:1] + (slot + eight + 16 * (21 * h - 84 * (h // 2))).astype(F32)


def half_of_zero(wave):
    return jnp.where(wave == 0.0, 0.5, 1.0)


def store_x(out_ref, results, group):
    for half in range(2):
        lanes = slice(128 * group, 128 * group + 128)
        blocks = [results[half][24 * jb : 24 * jb + 24, lanes] for jb in range(4)]
        for slot, block in enumerate(regroup(blocks, range(4))):
            start = (8 * (4 * group + slot) + 4 * half) * CHUNK
            out_ref[start : start + 4 * CHUNK, :] = block


def state_kernel(
    state_hbm, twiddle_hbm, table_hbm, out_hbm, state_ref, twiddle_ref, table_ref, out_ref, sems
):
    pairs = ((state_hbm, state_ref), (twiddle_hbm, twiddle_ref), (table_hbm, table_ref))
    copies = [pltpu.make_async_copy(a, b, sems.at[i]) for i, (a, b) in enumerate(pairs)]
    for copy in copies:
        copy.start()
    copies[0].wait()
    x = [state_ref[0, :, 128 * a : 128 * a + 128] for a in range(16)]
    real, imag = real_analysis(x)
    copies[1].wait()
    copies[2].wait()
    results = x_forward(real, imag, twiddle_ref[...], table_ref)
    for group in range(2):
        store_x(out_ref, results, group)
        rows = pl.ds(32 * group * CHUNK, 32 * CHUNK)
        pltpu.make_async_copy(out_ref.at[rows], out_hbm.at[rows], sems.at[3]).start()
    pltpu.make_async_copy(out_ref, out_hbm, sems.at[3]).wait()


def weights_kernel(to_ref, from_ref, deform_ref, facts_ref, out_ref):
    facts = facts_ref[...]
    wave_x = x_waves(facts, lax.axis_index("row"))
    wave_y = y_waves(facts, 8)
    square = wave_x * wave_x + wave_y * wave_y
    layer = lax.axis_index("layer")
    modes = [from_ref[layer, m] * (-1.0 / (square + deform_ref[m])) for m in range(8)]
    for n in range(8):
        total = None
        for m in range(8):
            term = modes[m] * to_ref[m, n]
            total = term if total is None else total + term
        out_ref[n] = total


def spectrum_kernel(in_ref, radix_ref, turn_ref, lanes_ref, facts_ref, spec_ref, used_ref):
    turned = split(jnp.concatenate(y_turned(in_ref, radix_ref, turn_ref), axis=0))
    spectrum = matmul_beside(turned, lanes_ref)
    kept = y_waves(facts_ref[...]) < KCUT
    tiles = [jnp.where(kept, spectrum[KAP * jr : KAP * jr + KAP], 0.0) for jr in range(6)]
    spec_ref[...] = jnp.concatenate(tiles, axis=0)
    for index, tile in enumerate(pack(tiles)):
        lanes = slice(128 * index, min(USED, 128 * index + 128))
        used_ref[:, lanes] = tile[:, : lanes.stop - lanes.start]


def stream_kernel(
    weights_ref, all_ref, spec_ref, unradix_ref, turn_ref, unlanes_ref, facts_ref, out_ref, stream_ref
):
    stream = None
    for n in range(8):
        term = weights_ref[n] * all_ref[n]
        stream = term if stream is None else stream + term
    stream_ref[:, 128 * TILES - 128 :] = jnp.zeros((8, 128), F32)
    stream_ref[:, :USED] = stream
    facts = facts_ref[...]
    wave_y = y_waves(facts)
    once = half_of_zero(wave_y)
    pieces = []
    for jr, tile in enumerate(unpack(stream_ref[...])):
        wave_x = x_waves(facts, lax.axis_index("row")) + 64 * jr
        along_y, along_x = wave_y * half_of_zero(wave_x), wave_x * once
        own = spec_ref[KAP * jr : KAP * jr + KAP, :]
        four = [along_y * tile, -along_y * own, along_x * tile, along_x * own]
        if jr < 5:
            pieces += four
            continue
        alone = lax.broadcasted_iota(jnp.int32, (1, 128), 1) < 2 * JP
        four = [jnp.where(alone, field, 0.0) for field in four]
        moved = [four[0]] + [pltpu.roll(four[f], 2 * JP * f, 1) for f in range(1, 4)]
        pieces.append((moved[0] + moved[1]) + (moved[2] + moved[3]))
    out = matmul_wide(split(jnp.concatenate(pieces, axis=0)), unlanes_ref)
    turned = [4, 4, 0, 0] * 5 + [2]
    pairs = [(out[KAP * i : KAP * i + KAP], turned[i]) for i in range(21)]
    out = y_returned(pairs, unradix_ref, turn_ref)
    for jr in range(5):
        blocks = [out[:, 128 * (4 * jr + f) : 128 * (4 * jr + f) + 128] for f in range(4)]
        for jb, block in enumerate(regroup(blocks, range(4))):
            out_ref[pl.ds(4 * jr + jb, 64, stride=MINE), :] = block
    out_ref[pl.ds(20, 64, stride=MINE), :] = out[:, 128 * 20 :]


def jacobian_kernel(in_ref, twiddle_ref, untable_ref, table_ref, out_ref, first_ref, whole_ref, jac):
    depth = 8 * MINE
    row = lax.broadcasted_iota(jnp.int32, (depth, 1), 0)
    spare = jnp.zeros((8, 4 * 128), F32)
    table = [untable_ref[0], untable_ref[1]]
    for part in range(2):
        slots = [
            in_ref[depth * slot : depth * slot + depth, :] for slot in range(4 * part, 4 * part + 4)
        ]
        side = jnp.concatenate([jnp.concatenate(slots, axis=1), spare], axis=0)
        whole_ref[512 * part : 512 * part + 512, :] = matmul(split(side), table, TN)
        if part == 0:
            own = jnp.concatenate([jnp.where(row < depth // 2, slots[0], 0.0), spare[:, :128]], axis=0)
            first_ref[...] = matmul(split(own), table, TN)
    twiddle = twiddle_ref[...]
    for block in range(4):
        rows = slice(8 * block, 8 * block + 8)

        def physical(field):
            def source(k):
                start = 32 * field + rows.start
                if k == 0:
                    return first_ref[start : start + 8, :]
                start += 128 * (k % 8)
                z = whole_ref[start : start + 8, :]
                return z if k < 8 else z - source(0)

            return real_synthesis(*modes_of(source, twiddle, field > 1))

        east, slope_x = physical(0), physical(3)
        product = [a * b for a, b in zip(east, slope_x)]
        north, slope_y = physical(2), physical(1)
        product = [p + a * b for p, a, b in zip(product, north, slope_y)]
        real, imag = real_analysis(product)
        for k in range(9):
            jac[0, k, rows, :] = real[k]
            if imag[k] is not None:
                jac[1, k, rows, :] = imag[k]
    real = [jac[0, k] for k in range(9)]
    imag = [None] + [jac[1, k] for k in range(1, 8)] + [None]
    results = x_forward(real, imag, twiddle, table_ref)
    for group in range(2):
        store_x(out_ref, results, group)


def projection_kernel(
    in_ref, spec_ref, radix_ref, unradix_ref, turn_ref, project_ref, mean_ref, unlanes_ref, facts_ref, out_ref
):
    facts = facts_ref[...]
    wave_y = y_waves(facts)
    once = half_of_zero(wave_y)
    damped = []
    for jr in range(6):
        wave_x = x_waves(facts, lax.axis_index("row")) + 64 * jr
        ratio = (wave_x * wave_x + wave_y * wave_y) * (1.0 / (KCUT * KCUT))
        ratio = ratio * ratio
        damped.append(((HYPER_RATE * (ratio * ratio)) * once) * spec_ref[KAP * jr : KAP * jr + KAP, :])
    damping = matmul_wide(split(jnp.concatenate(damped, axis=0)), unlanes_ref)
    left = [split(pair) for pair in y_turned(in_ref, radix_ref, turn_ref)]
    sides = []
    for side in range(2):
        rows = slice(32 * side, 32 * side + 32)
        stacked = [jnp.concatenate([pair[i][rows] for pair in left], axis=0) for i in range(2)]
        sides.append(matmul(stacked, [project_ref[i, side] for i in range(2)], NN))
    heads = [jnp.concatenate([pair[i][:16] for pair in left], axis=0) for i in range(2)]
    mean = dot(heads[0], mean_ref[...], NN) + dot(heads[1], mean_ref[...], NN)
    first = lax.broadcasted_iota(jnp.int32, (16, 1), 0) == 0
    lane = lax.broadcasted_iota(jnp.int32, (1, 256), 1)
    zero_wave = (lax.axis_index("row") < 2) & (lane % 128 < 32)
    pairs = []
    for jr in range(6):
        low, high = [side[32 * jr : 32 * jr + 32] for side in sides]
        own = jnp.where(first, mean[16 * jr : 16 * jr + 16], 0.0)
        flux = jnp.concatenate([low[:16] - own, low[16:], high], axis=0)
        total = flux - damping[KAP * jr : KAP * jr + KAP]
        pairs.append((total * jnp.where(zero_wave, 0.5, 1.0) if jr == 0 else total, 0))
    out = y_returned(pairs, unradix_ref, turn_ref)
    for jr in range(6):
        out_ref[pl.ds(jr, 64, stride=CHUNK), :] = out[:, 128 * jr : 128 * jr + 128]


def state_update_kernel(
    in_ref,
    state_ref,
    start_ref,
    twiddle_ref,
    untable_ref,
    tendency_hbm,
    new_hbm,
    first,
    whole,
    tendency_ref,
    new_ref,
    sems,
):
    depth = 8 * CHUNK
    table = [untable_ref[0], untable_ref[1]]
    for group in range(2):
        blocks = [in_ref[depth * slot : depth * slot + depth, :] for slot in range(4 * group, 4 * group + 4)]
        side = jnp.concatenate(regroup(blocks, range(4)), axis=0)
        whole[128 * group : 128 * group + 128, :] = matmul(split(side), table, TN)
        if group == 0:
            row = lax.broadcasted_iota(jnp.int32, (4 * depth, 1), 0)
            own = jnp.where(row % depth < depth // 2, side, 0.0)
            first[...] = matmul(split(own), table, TN)
    twiddle = twiddle_ref[...]
    for block in range(4):
        rows = slice(8 * block, 8 * block + 8)

        def source(k):
            if k == 0:
                return first[rows, :]
            start = 32 * (k % 8) + rows.start
            z = whole[start : start + 8, :]
            return z if k < 8 else z - source(0)

        tendency = real_synthesis(*modes_of(source, twiddle))
        for a in range(16):
            columns = slice(128 * a, 128 * a + 128)
            tendency_ref[0, rows, columns] = tendency[a]
            new_ref[0, rows, columns] = 0.75 * start_ref[0, rows, columns] + 0.25 * (
                state_ref[0, rows, columns] + STEP_SIZE * tendency[a]
            )
        for i, (near, far) in enumerate(((tendency_ref, tendency_hbm), (new_ref, new_hbm))):
            own = (slice(None), pl.ds(8 * block, 8))
            pltpu.make_async_copy(near.at[own], far.at[own], sems.at[i]).start()
    pltpu.make_async_copy(tendency_ref, tendency_hbm, sems.at[0]).wait()
    pltpu.make_async_copy(new_ref, new_hbm, sems.at[1]).wait()


VMEM = pl.BlockSpec(memory_space=pltpu.VMEM)
SMEM = pl.BlockSpec(memory_space=pltpu.SMEM)
ANY = pl.BlockSpec(memory_space=pl.ANY)
MIB = 1024 * 1024


def call(kernel, outs, operands, scalars=0, scratch=(), far_in=False, far_out=False, copies=0, cost=None):
    scratch_shapes = [pltpu.VMEM(operand.shape, operand.dtype) for operand in operands] if far_in else []
    scratch_shapes += [pltpu.VMEM(shape, F32) for shape in scratch]
    scratch_shapes += [pltpu.VMEM(shape, F32) for shape in outs] if far_out else []
    scratch_shapes += [pltpu.SemaphoreType.DMA((copies,))] if copies else []
    near = [SMEM] * scalars + [VMEM] * (len(operands) - scalars)
    return pl.pallas_call(
        kernel,
        out_shape=[jax.ShapeDtypeStruct(shape, F32) for shape in outs],
        in_specs=[ANY] * len(operands) if far_in else near,
        out_specs=[ANY if far_out else VMEM] * len(outs),
        scratch_shapes=scratch_shapes,
        compiler_params=pltpu.CompilerParams(vmem_limit_bytes=(60 if far_in else 32) * MIB),
        cost_estimate=cost,
    )(*operands)


def exchange(chunks, devices):
    length = chunks.shape[0]
    sent = chunks.reshape(devices, 1, length * 128 // devices)
    return lax.all_to_all(sent, "row", split_axis=0, concat_axis=0, tiled=True).reshape(length, 128)


def per_device(state, start_state, to_modes, from_modes, deform):
    devices = lax.axis_size("row")
    turn_x = jnp.asarray(x_twiddle())
    forward_x = jnp.asarray(x_forward_table())
    inverse_x = jnp.asarray(x_inverse_table(False))
    inverse_chunk = jnp.asarray(x_inverse_table(True))
    radix = jnp.asarray(y_radix_table())
    unradix = jnp.asarray(y_radix_inverse_table())
    turn_y = jnp.asarray(y_twiddle())
    lanes = jnp.asarray(y_lane_table())
    unlanes = jnp.asarray(y_lane_inverse_table())
    project = jnp.asarray(y_projection_table())
    mean = jnp.asarray(y_mean_table())
    facts = jnp.asarray(lane_facts())

    one, four = (64 * CHUNK, 128), (64 * MINE, 128)
    (columns,) = call(state_kernel, [one], [state, turn_x, forward_x], far_in=True, far_out=True, copies=4)
    columns = exchange(columns, devices)
    spectrum, used = call(
        spectrum_kernel, [(6 * KAP, 128), (8, USED)], [columns, radix, turn_y, lanes, facts]
    )
    (weights,) = call(
        weights_kernel,
        [(8, 8, USED)],
        [to_modes, from_modes, deform, jnp.asarray(packed_facts())],
        scalars=3,
        cost=pl.CostEstimate(flops=8_000_000, bytes_accessed=2_000_000, transcendentals=0),
    )
    gathered = lax.all_gather(used, "layer", axis=0, tiled=False)
    (fields,) = call(
        stream_kernel,
        [four],
        [weights, gathered, spectrum, unradix, turn_y, unlanes, facts],
        scratch=[(8, 128 * TILES)],
    )
    fields = exchange(fields, devices)
    (flux,) = call(
        jacobian_kernel,
        [one],
        [fields, turn_x, inverse_x, forward_x],
        scratch=[(128, 256), (1024, 256), (2, 9, ROWS, 128)],
    )
    flux = exchange(flux, devices)
    (total,) = call(
        projection_kernel,
        [one],
        [flux, spectrum, radix, unradix, turn_y, project, mean, unlanes, facts],
    )
    total = exchange(total, devices)
    return tuple(
        call(
            state_update_kernel,
            [(1, ROWS, GRID)] * 2,
            [total, state, start_state, turn_x, inverse_chunk],
            scratch=[(128, 256), (256, 256)],
            far_out=True,
            copies=2,
        )
    )


def solution(mesh):
    in_specs = (P("layer", "row", None), P("layer", "row", None), P(), P(), P())
    out_specs = (P("layer", "row", None), P("layer", "row", None))
    return jax.shard_map(
        per_device, mesh=mesh, in_specs=in_specs, out_specs=out_specs, check_vma=False
    )
```

```python
import functools
import math

import jax
import jax.numpy as jnp
import ml_dtypes
import numpy as np
from jax import lax
from jax.experimental import pallas as pl
from jax.experimental.pallas import tpu as pltpu
from jax.sharding import PartitionSpec as P

GRID = 2048
KCUT = 672
ROWS = 32
MINE = 21
CHUNK = 6
KAP = 64
JP = 11
PIECE = 4 * 2 * JP
USED = 8 * MINE * 2 * JP
TILES = -(-USED // 128)
HYPER_RATE = 0.2
STEP_SIZE = 0.5
BF16 = jnp.bfloat16
F32 = jnp.float32


def halves(table):
    high = table.astype(ml_dtypes.bfloat16)
    low = (table - high.astype(np.float64)).astype(ml_dtypes.bfloat16)
    return np.stack([high, low])


def turn(numerator, denominator):
    angle = 2.0 * math.pi * (np.mod(numerator, denominator) / denominator)
    return np.cos(angle), np.sin(angle)


def column_j(h, i):
    return 21 * h + i - 84 * (h // 2)


def x_forward_table():
    b = np.arange(128)
    table = np.zeros((2, 4, 2, 2, 6, 2, 128))
    for h in range(4):
        for i in range(MINE):
            c, s = turn(column_j(h, i) * b, 128)
            own = table[h // 2, i % 4, h % 2, :, i // 4]
            own[0, 0], own[0, 1], own[1, 0], own[1, 1] = c, s, -s, c
    return np.concatenate(list(halves(table.reshape(2, 96, 256))), axis=1)


def x_inverse_table(by_chunk):
    b = np.arange(128)
    table = np.zeros((4, 4, 2, 6, 2, 128)) if by_chunk else np.zeros((4, 2, MINE, 2, 128))
    for h in range(4):
        for i in range(MINE):
            c, s = turn(column_j(h, i) * b, 128)
            own = table[i % 4, h, :, i // 4] if by_chunk else table[h, :, i]
            own[0, 0], own[0, 1], own[1, 0], own[1, 1] = c, s, -s, c
    table = table.reshape(-1, 256) * (2.0 / (GRID * GRID))
    return halves(table if by_chunk else np.pad(table, ((0, 8), (0, 0))))


def x_twiddle():
    table = np.zeros((32, 128))
    c, s = turn(np.arange(9)[:, None] * np.arange(128)[None, :], GRID)
    table[0:9] = c
    table[16:25] = s
    return table.astype(np.float32)


def y_radix_table():
    c, s = turn(np.arange(KAP)[:, None] * np.arange(64)[None, :], 64)
    high, low = halves(np.concatenate([c, -s], axis=0))
    return np.concatenate([high, high, low], axis=1)


def y_radix_inverse_table():
    c, s = turn(np.arange(64)[:, None] * np.arange(KAP)[None, :], 64)
    high, low = halves(np.concatenate([c, -s], axis=1))
    return np.block([[high, high], [low, np.zeros_like(low)]])


def y_twiddle():
    c, s = turn(np.arange(KAP)[:, None] * np.arange(ROWS)[None, :], GRID)
    return np.stack([np.tile(c, (1, 4)), np.tile(s, (1, 4))]).astype(np.float32)


def lanes_of():
    c, s = turn(np.arange(ROWS)[:, None] * np.arange(JP)[None, :], ROWS)
    table = np.zeros((2, 4, ROWS, 128))
    for jb in range(4):
        re = slice(2 * JP * jb, 2 * JP * jb + JP)
        im = slice(2 * JP * jb + JP, 2 * JP * jb + 2 * JP)
        table[0, jb, :, re], table[1, jb, :, re] = c, s
        table[0, jb, :, im], table[1, jb, :, im] = -s, c
    return table.reshape(256, 128)


def y_lane_table():
    return np.concatenate(list(halves(lanes_of())), axis=1)


def y_lane_inverse_table():
    high, low = halves(2.0 * lanes_of().T)
    return np.concatenate([high, high, low], axis=0)


def y_projection_table():
    difference = np.arange(ROWS)[None, :] - np.arange(ROWS)[:, None]
    tables = []
    for count in (JP, JP - 1):
        c, s = turn(difference[:, :, None] * np.arange(count)[None, None, :], ROWS)
        c, s = np.kron(np.eye(4), 2 * c.sum(-1)), np.kron(np.eye(4), 2 * s.sum(-1))
        tables.append(np.block([[c, s], [-s, c]]))
    return halves(np.stack(tables))


def y_mean_table():
    return np.kron(np.eye(8), np.ones((ROWS, ROWS))).astype(ml_dtypes.bfloat16)


def lane_facts():
    lane = np.arange(128)
    facts = np.zeros((8, 128))
    facts[0] = 16 * (lane // (2 * JP))
    facts[1] = 64 * (lane % JP)
    return facts.astype(np.float32)


def packed_facts():
    lane = np.arange(USED)
    own = lane % (USED // 8)
    facts = np.zeros((8, USED))
    facts[0] = 16 * (own // (2 * JP))
    facts[1] = 64 * (own % JP) + 8 * (lane // (USED // 8))
    return facts.astype(np.float32)


def split(value):
    high = value.astype(BF16)
    low = (value - high.astype(F32)).astype(BF16)
    return high, low


def dot(a, b, dims):
    return lax.dot_general(a, b, (dims, ((), ())), preferred_element_type=F32)


def matmul(left, right, dims):
    return dot(left[0], right[0], dims) + (dot(left[0], right[1], dims) + dot(left[1], right[0], dims))


def matmul_tall(table, right):
    out = dot(table[...], jnp.concatenate(right, axis=0), NN)
    size = table.shape[0] // 2
    return out[:size] + out[size:]


def matmul_wide(left, table):
    depth = left[0].shape[1]
    both = jnp.concatenate(left, axis=1)
    return dot(both, table[: 2 * depth], NN) + dot(left[0], table[2 * depth :], NN)


def matmul_beside(left, table):
    size = table.shape[1] // 2
    out = dot(left[0], table[...], NN)
    return out[:, :size] + (out[:, size:] + dot(left[1], table[:, :size], NN))


NN = ((1,), (0,))
NT = ((1,), (1,))
TN = ((0,), (0,))

C1 = math.cos(math.pi / 8)
C2 = math.cos(math.pi / 4)
C3 = math.cos(3 * math.pi / 8)


def real_analysis(x):
    s = [x[a] + x[a + 8] for a in range(8)]
    d = [x[a] - x[a + 8] for a in range(8)]
    e = [None] + [d[a] - d[8 - a] for a in range(1, 4)]
    f = [None] + [d[a] + d[8 - a] for a in range(1, 4)]
    e2, f2 = e[2] * C2, f[2] * C2
    plus, minus = d[0] + e2, d[0] - e2
    first, second = e[1] * C1 + e[3] * C3, e[1] * C3 - e[3] * C1
    third, fourth = f[1] * C3 + f[3] * C1, f[1] * C1 - f[3] * C3
    u, v = d[4] + f2, f2 - d[4]
    p = [s[a] + s[a + 4] for a in range(4)]
    q = [s[a] - s[a + 4] for a in range(4)]
    even, odd = p[0] + p[2], p[1] + p[3]
    hd, hs = (q[1] - q[3]) * C2, (q[1] + q[3]) * C2
    real = [
        even + odd,
        plus + first,
        q[0] + hd,
        minus + second,
        p[0] - p[2],
        minus - second,
        q[0] - hd,
        plus - first,
        even - odd,
    ]
    imag = [
        None,
        -(third + u),
        -(q[2] + hs),
        -(fourth + v),
        p[3] - p[1],
        v - fourth,
        q[2] - hs,
        u - third,
        None,
    ]
    return real, imag


def real_synthesis(real, imag):
    plus, first = real[1] + real[7], real[1] - real[7]
    minus, second = real[3] + real[5], real[3] - real[5]
    third, u = -(imag[1] + imag[7]), imag[7] - imag[1]
    fourth, v = -(imag[3] + imag[5]), imag[5] - imag[3]
    d = [None] * 8
    d[0], d[4] = plus + minus, u - v
    e = [None, first * C1 + second * C3, (plus - minus) * C2, first * C3 - second * C1]
    f = [None, third * C3 + fourth * C1, (u + v) * C2, third * C1 - fourth * C3]
    for a in range(1, 4):
        d[a], d[8 - a] = f[a] + e[a], f[a] - e[a]
    even, odd = real[0] + real[8], real[0] - real[8]
    p = [even + real[4], odd - imag[4], even - real[4], odd + imag[4]]
    hr, hi = (real[2] - real[6]) * C2, (imag[2] + imag[6]) * C2
    q = [real[2] + real[6], hr - hi, imag[6] - imag[2], -(hr + hi)]
    s = [p[a] + q[a] for a in range(4)] + [p[a] - q[a] for a in range(4)]
    return [s[a] + d[a] for a in range(8)] + [s[a] - d[a] for a in range(8)]


def regroup(blocks, wanted):
    block = lax.broadcasted_iota(jnp.int32, (1, 128), 1) // 32
    turned = [
        b if b is None or i == 0 else pltpu.roll(b, 32 * i, 1) for i, b in enumerate(blocks)
    ]
    results = []
    for p in wanted:
        total = None
        for i in range(4):
            part = jnp.zeros_like(turned[0]) if turned[i] is None else turned[i]
            total = part if total is None else jnp.where(block == (p + i) % 4, part, total)
        results.append(total if p == 0 else pltpu.roll(total, 128 - 32 * p, 1))
    return results


def turn_by(re, im, c, s):
    return re * c + im * s, im * c - re * s


def x_forward(real, imag, twiddle, table):
    pieces = []
    for k in range(9):
        if k == 0:
            pieces.append(jnp.concatenate([real[0], jnp.zeros_like(real[0])], axis=1))
            continue
        c, s = twiddle[k : k + 1], twiddle[16 + k : 17 + k]
        if k == 8:
            re, im = real[8] * c, -(real[8] * s)
        else:
            re, im = real[k] * c + imag[k] * s, imag[k] * c - real[k] * s
        pieces.append(jnp.concatenate([re, im], axis=1))
    shared = split(jnp.concatenate(pieces[1:8], axis=0))
    results = []
    for half, own in enumerate((pieces[0], pieces[8])):
        own = split(own)
        right = [jnp.concatenate([own[i], shared[i]], axis=0) for i in range(2)]
        out = dot(table[half], right[0], NT)
        results.append(out[:96] + (out[96:] + dot(table[half, :96], right[1], NT)))
    return results


def modes_of(source, twiddle, turned=False):
    real, imag = [], []
    for k in range(9):
        c, s = twiddle[k : k + 1], twiddle[16 + k : 17 + k]
        z = source(k)
        re, im = z[:, :128], z[:, 128:]
        if k == 0:
            real.append(im if turned else re)
            imag.append(None)
            continue
        real.append(im * c + re * s if turned else re * c - im * s)
        if k == 8:
            imag.append(None)
        else:
            imag.append(im * s - re * c if turned else re * s + im * c)
    return real, imag


def y_turned(in_ref, radix, twiddle):
    columns = [in_ref[pl.ds(jr, 64, stride=CHUNK), :] for jr in range(6)]
    high, low = split(jnp.concatenate(columns, axis=1))
    mixed = dot(radix[...], jnp.concatenate([high, low, high], axis=0), NN)
    results = []
    for jr in range(6):
        lanes = slice(128 * jr, 128 * jr + 128)
        re, im = turn_by(mixed[:KAP, lanes], mixed[KAP:, lanes], twiddle[0], twiddle[1])
        results.append(jnp.concatenate([re, im], axis=1))
    return results


def y_returned(pairs, radix, twiddle):
    lane = lax.broadcasted_iota(jnp.int32, (1, 128), 1)
    c, s = twiddle[0], twiddle[1]
    real, imag = [], []
    for pair, turned in pairs:
        re, im = pair[:, :128], pair[:, 128:]
        if turned in (0, 4):
            real.append(im * c + re * s if turned else re * c - im * s)
            imag.append(im * s - re * c if turned else re * s + im * c)
            continue
        early = lane < 32 * turned
        re, im = jnp.where(early, im, re), jnp.where(early, -re, im)
        real.append(re * c - im * s)
        imag.append(re * s + im * c)
    right = jnp.concatenate([jnp.concatenate(real, axis=1), jnp.concatenate(imag, axis=1)], axis=0)
    return matmul_tall(radix, split(right))


def pieces_of():
    for rows in range(8):
        for jr in range(6):
            index, offset = divmod(rows * (USED // 8) + PIECE * jr, 128)
            yield rows, jr, index, offset, PIECE if jr < 5 else 2 * JP


def pack(tiles):
    lane = lax.broadcasted_iota(jnp.int32, (1, 128), 1)
    packed = [None] * TILES
    for rows, jr, index, offset, used in pieces_of():
        moved = tiles[jr][8 * rows : 8 * rows + 8]
        moved = pltpu.roll(moved, offset, 1) if offset else moved
        parts = [(index, moved)]
        if offset + used > 128:
            parts = [(index, jnp.where(lane >= offset, moved, 0.0))]
            parts.append((index + 1, jnp.where(lane < offset, moved, 0.0)))
        for own, part in parts:
            packed[own] = part if packed[own] is None else packed[own] + part
    return packed


def unpack(packed):
    lane = lax.broadcasted_iota(jnp.int32, (1, 128), 1)
    tiles = [[] for _ in range(6)]
    for rows, jr, index, offset, used in pieces_of():
        tile = packed[:, 128 * index : 128 * index + 128]
        if offset + used > 128:
            tile = jnp.where(lane >= offset, tile, packed[:, 128 * index + 128 : 128 * index + 256])
        tiles[jr].append(pltpu.roll(tile, 128 - offset, 1) if offset else tile)
    return [jnp.concatenate(tile, axis=0) for tile in tiles]


def y_waves(facts, count=KAP):
    row = lax.broadcasted_iota(jnp.int32, (count, 1), 0).astype(F32)
    return row + facts[1:2]


def x_waves(facts, owner):
    slot = owner // 8
    h = (owner % 8) // 2
    eight = jnp.where(slot == 0, 8 * (h // 2), 0)
    return facts[0:1] + (slot + eight + 16 * (21 * h - 84 * (h // 2))).astype(F32)


def half_of_zero(wave):
    return jnp.where(wave == 0.0, 0.5, 1.0)


def store_x(out_ref, results, group):
    for half in range(2):
        lanes = slice(128 * group, 128 * group + 128)
        blocks = [results[half][24 * jb : 24 * jb + 24, lanes] for jb in range(4)]
        for slot, block in enumerate(regroup(blocks, range(4))):
            start = (8 * (4 * group + slot) + 4 * half) * CHUNK
            out_ref[start : start + 4 * CHUNK, :] = block


def state_kernel(
    state_hbm, twiddle_hbm, table_hbm, out_hbm, state_ref, twiddle_ref, table_ref, out_ref, sems
):
    pairs = ((state_hbm, state_ref), (twiddle_hbm, twiddle_ref), (table_hbm, table_ref))
    copies = [pltpu.make_async_copy(a, b, sems.at[i]) for i, (a, b) in enumerate(pairs)]
    for copy in copies:
        copy.start()
    copies[0].wait()
    x = [state_ref[0, :, 128 * a : 128 * a + 128] for a in range(16)]
    real, imag = real_analysis(x)
    copies[1].wait()
    copies[2].wait()
    results = x_forward(real, imag, twiddle_ref[...], table_ref)
    for group in range(2):
        store_x(out_ref, results, group)
        rows = pl.ds(32 * group * CHUNK, 32 * CHUNK)
        pltpu.make_async_copy(out_ref.at[rows], out_hbm.at[rows], sems.at[3]).start()
    pltpu.make_async_copy(out_ref, out_hbm, sems.at[3]).wait()


def weights_kernel(to_ref, from_ref, deform_ref, facts_ref, out_ref):
    facts = facts_ref[...]
    wave_x = x_waves(facts, lax.axis_index("row"))
    wave_y = y_waves(facts, 8)
    square = wave_x * wave_x + wave_y * wave_y
    layer = lax.axis_index("layer")
    modes = [from_ref[layer, m] * (-1.0 / (square + deform_ref[m])) for m in range(8)]
    for n in range(8):
        total = None
        for m in range(8):
            term = modes[m] * to_ref[m, n]
            total = term if total is None else total + term
        out_ref[n] = total


def spectrum_kernel(in_ref, radix_ref, turn_ref, lanes_ref, facts_ref, spec_ref, used_ref):
    turned = split(jnp.concatenate(y_turned(in_ref, radix_ref, turn_ref), axis=0))
    spectrum = matmul_beside(turned, lanes_ref)
    kept = y_waves(facts_ref[...]) < KCUT
    tiles = [jnp.where(kept, spectrum[KAP * jr : KAP * jr + KAP], 0.0) for jr in range(6)]
    spec_ref[...] = jnp.concatenate(tiles, axis=0)
    for index, tile in enumerate(pack(tiles)):
        lanes = slice(128 * index, min(USED, 128 * index + 128))
        used_ref[:, lanes] = tile[:, : lanes.stop - lanes.start]


def stream_kernel(
    weights_ref, all_ref, spec_ref, unradix_ref, turn_ref, unlanes_ref, facts_ref, out_ref, stream_ref
):
    stream = None
    for n in range(8):
        term = weights_ref[n] * all_ref[n]
        stream = term if stream is None else stream + term
    stream_ref[:, 128 * TILES - 128 :] = jnp.zeros((8, 128), F32)
    stream_ref[:, :USED] = stream
    facts = facts_ref[...]
    wave_y = y_waves(facts)
    once = half_of_zero(wave_y)
    pieces = []
    for jr, tile in enumerate(unpack(stream_ref[...])):
        wave_x = x_waves(facts, lax.axis_index("row")) + 64 * jr
        along_y, along_x = wave_y * half_of_zero(wave_x), wave_x * once
        own = spec_ref[KAP * jr : KAP * jr + KAP, :]
        four = [along_y * tile, -along_y * own, along_x * tile, along_x * own]
        if jr < 5:
            pieces += four
            continue
        alone = lax.broadcasted_iota(jnp.int32, (1, 128), 1) < 2 * JP
        four = [jnp.where(alone, field, 0.0) for field in four]
        moved = [four[0]] + [pltpu.roll(four[f], 2 * JP * f, 1) for f in range(1, 4)]
        pieces.append((moved[0] + moved[1]) + (moved[2] + moved[3]))
    out = matmul_wide(split(jnp.concatenate(pieces, axis=0)), unlanes_ref)
    turned = [4, 4, 0, 0] * 5 + [2]
    pairs = [(out[KAP * i : KAP * i + KAP], turned[i]) for i in range(21)]
    out = y_returned(pairs, unradix_ref, turn_ref)
    for jr in range(5):
        blocks = [out[:, 128 * (4 * jr + f) : 128 * (4 * jr + f) + 128] for f in range(4)]
        for jb, block in enumerate(regroup(blocks, range(4))):
            out_ref[pl.ds(4 * jr + jb, 64, stride=MINE), :] = block
    out_ref[pl.ds(20, 64, stride=MINE), :] = out[:, 128 * 20 :]


def jacobian_kernel(in_ref, twiddle_ref, untable_ref, table_ref, out_ref, first_ref, whole_ref, jac):
    depth = 8 * MINE
    row = lax.broadcasted_iota(jnp.int32, (depth, 1), 0)
    spare = jnp.zeros((8, 4 * 128), F32)
    table = [untable_ref[0], untable_ref[1]]
    for part in range(2):
        slots = [
            in_ref[depth * slot : depth * slot + depth, :] for slot in range(4 * part, 4 * part + 4)
        ]
        side = jnp.concatenate([jnp.concatenate(slots, axis=1), spare], axis=0)
        whole_ref[512 * part : 512 * part + 512, :] = matmul(split(side), table, TN)
        if part == 0:
            own = jnp.concatenate([jnp.where(row < depth // 2, slots[0], 0.0), spare[:, :128]], axis=0)
            first_ref[...] = matmul(split(own), table, TN)
    twiddle = twiddle_ref[...]
    for block in range(4):
        rows = slice(8 * block, 8 * block + 8)

        def physical(field):
            def source(k):
                start = 32 * field + rows.start
                if k == 0:
                    return first_ref[start : start + 8, :]
                start += 128 * (k % 8)
                z = whole_ref[start : start + 8, :]
                return z if k < 8 else z - source(0)

            return real_synthesis(*modes_of(source, twiddle, field > 1))

        east, slope_x = physical(0), physical(3)
        product = [a * b for a, b in zip(east, slope_x)]
        north, slope_y = physical(2), physical(1)
        product = [p + a * b for p, a, b in zip(product, north, slope_y)]
        real, imag = real_analysis(product)
        for k in range(9):
            jac[0, k, rows, :] = real[k]
            if imag[k] is not None:
                jac[1, k, rows, :] = imag[k]
    real = [jac[0, k] for k in range(9)]
    imag = [None] + [jac[1, k] for k in range(1, 8)] + [None]
    results = x_forward(real, imag, twiddle, table_ref)
    for group in range(2):
        store_x(out_ref, results, group)


def damping_kernel(spec_ref, unlanes_ref, facts_ref, out_ref):
    facts = facts_ref[...]
    wave_y = y_waves(facts)
    once = half_of_zero(wave_y)
    damped = []
    for jr in range(6):
        wave_x = x_waves(facts, lax.axis_index("row")) + 64 * jr
        ratio = (wave_x * wave_x + wave_y * wave_y) * (1.0 / (KCUT * KCUT))
        ratio = ratio * ratio
        damped.append(((HYPER_RATE * (ratio * ratio)) * once) * spec_ref[KAP * jr : KAP * jr + KAP, :])
    out_ref[...] = matmul_wide(split(jnp.concatenate(damped, axis=0)), unlanes_ref)


def projection_kernel(
    in_ref, damping_ref, radix_ref, unradix_ref, turn_ref, project_ref, mean_ref, out_ref
):
    left = [split(pair) for pair in y_turned(in_ref, radix_ref, turn_ref)]
    sides = []
    for side in range(2):
        rows = slice(32 * side, 32 * side + 32)
        stacked = [jnp.concatenate([pair[i][rows] for pair in left], axis=0) for i in range(2)]
        sides.append(matmul(stacked, [project_ref[i, side] for i in range(2)], NN))
    heads = [jnp.concatenate([pair[i][:16] for pair in left], axis=0) for i in range(2)]
    mean = dot(heads[0], mean_ref[...], NN) + dot(heads[1], mean_ref[...], NN)
    first = lax.broadcasted_iota(jnp.int32, (16, 1), 0) == 0
    lane = lax.broadcasted_iota(jnp.int32, (1, 256), 1)
    zero_wave = (lax.axis_index("row") < 2) & (lane % 128 < 32)
    pairs = []
    for jr in range(6):
        low, high = [side[32 * jr : 32 * jr + 32] for side in sides]
        own = jnp.where(first, mean[16 * jr : 16 * jr + 16], 0.0)
        flux = jnp.concatenate([low[:16] - own, low[16:], high], axis=0)
        total = flux - damping_ref[KAP * jr : KAP * jr + KAP, :]
        pairs.append((total * jnp.where(zero_wave, 0.5, 1.0) if jr == 0 else total, 0))
    out = y_returned(pairs, unradix_ref, turn_ref)
    for jr in range(6):
        out_ref[pl.ds(jr, 64, stride=CHUNK), :] = out[:, 128 * jr : 128 * jr + 128]


def state_update_kernel(
    in_ref,
    state_ref,
    start_ref,
    twiddle_ref,
    untable_ref,
    tendency_hbm,
    new_hbm,
    first,
    whole,
    tendency_ref,
    new_ref,
    sems,
):
    depth = 8 * CHUNK
    table = [untable_ref[0], untable_ref[1]]
    for group in range(2):
        blocks = [in_ref[depth * slot : depth * slot + depth, :] for slot in range(4 * group, 4 * group + 4)]
        side = jnp.concatenate(regroup(blocks, range(4)), axis=0)
        whole[128 * group : 128 * group + 128, :] = matmul(split(side), table, TN)
        if group == 0:
            row = lax.broadcasted_iota(jnp.int32, (4 * depth, 1), 0)
            own = jnp.where(row % depth < depth // 2, side, 0.0)
            first[...] = matmul(split(own), table, TN)
    twiddle = twiddle_ref[...]
    for block in range(4):
        rows = slice(8 * block, 8 * block + 8)

        def source(k):
            if k == 0:
                return first[rows, :]
            start = 32 * (k % 8) + rows.start
            z = whole[start : start + 8, :]
            return z if k < 8 else z - source(0)

        tendency = real_synthesis(*modes_of(source, twiddle))
        for a in range(16):
            columns = slice(128 * a, 128 * a + 128)
            tendency_ref[0, rows, columns] = tendency[a]
            new_ref[0, rows, columns] = 0.75 * start_ref[0, rows, columns] + 0.25 * (
                state_ref[0, rows, columns] + STEP_SIZE * tendency[a]
            )
        for i, (near, far) in enumerate(((tendency_ref, tendency_hbm), (new_ref, new_hbm))):
            own = (slice(None), pl.ds(8 * block, 8))
            pltpu.make_async_copy(near.at[own], far.at[own], sems.at[i]).start()
    pltpu.make_async_copy(tendency_ref, tendency_hbm, sems.at[0]).wait()
    pltpu.make_async_copy(new_ref, new_hbm, sems.at[1]).wait()


VMEM = pl.BlockSpec(memory_space=pltpu.VMEM)
SMEM = pl.BlockSpec(memory_space=pltpu.SMEM)
ANY = pl.BlockSpec(memory_space=pl.ANY)
MIB = 1024 * 1024


def call(kernel, outs, operands, scalars=0, scratch=(), far_in=False, far_out=False, copies=0, cost=None):
    scratch_shapes = [pltpu.VMEM(operand.shape, operand.dtype) for operand in operands] if far_in else []
    scratch_shapes += [pltpu.VMEM(shape, F32) for shape in scratch]
    scratch_shapes += [pltpu.VMEM(shape, F32) for shape in outs] if far_out else []
    scratch_shapes += [pltpu.SemaphoreType.DMA((copies,))] if copies else []
    near = [SMEM] * scalars + [VMEM] * (len(operands) - scalars)
    return pl.pallas_call(
        kernel,
        out_shape=[jax.ShapeDtypeStruct(shape, F32) for shape in outs],
        in_specs=[ANY] * len(operands) if far_in else near,
        out_specs=[ANY if far_out else VMEM] * len(outs),
        scratch_shapes=scratch_shapes,
        compiler_params=pltpu.CompilerParams(vmem_limit_bytes=(60 if far_in else 32) * MIB),
        cost_estimate=cost,
    )(*operands)


def exchange(chunks, devices):
    length = chunks.shape[0]
    sent = chunks.reshape(devices, 1, length * 128 // devices)
    return lax.all_to_all(sent, "row", split_axis=0, concat_axis=0, tiled=True).reshape(length, 128)


def per_device(state, start_state, to_modes, from_modes, deform):
    devices = lax.axis_size("row")
    turn_x = jnp.asarray(x_twiddle())
    forward_x = jnp.asarray(x_forward_table())
    inverse_x = jnp.asarray(x_inverse_table(False))
    inverse_chunk = jnp.asarray(x_inverse_table(True))
    radix = jnp.asarray(y_radix_table())
    unradix = jnp.asarray(y_radix_inverse_table())
    turn_y = jnp.asarray(y_twiddle())
    lanes = jnp.asarray(y_lane_table())
    unlanes = jnp.asarray(y_lane_inverse_table())
    project = jnp.asarray(y_projection_table())
    mean = jnp.asarray(y_mean_table())
    facts = jnp.asarray(lane_facts())

    one, four = (64 * CHUNK, 128), (64 * MINE, 128)
    (columns,) = call(state_kernel, [one], [state, turn_x, forward_x], far_in=True, far_out=True, copies=4)
    columns = exchange(columns, devices)
    spectrum, used = call(
        spectrum_kernel, [(6 * KAP, 128), (8, USED)], [columns, radix, turn_y, lanes, facts]
    )
    (weights,) = call(
        weights_kernel,
        [(8, 8, USED)],
        [to_modes, from_modes, deform, jnp.asarray(packed_facts())],
        scalars=3,
        cost=pl.CostEstimate(flops=8_000_000, bytes_accessed=2_000_000, transcendentals=0),
    )
    gathered = lax.all_gather(used, "layer", axis=0, tiled=False)
    (fields,) = call(
        stream_kernel,
        [four],
        [weights, gathered, spectrum, unradix, turn_y, unlanes, facts],
        scratch=[(8, 128 * TILES)],
    )
    fields = exchange(fields, devices)
    (flux,) = call(
        jacobian_kernel,
        [one],
        [fields, turn_x, inverse_x, forward_x],
        scratch=[(128, 256), (1024, 256), (2, 9, ROWS, 128)],
    )
    flux = exchange(flux, devices)
    (damping,) = call(
        damping_kernel,
        [(6 * KAP, 256)],
        [spectrum, unlanes, facts],
        cost=pl.CostEstimate(flops=150_000_000, bytes_accessed=1_000_000, transcendentals=0),
    )
    (total,) = call(
        projection_kernel,
        [one],
        [flux, damping, radix, unradix, turn_y, project, mean],
    )
    total = exchange(total, devices)
    return tuple(
        call(
            state_update_kernel,
            [(1, ROWS, GRID)] * 2,
            [total, state, start_state, turn_x, inverse_chunk],
            scratch=[(128, 256), (256, 256)],
            far_out=True,
            copies=2,
        )
    )


def solution(mesh):
    in_specs = (P("layer", "row", None), P("layer", "row", None), P(), P(), P())
    out_specs = (P("layer", "row", None), P("layer", "row", None))
    return jax.shard_map(
        per_device, mesh=mesh, in_specs=in_specs, out_specs=out_specs, check_vma=False
    )
```

```python
import functools
import math

import jax
import jax.numpy as jnp
import ml_dtypes
import numpy as np
from jax import lax
from jax.experimental import pallas as pl
from jax.experimental.pallas import tpu as pltpu
from jax.sharding import PartitionSpec as P

GRID = 2048
KCUT = 672
ROWS = 32
MINE = 21
CHUNK = 6
KAP = 64
JP = 11
PIECE = 4 * 2 * JP
USED = 8 * MINE * 2 * JP
TILES = -(-USED // 128)
HYPER_RATE = 0.2
STEP_SIZE = 0.5
BF16 = jnp.bfloat16
F32 = jnp.float32


def halves(table):
    high = table.astype(ml_dtypes.bfloat16)
    low = (table - high.astype(np.float64)).astype(ml_dtypes.bfloat16)
    return np.stack([high, low])


def turn(numerator, denominator):
    angle = 2.0 * math.pi * (np.mod(numerator, denominator) / denominator)
    return np.cos(angle), np.sin(angle)


def column_j(h, i):
    return 21 * h + i - 84 * (h // 2)


def x_forward_table():
    b = np.arange(128)
    table = np.zeros((2, 4, 2, 2, 6, 2, 128))
    for h in range(4):
        for i in range(MINE):
            c, s = turn(column_j(h, i) * b, 128)
            own = table[h // 2, i % 4, h % 2, :, i // 4]
            own[0, 0], own[0, 1], own[1, 0], own[1, 1] = c, s, -s, c
    return np.concatenate(list(halves(table.reshape(2, 96, 256))), axis=1)


def x_inverse_table(by_chunk):
    b = np.arange(128)
    table = np.zeros((4, 4, 2, 6, 2, 128)) if by_chunk else np.zeros((4, 2, MINE, 2, 128))
    for h in range(4):
        for i in range(MINE):
            c, s = turn(column_j(h, i) * b, 128)
            own = table[i % 4, h, :, i // 4] if by_chunk else table[h, :, i]
            own[0, 0], own[0, 1], own[1, 0], own[1, 1] = c, s, -s, c
    table = table.reshape(-1, 256) * (2.0 / (GRID * GRID))
    return halves(table if by_chunk else np.pad(table, ((0, 8), (0, 0))))


def x_twiddle():
    table = np.zeros((32, 128))
    c, s = turn(np.arange(9)[:, None] * np.arange(128)[None, :], GRID)
    table[0:9] = c
    table[16:25] = s
    return table.astype(np.float32)


def y_radix_table():
    c, s = turn(np.arange(KAP)[:, None] * np.arange(64)[None, :], 64)
    high, low = halves(np.concatenate([c, -s], axis=0))
    return np.concatenate([high, high, low], axis=1)


def y_radix_inverse_table():
    c, s = turn(np.arange(64)[:, None] * np.arange(KAP)[None, :], 64)
    high, low = halves(np.concatenate([c, -s], axis=1))
    return np.block([[high, high], [low, np.zeros_like(low)]])


def y_twiddle():
    c, s = turn(np.arange(KAP)[:, None] * np.arange(ROWS)[None, :], GRID)
    return np.stack([np.tile(c, (1, 4)), np.tile(s, (1, 4))]).astype(np.float32)


def lanes_of():
    c, s = turn(np.arange(ROWS)[:, None] * np.arange(JP)[None, :], ROWS)
    table = np.zeros((2, 4, ROWS, 128))
    for jb in range(4):
        re = slice(2 * JP * jb, 2 * JP * jb + JP)
        im = slice(2 * JP * jb + JP, 2 * JP * jb + 2 * JP)
        table[0, jb, :, re], table[1, jb, :, re] = c, s
        table[0, jb, :, im], table[1, jb, :, im] = -s, c
    return table.reshape(256, 128)


def y_lane_table():
    return np.concatenate(list(halves(lanes_of())), axis=1)


def y_lane_inverse_table():
    high, low = halves(2.0 * lanes_of().T)
    return np.concatenate([high, high, low], axis=0)


def y_projection_table():
    difference = np.arange(ROWS)[None, :] - np.arange(ROWS)[:, None]
    tables = []
    for count in (JP, JP - 1):
        c, s = turn(difference[:, :, None] * np.arange(count)[None, None, :], ROWS)
        c, s = np.kron(np.eye(4), 2 * c.sum(-1)), np.kron(np.eye(4), 2 * s.sum(-1))
        tables.append(np.block([[c, s], [-s, c]]))
    return halves(np.stack(tables))


def y_mean_table():
    return np.kron(np.eye(8), np.ones((ROWS, ROWS))).astype(ml_dtypes.bfloat16)


def lane_facts():
    lane = np.arange(128)
    facts = np.zeros((8, 128))
    facts[0] = 16 * (lane // (2 * JP))
    facts[1] = 64 * (lane % JP)
    return facts.astype(np.float32)


def packed_facts():
    lane = np.arange(USED)
    own = lane % (USED // 8)
    facts = np.zeros((8, USED))
    facts[0] = 16 * (own // (2 * JP))
    facts[1] = 64 * (own % JP) + 8 * (lane // (USED // 8))
    return facts.astype(np.float32)


def split(value):
    high = value.astype(BF16)
    low = (value - high.astype(F32)).astype(BF16)
    return high, low


def dot(a, b, dims):
    return lax.dot_general(a, b, (dims, ((), ())), preferred_element_type=F32)


def matmul(left, right, dims):
    return dot(left[0], right[0], dims) + (dot(left[0], right[1], dims) + dot(left[1], right[0], dims))


def matmul_tall(table, right):
    out = dot(table[...], jnp.concatenate(right, axis=0), NN)
    size = table.shape[0] // 2
    return out[:size] + out[size:]


def matmul_wide(left, table):
    depth = left[0].shape[1]
    both = jnp.concatenate(left, axis=1)
    return dot(both, table[: 2 * depth], NN) + dot(left[0], table[2 * depth :], NN)


def matmul_beside(left, table):
    size = table.shape[1] // 2
    out = dot(left[0], table[...], NN)
    return out[:, :size] + (out[:, size:] + dot(left[1], table[:, :size], NN))


NN = ((1,), (0,))
NT = ((1,), (1,))
TN = ((0,), (0,))

C1 = math.cos(math.pi / 8)
C2 = math.cos(math.pi / 4)
C3 = math.cos(3 * math.pi / 8)


def real_analysis(x):
    s = [x[a] + x[a + 8] for a in range(8)]
    d = [x[a] - x[a + 8] for a in range(8)]
    e = [None] + [d[a] - d[8 - a] for a in range(1, 4)]
    f = [None] + [d[a] + d[8 - a] for a in range(1, 4)]
    e2, f2 = e[2] * C2, f[2] * C2
    plus, minus = d[0] + e2, d[0] - e2
    first, second = e[1] * C1 + e[3] * C3, e[1] * C3 - e[3] * C1
    third, fourth = f[1] * C3 + f[3] * C1, f[1] * C1 - f[3] * C3
    u, v = d[4] + f2, f2 - d[4]
    p = [s[a] + s[a + 4] for a in range(4)]
    q = [s[a] - s[a + 4] for a in range(4)]
    even, odd = p[0] + p[2], p[1] + p[3]
    hd, hs = (q[1] - q[3]) * C2, (q[1] + q[3]) * C2
    real = [
        even + odd,
        plus + first,
        q[0] + hd,
        minus + second,
        p[0] - p[2],
        minus - second,
        q[0] - hd,
        plus - first,
        even - odd,
    ]
    imag = [
        None,
        -(third + u),
        -(q[2] + hs),
        -(fourth + v),
        p[3] - p[1],
        v - fourth,
        q[2] - hs,
        u - third,
        None,
    ]
    return real, imag


def real_synthesis(real, imag):
    plus, first = real[1] + real[7], real[1] - real[7]
    minus, second = real[3] + real[5], real[3] - real[5]
    third, u = -(imag[1] + imag[7]), imag[7] - imag[1]
    fourth, v = -(imag[3] + imag[5]), imag[5] - imag[3]
    d = [None] * 8
    d[0], d[4] = plus + minus, u - v
    e = [None, first * C1 + second * C3, (plus - minus) * C2, first * C3 - second * C1]
    f = [None, third * C3 + fourth * C1, (u + v) * C2, third * C1 - fourth * C3]
    for a in range(1, 4):
        d[a], d[8 - a] = f[a] + e[a], f[a] - e[a]
    even, odd = real[0] + real[8], real[0] - real[8]
    p = [even + real[4], odd - imag[4], even - real[4], odd + imag[4]]
    hr, hi = (real[2] - real[6]) * C2, (imag[2] + imag[6]) * C2
    q = [real[2] + real[6], hr - hi, imag[6] - imag[2], -(hr + hi)]
    s = [p[a] + q[a] for a in range(4)] + [p[a] - q[a] for a in range(4)]
    return [s[a] + d[a] for a in range(8)] + [s[a] - d[a] for a in range(8)]


def regroup(blocks, wanted):
    block = lax.broadcasted_iota(jnp.int32, (1, 128), 1) // 32
    turned = [
        b if b is None or i == 0 else pltpu.roll(b, 32 * i, 1) for i, b in enumerate(blocks)
    ]
    results = []
    for p in wanted:
        total = None
        for i in range(4):
            part = jnp.zeros_like(turned[0]) if turned[i] is None else turned[i]
            total = part if total is None else jnp.where(block == (p + i) % 4, part, total)
        results.append(total if p == 0 else pltpu.roll(total, 128 - 32 * p, 1))
    return results


def turn_by(re, im, c, s):
    return re * c + im * s, im * c - re * s


def x_forward(real, imag, twiddle, table):
    pieces = []
    for k in range(9):
        if k == 0:
            pieces.append(jnp.concatenate([real[0], jnp.zeros_like(real[0])], axis=1))
            continue
        c, s = twiddle[k : k + 1], twiddle[16 + k : 17 + k]
        if k == 8:
            re, im = real[8] * c, -(real[8] * s)
        else:
            re, im = real[k] * c + imag[k] * s, imag[k] * c - real[k] * s
        pieces.append(jnp.concatenate([re, im], axis=1))
    shared = split(jnp.concatenate(pieces[1:8], axis=0))
    results = []
    for half, own in enumerate((pieces[0], pieces[8])):
        own = split(own)
        right = [jnp.concatenate([own[i], shared[i]], axis=0) for i in range(2)]
        out = dot(table[half], right[0], NT)
        results.append(out[:96] + (out[96:] + dot(table[half, :96], right[1], NT)))
    return results


def modes_of(source, twiddle, turned=False):
    real, imag = [], []
    for k in range(9):
        c, s = twiddle[k : k + 1], twiddle[16 + k : 17 + k]
        z = source(k)
        re, im = z[:, :128], z[:, 128:]
        if k == 0:
            real.append(im if turned else re)
            imag.append(None)
            continue
        real.append(im * c + re * s if turned else re * c - im * s)
        if k == 8:
            imag.append(None)
        else:
            imag.append(im * s - re * c if turned else re * s + im * c)
    return real, imag


def y_turned(in_ref, radix, twiddle):
    columns = [in_ref[pl.ds(jr, 64, stride=CHUNK), :] for jr in range(6)]
    high, low = split(jnp.concatenate(columns, axis=1))
    mixed = dot(radix[...], jnp.concatenate([high, low, high], axis=0), NN)
    results = []
    for jr in range(6):
        lanes = slice(128 * jr, 128 * jr + 128)
        re, im = turn_by(mixed[:KAP, lanes], mixed[KAP:, lanes], twiddle[0], twiddle[1])
        results.append(jnp.concatenate([re, im], axis=1))
    return results


def y_returned(pairs, radix, twiddle):
    lane = lax.broadcasted_iota(jnp.int32, (1, 128), 1)
    c, s = twiddle[0], twiddle[1]
    real, imag = [], []
    for pair, turned in pairs:
        re, im = pair[:, :128], pair[:, 128:]
        if turned in (0, 4):
            real.append(im * c + re * s if turned else re * c - im * s)
            imag.append(im * s - re * c if turned else re * s + im * c)
            continue
        early = lane < 32 * turned
        re, im = jnp.where(early, im, re), jnp.where(early, -re, im)
        real.append(re * c - im * s)
        imag.append(re * s + im * c)
    right = jnp.concatenate([jnp.concatenate(real, axis=1), jnp.concatenate(imag, axis=1)], axis=0)
    return matmul_tall(radix, split(right))


def pieces_of():
    for rows in range(8):
        for jr in range(6):
            index, offset = divmod(rows * (USED // 8) + PIECE * jr, 128)
            yield rows, jr, index, offset, PIECE if jr < 5 else 2 * JP


def pack(tiles):
    lane = lax.broadcasted_iota(jnp.int32, (1, 128), 1)
    packed = [None] * TILES
    for rows, jr, index, offset, used in pieces_of():
        moved = tiles[jr][8 * rows : 8 * rows + 8]
        moved = pltpu.roll(moved, offset, 1) if offset else moved
        parts = [(index, moved)]
        if offset + used > 128:
            parts = [(index, jnp.where(lane >= offset, moved, 0.0))]
            parts.append((index + 1, jnp.where(lane < offset, moved, 0.0)))
        for own, part in parts:
            packed[own] = part if packed[own] is None else packed[own] + part
    return packed


def unpack(packed):
    lane = lax.broadcasted_iota(jnp.int32, (1, 128), 1)
    tiles = [[] for _ in range(6)]
    for rows, jr, index, offset, used in pieces_of():
        tile = packed[:, 128 * index : 128 * index + 128]
        if offset + used > 128:
            tile = jnp.where(lane >= offset, tile, packed[:, 128 * index + 128 : 128 * index + 256])
        tiles[jr].append(pltpu.roll(tile, 128 - offset, 1) if offset else tile)
    return [jnp.concatenate(tile, axis=0) for tile in tiles]


def y_waves(facts, count=KAP):
    row = lax.broadcasted_iota(jnp.int32, (count, 1), 0).astype(F32)
    return row + facts[1:2]


def x_waves(facts, owner):
    slot = owner // 8
    h = (owner % 8) // 2
    eight = jnp.where(slot == 0, 8 * (h // 2), 0)
    return facts[0:1] + (slot + eight + 16 * (21 * h - 84 * (h // 2))).astype(F32)


def half_of_zero(wave):
    return jnp.where(wave == 0.0, 0.5, 1.0)


def store_x(out_ref, results, group):
    for half in range(2):
        lanes = slice(128 * group, 128 * group + 128)
        blocks = [results[half][24 * jb : 24 * jb + 24, lanes] for jb in range(4)]
        for slot, block in enumerate(regroup(blocks, range(4))):
            start = (8 * (4 * group + slot) + 4 * half) * CHUNK
            out_ref[start : start + 4 * CHUNK, :] = block


def state_kernel(
    state_hbm, twiddle_hbm, table_hbm, out_hbm, state_ref, twiddle_ref, table_ref, out_ref, sems
):
    pairs = ((state_hbm, state_ref), (twiddle_hbm, twiddle_ref), (table_hbm, table_ref))
    copies = [pltpu.make_async_copy(a, b, sems.at[i]) for i, (a, b) in enumerate(pairs)]
    for copy in copies:
        copy.start()
    copies[0].wait()
    x = [state_ref[0, :, 128 * a : 128 * a + 128] for a in range(16)]
    real, imag = real_analysis(x)
    copies[1].wait()
    copies[2].wait()
    results = x_forward(real, imag, twiddle_ref[...], table_ref)
    for group in range(2):
        store_x(out_ref, results, group)
        rows = pl.ds(32 * group * CHUNK, 32 * CHUNK)
        pltpu.make_async_copy(out_ref.at[rows], out_hbm.at[rows], sems.at[3]).start()
    pltpu.make_async_copy(out_ref, out_hbm, sems.at[3]).wait()


def weights_kernel(to_ref, from_ref, deform_ref, packed_ref, facts_ref, out_ref, damping_ref):
    facts = packed_ref[...]
    wave_x = x_waves(facts, lax.axis_index("row"))
    wave_y = y_waves(facts, 8)
    square = wave_x * wave_x + wave_y * wave_y
    layer = lax.axis_index("layer")
    modes = [from_ref[layer, m] * (-1.0 / (square + deform_ref[m])) for m in range(8)]
    for n in range(8):
        total = None
        for m in range(8):
            term = modes[m] * to_ref[m, n]
            total = term if total is None else total + term
        out_ref[n] = total
    facts = facts_ref[...]
    wave_y = y_waves(facts)
    once = half_of_zero(wave_y)
    for jr in range(6):
        wave_x = x_waves(facts, lax.axis_index("row")) + 64 * jr
        ratio = (wave_x * wave_x + wave_y * wave_y) * (1.0 / (KCUT * KCUT))
        ratio = ratio * ratio
        damping_ref[KAP * jr : KAP * jr + KAP, :] = (HYPER_RATE * (ratio * ratio)) * once


def spectrum_kernel(in_ref, radix_ref, turn_ref, lanes_ref, facts_ref, spec_ref, used_ref):
    turned = split(jnp.concatenate(y_turned(in_ref, radix_ref, turn_ref), axis=0))
    spectrum = matmul_beside(turned, lanes_ref)
    kept = y_waves(facts_ref[...]) < KCUT
    tiles = [jnp.where(kept, spectrum[KAP * jr : KAP * jr + KAP], 0.0) for jr in range(6)]
    spec_ref[...] = jnp.concatenate(tiles, axis=0)
    for index, tile in enumerate(pack(tiles)):
        lanes = slice(128 * index, min(USED, 128 * index + 128))
        used_ref[:, lanes] = tile[:, : lanes.stop - lanes.start]


def stream_kernel(
    weights_ref, all_ref, spec_ref, unradix_ref, turn_ref, unlanes_ref, facts_ref, out_ref, stream_ref
):
    stream = None
    for n in range(8):
        term = weights_ref[n] * all_ref[n]
        stream = term if stream is None else stream + term
    stream_ref[:, 128 * TILES - 128 :] = jnp.zeros((8, 128), F32)
    stream_ref[:, :USED] = stream
    facts = facts_ref[...]
    wave_y = y_waves(facts)
    once = half_of_zero(wave_y)
    pieces = []
    for jr, tile in enumerate(unpack(stream_ref[...])):
        wave_x = x_waves(facts, lax.axis_index("row")) + 64 * jr
        along_y, along_x = wave_y * half_of_zero(wave_x), wave_x * once
        own = spec_ref[KAP * jr : KAP * jr + KAP, :]
        four = [along_y * tile, -along_y * own, along_x * tile, along_x * own]
        if jr < 5:
            pieces += four
            continue
        alone = lax.broadcasted_iota(jnp.int32, (1, 128), 1) < 2 * JP
        four = [jnp.where(alone, field, 0.0) for field in four]
        moved = [four[0]] + [pltpu.roll(four[f], 2 * JP * f, 1) for f in range(1, 4)]
        pieces.append((moved[0] + moved[1]) + (moved[2] + moved[3]))
    out = matmul_wide(split(jnp.concatenate(pieces, axis=0)), unlanes_ref)
    turned = [4, 4, 0, 0] * 5 + [2]
    pairs = [(out[KAP * i : KAP * i + KAP], turned[i]) for i in range(21)]
    out = y_returned(pairs, unradix_ref, turn_ref)
    for jr in range(5):
        blocks = [out[:, 128 * (4 * jr + f) : 128 * (4 * jr + f) + 128] for f in range(4)]
        for jb, block in enumerate(regroup(blocks, range(4))):
            out_ref[pl.ds(4 * jr + jb, 64, stride=MINE), :] = block
    out_ref[pl.ds(20, 64, stride=MINE), :] = out[:, 128 * 20 :]


def jacobian_kernel(in_ref, twiddle_ref, untable_ref, table_ref, out_ref, first_ref, whole_ref, jac):
    depth = 8 * MINE
    row = lax.broadcasted_iota(jnp.int32, (depth, 1), 0)
    spare = jnp.zeros((8, 4 * 128), F32)
    table = [untable_ref[0], untable_ref[1]]
    for part in range(2):
        slots = [
            in_ref[depth * slot : depth * slot + depth, :] for slot in range(4 * part, 4 * part + 4)
        ]
        side = jnp.concatenate([jnp.concatenate(slots, axis=1), spare], axis=0)
        whole_ref[512 * part : 512 * part + 512, :] = matmul(split(side), table, TN)
        if part == 0:
            own = jnp.concatenate([jnp.where(row < depth // 2, slots[0], 0.0), spare[:, :128]], axis=0)
            first_ref[...] = matmul(split(own), table, TN)
    twiddle = twiddle_ref[...]
    for block in range(4):
        rows = slice(8 * block, 8 * block + 8)

        def physical(field):
            def source(k):
                start = 32 * field + rows.start
                if k == 0:
                    return first_ref[start : start + 8, :]
                start += 128 * (k % 8)
                z = whole_ref[start : start + 8, :]
                return z if k < 8 else z - source(0)

            return real_synthesis(*modes_of(source, twiddle, field > 1))

        east, slope_x = physical(0), physical(3)
        product = [a * b for a, b in zip(east, slope_x)]
        north, slope_y = physical(2), physical(1)
        product = [p + a * b for p, a, b in zip(product, north, slope_y)]
        real, imag = real_analysis(product)
        for k in range(9):
            jac[0, k, rows, :] = real[k]
            if imag[k] is not None:
                jac[1, k, rows, :] = imag[k]
    real = [jac[0, k] for k in range(9)]
    imag = [None] + [jac[1, k] for k in range(1, 8)] + [None]
    results = x_forward(real, imag, twiddle, table_ref)
    for group in range(2):
        store_x(out_ref, results, group)


def projection_kernel(
    in_ref, spec_ref, radix_ref, unradix_ref, turn_ref, project_ref, mean_ref, unlanes_ref, damping_ref, out_ref
):
    damping = matmul_wide(split(damping_ref[...] * spec_ref[...]), unlanes_ref)
    left = [split(pair) for pair in y_turned(in_ref, radix_ref, turn_ref)]
    sides = []
    for side in range(2):
        rows = slice(32 * side, 32 * side + 32)
        stacked = [jnp.concatenate([pair[i][rows] for pair in left], axis=0) for i in range(2)]
        sides.append(matmul(stacked, [project_ref[i, side] for i in range(2)], NN))
    heads = [jnp.concatenate([pair[i][:16] for pair in left], axis=0) for i in range(2)]
    mean = dot(heads[0], mean_ref[...], NN) + dot(heads[1], mean_ref[...], NN)
    first = lax.broadcasted_iota(jnp.int32, (16, 1), 0) == 0
    lane = lax.broadcasted_iota(jnp.int32, (1, 256), 1)
    zero_wave = (lax.axis_index("row") < 2) & (lane % 128 < 32)
    pairs = []
    for jr in range(6):
        low, high = [side[32 * jr : 32 * jr + 32] for side in sides]
        own = jnp.where(first, mean[16 * jr : 16 * jr + 16], 0.0)
        flux = jnp.concatenate([low[:16] - own, low[16:], high], axis=0)
        total = flux - damping[KAP * jr : KAP * jr + KAP]
        pairs.append((total * jnp.where(zero_wave, 0.5, 1.0) if jr == 0 else total, 0))
    out = y_returned(pairs, unradix_ref, turn_ref)
    for jr in range(6):
        out_ref[pl.ds(jr, 64, stride=CHUNK), :] = out[:, 128 * jr : 128 * jr + 128]


def state_update_kernel(
    in_ref,
    state_ref,
    start_ref,
    twiddle_ref,
    untable_ref,
    tendency_hbm,
    new_hbm,
    first,
    whole,
    tendency_ref,
    new_ref,
    sems,
):
    depth = 8 * CHUNK
    table = [untable_ref[0], untable_ref[1]]
    for group in range(2):
        blocks = [in_ref[depth * slot : depth * slot + depth, :] for slot in range(4 * group, 4 * group + 4)]
        side = jnp.concatenate(regroup(blocks, range(4)), axis=0)
        whole[128 * group : 128 * group + 128, :] = matmul(split(side), table, TN)
        if group == 0:
            row = lax.broadcasted_iota(jnp.int32, (4 * depth, 1), 0)
            own = jnp.where(row % depth < depth // 2, side, 0.0)
            first[...] = matmul(split(own), table, TN)
    twiddle = twiddle_ref[...]
    for block in range(4):
        rows = slice(8 * block, 8 * block + 8)

        def source(k):
            if k == 0:
                return first[rows, :]
            start = 32 * (k % 8) + rows.start
            z = whole[start : start + 8, :]
            return z if k < 8 else z - source(0)

        tendency = real_synthesis(*modes_of(source, twiddle))
        for a in range(16):
            columns = slice(128 * a, 128 * a + 128)
            tendency_ref[0, rows, columns] = tendency[a]
            new_ref[0, rows, columns] = 0.75 * start_ref[0, rows, columns] + 0.25 * (
                state_ref[0, rows, columns] + STEP_SIZE * tendency[a]
            )
        for i, (near, far) in enumerate(((tendency_ref, tendency_hbm), (new_ref, new_hbm))):
            own = (slice(None), pl.ds(8 * block, 8))
            pltpu.make_async_copy(near.at[own], far.at[own], sems.at[i]).start()
    pltpu.make_async_copy(tendency_ref, tendency_hbm, sems.at[0]).wait()
    pltpu.make_async_copy(new_ref, new_hbm, sems.at[1]).wait()


VMEM = pl.BlockSpec(memory_space=pltpu.VMEM)
SMEM = pl.BlockSpec(memory_space=pltpu.SMEM)
ANY = pl.BlockSpec(memory_space=pl.ANY)
MIB = 1024 * 1024


def call(kernel, outs, operands, scalars=0, scratch=(), far_in=False, far_out=False, copies=0, cost=None):
    scratch_shapes = [pltpu.VMEM(operand.shape, operand.dtype) for operand in operands] if far_in else []
    scratch_shapes += [pltpu.VMEM(shape, F32) for shape in scratch]
    scratch_shapes += [pltpu.VMEM(shape, F32) for shape in outs] if far_out else []
    scratch_shapes += [pltpu.SemaphoreType.DMA((copies,))] if copies else []
    near = [SMEM] * scalars + [VMEM] * (len(operands) - scalars)
    return pl.pallas_call(
        kernel,
        out_shape=[jax.ShapeDtypeStruct(shape, F32) for shape in outs],
        in_specs=[ANY] * len(operands) if far_in else near,
        out_specs=[ANY if far_out else VMEM] * len(outs),
        scratch_shapes=scratch_shapes,
        compiler_params=pltpu.CompilerParams(vmem_limit_bytes=(60 if far_in else 32) * MIB),
        cost_estimate=cost,
    )(*operands)


def exchange(chunks, devices):
    length = chunks.shape[0]
    sent = chunks.reshape(devices, 1, length * 128 // devices)
    return lax.all_to_all(sent, "row", split_axis=0, concat_axis=0, tiled=True).reshape(length, 128)


def per_device(state, start_state, to_modes, from_modes, deform):
    devices = lax.axis_size("row")
    turn_x = jnp.asarray(x_twiddle())
    forward_x = jnp.asarray(x_forward_table())
    inverse_x = jnp.asarray(x_inverse_table(False))
    inverse_chunk = jnp.asarray(x_inverse_table(True))
    radix = jnp.asarray(y_radix_table())
    unradix = jnp.asarray(y_radix_inverse_table())
    turn_y = jnp.asarray(y_twiddle())
    lanes = jnp.asarray(y_lane_table())
    unlanes = jnp.asarray(y_lane_inverse_table())
    project = jnp.asarray(y_projection_table())
    mean = jnp.asarray(y_mean_table())
    facts = jnp.asarray(lane_facts())

    one, four = (64 * CHUNK, 128), (64 * MINE, 128)
    (columns,) = call(state_kernel, [one], [state, turn_x, forward_x], far_in=True, far_out=True, copies=4)
    columns = exchange(columns, devices)
    spectrum, used = call(
        spectrum_kernel, [(6 * KAP, 128), (8, USED)], [columns, radix, turn_y, lanes, facts]
    )
    weights, damping = call(
        weights_kernel,
        [(8, 8, USED), (6 * KAP, 128)],
        [to_modes, from_modes, deform, jnp.asarray(packed_facts()), facts],
        scalars=3,
        cost=pl.CostEstimate(flops=8_000_000, bytes_accessed=2_000_000, transcendentals=0),
    )
    gathered = lax.all_gather(used, "layer", axis=0, tiled=False)
    (fields,) = call(
        stream_kernel,
        [four],
        [weights, gathered, spectrum, unradix, turn_y, unlanes, facts],
        scratch=[(8, 128 * TILES)],
    )
    fields = exchange(fields, devices)
    (flux,) = call(
        jacobian_kernel,
        [one],
        [fields, turn_x, inverse_x, forward_x],
        scratch=[(128, 256), (1024, 256), (2, 9, ROWS, 128)],
    )
    flux = exchange(flux, devices)
    (total,) = call(
        projection_kernel,
        [one],
        [flux, spectrum, radix, unradix, turn_y, project, mean, unlanes, damping],
    )
    total = exchange(total, devices)
    return tuple(
        call(
            state_update_kernel,
            [(1, ROWS, GRID)] * 2,
            [total, state, start_state, turn_x, inverse_chunk],
            scratch=[(128, 256), (256, 256)],
            far_out=True,
            copies=2,
        )
    )


def solution(mesh):
    in_specs = (P("layer", "row", None), P("layer", "row", None), P(), P(), P())
    out_specs = (P("layer", "row", None), P("layer", "row", None))
    return jax.shard_map(
        per_device, mesh=mesh, in_specs=in_specs, out_specs=out_specs, check_vma=False
    )
```
